512 devices in a mesh: gx: 32 (over x, y, core), gy: 16 (over z).
Axes of the slice: x: 4, y: 4, z: 16, core: 2. Of those that a mesh axis runs over, the one named last changes fastest.
Arguments:
- state: float32 [5, 512, 128, 128], P(None, 'gx', 'gy'), may hold values from -4 to 4
- pinning: float32 [512, 128, 128], P('gx', 'gy'), may hold values from -1 to 1
- lead_values: float32 [2, 128, 128], P(None, 'gy'), may hold values from -4 to 4
Outputs:
- next_state: float32 [5, 512, 128, 128], P(None, 'gx', 'gy')
- potential: float32 [512, 128, 128], P('gx', 'gy')
The draws below stay inside these ranges and needn't reach their ends.
All inputs are finite; a program needn't handle non-finite values.
Results may differ from the reference program's by a relative error of at most 0.0003.
Values sent between devices are 32-bit elements; how exact they have to be, the bound alone decides.
A program may use at most 128 MiB of HBM per device.

```python
import math
import jax
import jax.numpy as jnp
from jax import lax

NZ = 128
LEVELS = 4
PRE = 3
POST = 2
NX = 512
NY = 128


def draw_lead_values(key, part):
    key = jax.random.fold_in(key, 11)
    second = jax.random.fold_in(key, 1)
    level = jnp.float32(1.5)
    noise = jnp.clip(0.6 * jax.random.normal(second, (2, NY, NZ), jnp.float32), -2.4, 2.4)
    signs = jnp.array([1.0, -1.0], jnp.float32)[:, None, None]
    return signs * (level + noise)


def levels(key, extent, shards, smallest, high):
    loudness, own = 1.0, jax.random.fold_in(key, 6)
    for dim, shards_of in shards:
        draws = jnp.exp(jax.random.uniform(jax.random.fold_in(own, dim), (shards_of,), jnp.float32, smallest / len(shards), high / len(shards)))
        loudness = loudness * jnp.repeat(draws, extent[dim] // shards_of).reshape([-1 if axis == dim else 1 for axis in range(len(extent))])
    return loudness


def scatter_about(key, extent, deviation, limit, shards=(), kind=jnp.bfloat16):
    drawn = deviation * jax.random.normal(key, extent, jnp.float32)
    if shards:
        drawn = drawn * levels(key, extent, shards, -0.22, 0.18)
    return jnp.clip(drawn, -limit, limit).astype(kind)


def setup_inputs(seed: int = 0) -> dict:
    splits = jax.random.split(jax.random.key(seed), 4)
    return {
        "state": scatter_about(splits[0], (5, NX, NY, NZ), 0.7, 4.0, ((1, 32), (2, 16)), jnp.float32),
        "pinning": jnp.clip(jax.random.uniform(splits[1], (NX, NY, NZ), jnp.float32, -1.0, 1.0) * levels(splits[1], (NX, NY, NZ), ((0, 32), (1, 16)), -0.4, 0.0), -1.0, 1.0),
        "lead_values": draw_lead_values(jax.random.fold_in(splits[3], 71), 0),
    }


OMEGA = 0.8
DT = 0.05
KAPPA2 = 2.0

def window_of(values, offset):
    ext_x, ext_y, ext_z = values.shape
    return values[1 + offset[0]:ext_x - 1 + offset[0], 1 + offset[1]:ext_y - 1 + offset[1], 1 + offset[2]:ext_z - 1 + offset[2]]

def unit_step(axis_no):
    return tuple((1 if place == axis_no else 0 for place in range(3)))

def offset_sum(first, second):
    return tuple((a + b for a, b in zip(first, second)))

def negated(offset):
    return tuple((-a for a in offset))

def plaquette(links, first, second, offset):
    ahead_first = offset_sum(offset, unit_step(first))
    ahead_second = offset_sum(offset, unit_step(second))
    return window_of(links[second], ahead_first) - window_of(links[second], offset) - (window_of(links[first], ahead_second) - window_of(links[first], offset))

def flow_terms(padded, pinning):
    psi_real = padded[0]
    psi_imag = padded[1]
    links = (padded[2], padded[3], padded[4])
    anchor = (0, 0, 0)
    here_re = window_of(psi_real, anchor)
    here_im = window_of(psi_imag, anchor)
    lap_re = jnp.zeros_like(here_re)
    lap_im = jnp.zeros_like(here_re)
    divergence = jnp.zeros_like(here_re)
    currents = []
    for comp in range(3):
        ahead = unit_step(comp)
        behind = negated(ahead)
        cos_ahead = jnp.cos(window_of(links[comp], anchor))
        sin_ahead = jnp.sin(window_of(links[comp], anchor))
        next_re = window_of(psi_real, ahead)
        next_im = window_of(psi_imag, ahead)
        moved_re = cos_ahead * next_re + sin_ahead * next_im
        moved_im = cos_ahead * next_im - sin_ahead * next_re
        cos_behind = jnp.cos(window_of(links[comp], behind))
        sin_behind = jnp.sin(window_of(links[comp], behind))
        prev_re = window_of(psi_real, behind)
        prev_im = window_of(psi_imag, behind)
        back_re = cos_behind * prev_re - sin_behind * prev_im
        back_im = cos_behind * prev_im + sin_behind * prev_re
        into_re = cos_behind * here_re + sin_behind * here_im
        into_im = cos_behind * here_im - sin_behind * here_re
        current_here = here_re * moved_im - here_im * moved_re
        current_back = prev_re * into_im - prev_im * into_re
        lap_re = lap_re + moved_re + back_re
        lap_im = lap_im + moved_im + back_im
        divergence = divergence + (current_here - current_back)
        currents.append(current_here)
    lap_re = lap_re - 6.0 * here_re
    lap_im = lap_im - 6.0 * here_im
    condense = pinning - (here_re * here_re + here_im * here_im)
    rate_re = lap_re + condense * here_re
    rate_im = lap_im + condense * here_im
    step_x = unit_step(0)
    step_y = unit_step(1)
    step_z = unit_step(2)
    curl_x = plaquette(links, 0, 1, anchor) - plaquette(links, 0, 1, negated(step_y)) - (plaquette(links, 2, 0, anchor) - plaquette(links, 2, 0, negated(step_z)))
    curl_y = plaquette(links, 1, 2, anchor) - plaquette(links, 1, 2, negated(step_z)) - (plaquette(links, 0, 1, anchor) - plaquette(links, 0, 1, negated(step_x)))
    curl_z = plaquette(links, 2, 0, anchor) - plaquette(links, 2, 0, negated(step_x)) - (plaquette(links, 1, 2, anchor) - plaquette(links, 1, 2, negated(step_y)))
    rates_link = [currents[0] - KAPPA2 * curl_x, currents[1] - KAPPA2 * curl_y, currents[2] - KAPPA2 * curl_z]
    return (rate_re, rate_im, rates_link, divergence, here_re, here_im)

def neighbours(padded):
    wider = jnp.pad(padded, ((0, 0), (0, 0), (1, 1)), mode='edge')
    centre = wider[1:-1, 1:-1]
    summed = wider[2:, 1:-1, 1:-1] + wider[:-2, 1:-1, 1:-1]
    summed = summed + wider[1:-1, 2:, 1:-1] + wider[1:-1, :-2, 1:-1]
    summed = summed + centre[:, :, 2:] + centre[:, :, :-2]
    return summed

def level_apply(iterate, around, factor):
    return (6.0 * iterate - around) * factor

def jacobi_sweep(iterate, applied, source, factor):
    return iterate + OMEGA * (source - applied) / (6.0 * factor)

def restrict(values):
    size_x, size_y, size_z = values.shape
    return values.reshape(size_x // 2, 2, size_y // 2, 2, size_z // 2, 2).sum(axis=(1, 3, 5)) * 0.125

def prolong(values):
    return jnp.repeat(jnp.repeat(jnp.repeat(values, 2, 0), 2, 1), 2, 2)

def sine_table(count):
    modes = jnp.arange(1, count + 1, dtype=jnp.float32)
    return jnp.sqrt(2.0 / (count + 1)) * jnp.sin(math.pi / (count + 1) * modes[:, None] * modes[None, :])

def sine_values(count):
    modes = jnp.arange(1, count + 1, dtype=jnp.float32)
    return 2.0 - 2.0 * jnp.cos(math.pi / (count + 1) * modes)

def cosine_table(count):
    modes = jnp.arange(count, dtype=jnp.float32)
    cells = jnp.arange(count, dtype=jnp.float32) + 0.5
    weights = jnp.where(modes == 0.0, 1.0, 2.0) / count
    return jnp.sqrt(weights)[:, None] * jnp.cos(math.pi / count * modes[:, None] * cells[None, :])

def cosine_values(count):
    modes = jnp.arange(count, dtype=jnp.float32)
    return 2.0 - 2.0 * jnp.cos(math.pi / count * modes)

def transform(values, table_x, table_y, table_z):
    highest = lax.Precision.HIGHEST
    spectral = jnp.einsum('ia,abc->ibc', table_x, values, precision=highest)
    spectral = jnp.einsum('jb,ibc->ijc', table_y, spectral, precision=highest)
    return jnp.einsum('kc,ijc->ijk', table_z, spectral, precision=highest)

def coarse_solve(source, factor):
    size_x, size_y, size_z = source.shape
    table_x = sine_table(size_x)
    table_y = cosine_table(size_y)
    table_z = cosine_table(size_z)
    spectral = transform(source, table_x, table_y, table_z)
    denom = (sine_values(size_x)[:, None, None] + cosine_values(size_y)[None, :, None] + cosine_values(size_z)[None, None, :]) * factor
    return transform(spectral / denom, table_x.T, table_y.T, table_z.T)

def operator_at(iterate, factor):
    padded = jnp.pad(jnp.pad(iterate, ((1, 1), (0, 0), (0, 0))), ((0, 0), (1, 1), (0, 0)), mode='edge')
    return level_apply(iterate, neighbours(padded), factor)

def reference(state, pinning, lead_values):
    padded = jnp.pad(state, ((0, 0), (1, 1), (1, 1), (1, 1)))
    rate_re, rate_im, rates_link, divergence, here_re, here_im = flow_terms(padded, pinning)
    lead_term = jnp.zeros((NX, NY, NZ), jnp.float32).at[0].set(lead_values[0]).at[NX - 1].set(lead_values[1])
    sources = [lead_term - divergence]
    saved = []
    for layer_no in range(LEVELS - 1):
        factor = 0.25 ** layer_no
        source = sources[layer_no]
        blank = jnp.zeros_like(source)
        iterate = jacobi_sweep(blank, blank, source, factor)
        for sweep_no in range(PRE - 1):
            iterate = jacobi_sweep(iterate, operator_at(iterate, factor), source, factor)
        saved.append(iterate)
        sources.append(restrict(source - operator_at(iterate, factor)))
    iterate = coarse_solve(sources[LEVELS - 1], 0.25 ** (LEVELS - 1))
    for layer_no in reversed(range(LEVELS - 1)):
        factor = 0.25 ** layer_no
        iterate = saved[layer_no] + prolong(iterate)
        for sweep_no in range(POST):
            iterate = jacobi_sweep(iterate, operator_at(iterate, factor), sources[layer_no], factor)
    potential = iterate
    extended = jnp.pad(potential, ((0, 1), (0, 1), (0, 1)))
    grad_x = extended[1:, :-1, :-1] - potential
    grad_y = extended[:-1, 1:, :-1] - potential
    grad_z = extended[:-1, :-1, 1:] - potential
    final_re = rate_re + potential * here_im
    final_im = rate_im - potential * here_re
    rates = jnp.stack([final_re, final_im, rates_link[0] - grad_x, rates_link[1] - grad_y, rates_link[2] - grad_z])
    return (state + DT * rates, potential)
```

```python
import functools
import math

import jax
import jax.numpy as jnp
import ml_dtypes
import numpy as np
from jax import lax
from jax.experimental import pallas as pl
from jax.experimental.pallas import tpu as pltpu
from jax.sharding import PartitionSpec as P

MESH = pl.DeviceIdType.MESH
OMEGA = 0.8
DT = 0.05
KAPPA2 = 2.0
KEEP = 1.0 - OMEGA
GAIN = OMEGA / 6.0
TX, TY, NZ = 16, 8, 128


def chebyshev_powers(function, terms):
    fit = np.polynomial.chebyshev.Chebyshev.interpolate(
        lambda u: function(np.sqrt(np.maximum(8.0 * (u + 1.0), 0.0))), terms, domain=[-1, 1]
    )
    return [float(c) for c in np.polynomial.chebyshev.cheb2poly(fit.coef)]


COS_POWERS = chebyshev_powers(np.cos, 8)
SIN_POWERS = chebyshev_powers(lambda a: np.sinc(a / np.pi), 8)


def horner(powers, u):
    total = powers[-1] * u + powers[-2]
    for power in powers[-3::-1]:
        total = total * u + power
    return total


def cos_sin(angle):
    u = angle * angle * 0.125 - 1.0
    return horner(COS_POWERS, u), horner(SIN_POWERS, u) * angle


def sine_table(count):
    modes = np.arange(1, count + 1, dtype=np.float64)
    return np.sqrt(2.0 / (count + 1)) * np.sin(np.pi / (count + 1) * modes[:, None] * modes[None])


def sine_values(count):
    return 2.0 - 2.0 * np.cos(np.pi / (count + 1) * np.arange(1, count + 1, dtype=np.float64))


def cosine_table(count):
    modes = np.arange(count, dtype=np.float64)
    weights = np.where(modes == 0.0, 1.0, 2.0) / count
    return np.sqrt(weights)[:, None] * np.cos(
        np.pi / count * modes[:, None] * (modes[None] + 0.5)
    )


def cosine_values(count):
    return 2.0 - 2.0 * np.cos(np.pi / count * np.arange(count, dtype=np.float64))


def split_pair(table):
    high = table.astype(ml_dtypes.bfloat16)
    low = (table - high.astype(np.float64)).astype(ml_dtypes.bfloat16)
    return np.stack([high, low])


def coarse_tables(ngx, ngy):
    nx, ny, nz = 2 * ngx, ngy, 16
    groups = max(1, ngy // 8)
    width = 128 * groups
    tx, ty, tz = sine_table(nx), cosine_table(ny), cosine_table(nz)
    lanes = np.arange(128)
    along_z = np.tile(tz[:, lanes // 8].T / 8.0, (1, 8))
    along_x = np.zeros((nx, ngx, 8))
    for cell in range(8):
        place = 2 * np.arange(ngx) + cell - 3
        within = (place >= 0) & (place < nx)
        along_x[:, within, cell] = tx[:, place[within]]
    along_x = along_x.reshape(nx, ngx // 2, 2, 8).swapaxes(1, 2).reshape(nx, 8 * ngx)
    along_y = np.zeros((width, width))
    inverse = np.zeros((nx, width))
    values = (
        sine_values(nx)[:, None, None]
        + cosine_values(ny)[None, :, None]
        + cosine_values(nz)[None, None, :]
    )
    inverse[:, : ny * nz] = (1.0 / values).reshape(nx, ny * nz)
    along_y[: ny * nz, : ny * nz] = np.kron(ty.T, np.eye(nz))
    back_x = np.zeros((ngx, 16, 128))
    for cell in range(12):
        place = 2 * np.arange(ngx) + cell // 2 - 2
        within = (place >= 0) & (place < nx)
        back_x[within, cell, :nx] = tx.T[place[within]]
    back_yz = np.zeros((ny + 4, width, 128))
    for y in range(ny):
        back_yz[2 + y, : ny * nz] = np.kron(ty[:, y : y + 1], tz[:, lanes // 8])
    return (
        split_pair(along_z),
        split_pair(along_x),
        split_pair(along_y),
        inverse.astype(np.float32),
        split_pair(back_x),
        split_pair(back_yz),
    )


def halves(values):
    high = values.astype(jnp.bfloat16)
    return high, (values - high.astype(jnp.float32)).astype(jnp.bfloat16)


def product(left, right):
    dot = functools.partial(jnp.dot, preferred_element_type=jnp.float32)
    return dot(left[0], right[0]) + (dot(left[0], right[1]) + dot(left[1], right[0]))


def kernel(
    ngx,
    ngy,
    state_ref,
    pinning_ref,
    lead_ref,
    along_z_ref,
    along_x_ref,
    along_y_ref,
    inverse_ref,
    back_x_ref,
    back_yz_ref,
    out_ref,
    potential_ref,
    ext,
    pin,
    lead,
    along_z,
    along_x,
    along_y,
    inverse,
    back_x,
    back_yz,
    face_out,
    face_in,
    diag_in,
    rates,
    work,
    tile0,
    low_out,
    high_out,
    low_in,
    high_in,
    src0,
    va0,
    vb0,
    tile1,
    va1,
    vb1,
    got2,
    src2,
    va2,
    vb2,
    part0,
    pa0,
    pb0,
    part1,
    pa1,
    pb1,
    part2,
    pa2,
    pb2,
    folded,
    coarse,
    gather1,
    gather2,
    local_sem,
    state_sem,
    halo_sem,
    level0_sem,
    level1_sem,
    level2_sem,
    gather_sem,
    relay_sem,
):
    gx, gy = lax.axis_index("gx"), lax.axis_index("gy")

    def device(dx, dy):
        return (lax.rem(gx + dx % ngx, ngx), lax.rem(gy + dy % ngy, ngy))

    def each(first, last, visit):
        def one(place, carry):
            visit(place)
            return carry

        lax.fori_loop(first, last, one, 0, unroll=True)

    own_state = pltpu.make_async_copy(state_ref, ext.at[:, 1:17, 8:16], state_sem)
    own_state.start()
    barrier = pltpu.get_barrier_semaphore()
    def within(dx, dy):
        tests = [gx >= -dx] * (dx < 0) + [gx < ngx - dx] * (dx > 0)
        tests += [gy >= -dy] * (dy < 0) + [gy < ngy - dy] * (dy > 0)
        return functools.reduce(jnp.logical_and, tests)

    near = [
        (dx, dy)
        for dy in range(-4, 5)
        for dx in range(-2, 3)
        if (dx or dy) and abs(dx) * abs(dy) < 4 and (dx == 0 or abs(dy) < 4)
    ]
    for dx, dy in near:

        @pl.when(within(dx, dy))
        def _():
            pl.semaphore_signal(
                barrier, inc=1, device_id=device(dx, dy), device_id_type=MESH
            )

    present = sum(within(dx, dy).astype(jnp.int32) for dx, dy in near)

    locals_ = [
        pltpu.make_async_copy(source, target, local_sem.at[place])
        for place, (source, target) in enumerate(
            [
                (pinning_ref, pin),
                (lead_ref, lead),
                (along_z_ref, along_z),
                (along_x_ref, along_x),
                (along_y_ref, along_y),
                (inverse_ref, inverse),
                (back_x_ref.at[:, gx], back_x),
                (back_yz_ref.at[:, pl.ds(gy, 5)], back_yz),
            ]
        )
    ]
    for ref in (part0, pa0, pb0, part1, pa1, pb1, part2, pa2, pb2):
        ref[...] = jnp.zeros(ref.shape, jnp.float32)

    def clear(*refs):
        for ref in refs:
            ref[...] = jnp.zeros(ref.shape, jnp.float32)

    @pl.when(gx == 0)
    def _():
        clear(tile0.at[:, 0:3], low_in.at[:, 0:3], high_in.at[:, 0:3])
        clear(tile1.at[:, 0:4], got2.at[0:2])

    @pl.when(gx == 1)
    def _():
        clear(got2.at[0:1])

    @pl.when(gx == ngx - 1)
    def _():
        clear(tile0.at[:, 19:22], low_in.at[:, 19:22], high_in.at[:, 19:22])
        clear(tile1.at[:, 12:16], got2.at[3:5])

    @pl.when(gx == ngx - 2)
    def _():
        clear(got2.at[4:5])

    for place in range(3):

        @pl.when(gy == place)
        def _():
            clear(got2.at[:, 0 : 3 - place])

        @pl.when(gy == ngy - 1 - place)
        def _():
            clear(got2.at[:, 4 + place : 7])

    @pl.when(gy == 0)
    def _():
        clear(low_in, tile1.at[:, :, 0:8])

    @pl.when(gy == ngy - 1)
    def _():
        clear(high_in, tile1.at[:, :, 16:24])

    own_state.wait()
    face_out[0] = ext[:, 1:17, 8:9, :]
    face_out[1] = ext[:, 1:17, 15:16, :]
    pl.semaphore_wait(barrier, present)

    sent = []

    def push(source, target, dx, dy, sems, place):
        copy = pltpu.make_async_remote_copy(
            src_ref=source,
            dst_ref=target,
            send_sem=sems.at[0, place],
            recv_sem=sems.at[1, place],
            device_id=device(dx, dy),
            device_id_type=MESH,
        )
        outward = within(dx, dy)
        pl.when(outward)(lambda: copy.start())
        sent.append((copy, outward))
        return copy, within(-dx, -dy)

    def receive(copies):
        for copy, inward in copies:
            pl.when(inward)(lambda: copy.wait_recv())

    halo = [
        push(face_out.at[0], face_in.at[0], 0, -1, halo_sem, 0),
        push(face_out.at[1], face_in.at[1], 0, 1, halo_sem, 1),
        push(ext.at[:, 1, 8:16], ext.at[:, 17, 8:16], -1, 0, halo_sem, 2),
        push(ext.at[:, 16, 8:16], ext.at[:, 0, 8:16], 1, 0, halo_sem, 3),
        push(face_out.at[1, 3, 0], diag_in.at[0], -1, 1, halo_sem, 4),
        push(face_out.at[0, 2, 15], diag_in.at[1], 1, -1, halo_sem, 5),
    ]
    for copy in locals_:
        copy.start()

    def relays(reach, count):
        steps = []
        while reach < count - 1:
            steps.append(reach)
            reach *= 2
        return steps

    relays_x = [(reach, 0) for reach in relays(2, ngx)]
    relays_y = [(0, reach) for reach in relays(4, ngy)]

    def tell(steps, first, place):
        if place < len(steps):
            dx, dy = steps[place]
            for side, sign in enumerate((-1, 1)):

                @pl.when(within(sign * dx, sign * dy))
                def _():
                    pl.semaphore_signal(
                        relay_sem.at[first + place, side],
                        inc=1,
                        device_id=device(sign * dx, sign * dy),
                        device_id_type=MESH,
                    )

    def hear(steps, first, place):
        if place < len(steps):
            dx, dy = steps[place]
            for side, sign in enumerate((-1, 1)):

                @pl.when(within(-sign * dx, -sign * dy))
                def _():
                    pl.semaphore_wait(relay_sem.at[first + place, side], 1)

    tell(relays_y, 4, 0)
    tell(relays_x, 0, 0)

    lane = lax.broadcasted_iota(jnp.int32, (1, NZ), 1)
    row8 = lax.broadcasted_iota(jnp.int32, (TY, NZ), 0)

    def ahead_z(values):
        return jnp.where(lane == NZ - 1, 0.0, pltpu.roll(values, NZ - 1, 1))

    def behind_z(values):
        return jnp.where(lane == 0, 0.0, pltpu.roll(values, 1, 1))

    def here(field, slab, dx=0, dy=0):
        return ext[field, slab + (1 + dx), 8 + dy : 16 + dy, :]

    def link(c, s, re, im, next_re, next_im):
        moved_re = c * next_re + s * next_im
        moved_im = c * next_im - s * next_re
        current = re * moved_im - im * moved_re
        return moved_re, moved_im, c * re - s * im, c * im + s * re, current

    def own_part(i):
        re, im = here(0, i), here(1, i)
        c, s = cos_sin(here(4, i))
        moved_re, moved_im, back_re, back_im, current = link(
            c, s, re, im, ahead_z(re), ahead_z(im)
        )
        rates[0, i] = moved_re + behind_z(back_re)
        rates[1, i] = moved_im + behind_z(back_im)
        rates[4, i] = current
        work[0, i] = behind_z(current) - current
        work[1, i], work[2, i] = cos_sin(here(2, i))
        work[3, i], work[4, i] = cos_sin(here(3, i))

    each(0, TX, own_part)
    hear(relays_y, 4, 0)
    tell(relays_y, 4, 1)
    hear(relays_x, 0, 0)
    tell(relays_x, 0, 1)
    for copy in locals_:
        copy.wait()
    work[0, 0] += jnp.where(gx == 0, 1.0, 0.0) * lead[0]
    work[0, TX - 1] += jnp.where(gx == ngx - 1, 1.0, 0.0) * lead[1]

    receive(halo)
    ext[:, 1:17, 16:17, :] = face_in[0]
    ext[:, 1:17, 7:8, :] = face_in[1]
    ext[3, 17, 7:8, :] = diag_in[0]
    ext[2, 0, 16:17, :] = diag_in[1]

    @pl.when(gx == 0)
    def _():
        ext[:, 0, :, :] = jnp.zeros((5, 24, NZ), jnp.float32)

    @pl.when(gx == ngx - 1)
    def _():
        ext[:, 17, :, :] = jnp.zeros((5, 24, NZ), jnp.float32)

    @pl.when(gy == 0)
    def _():
        ext[:, :, 7:8, :] = jnp.zeros((5, 18, 1, NZ), jnp.float32)

    @pl.when(gy == ngy - 1)
    def _():
        ext[:, :, 16:17, :] = jnp.zeros((5, 18, 1, NZ), jnp.float32)

    def source_part(i, carry):
        from_re, from_im, from_current = carry
        re, im = here(0, i), here(1, i)
        moved_re, moved_im, back_re, back_im, current = link(
            work[1, i], work[2, i], re, im, here(0, i, 1), here(1, i, 1)
        )
        up_re, up_im, _, _, up_current = link(
            work[3, i], work[4, i], re, im, here(0, i, 0, 1), here(1, i, 0, 1)
        )
        c, s = cos_sin(here(3, i, 0, -1))
        _, _, down_re, down_im, down_current = link(
            c, s, here(0, i, 0, -1), here(1, i, 0, -1), re, im
        )
        rates[0, i] += (moved_re + from_re) + (up_re + down_re)
        rates[1, i] += (moved_im + from_im) + (up_im + down_im)
        rates[2, i] = current
        rates[3, i] = up_current
        source = work[0, i] - (current - from_current) - (up_current - down_current)
        tile0[0, i + 3] = source
        part0[i + 4, 4:12] = source
        low_out[0, i] = source[0:4]
        high_out[0, i] = source[4:8]
        return back_re, back_im, current

    c, s = cos_sin(here(2, -1))
    _, _, back_re, back_im, current = link(
        c, s, here(0, -1), here(1, -1), here(0, 0), here(1, 0)
    )
    lax.fori_loop(0, TX, source_part, (back_re, back_im, current), unroll=True)

    def exchange0(kind):
        tile, low, high = tile0.at[kind], low_out.at[kind], high_out.at[kind]
        low_to, high_to = low_in.at[kind], high_in.at[kind]
        sems = level0_sem.at[kind]
        return [
            push(low, high_to.at[3:19], 0, -1, sems, 0),
            push(high, low_to.at[3:19], 0, 1, sems, 1),
            push(tile.at[3:6], tile.at[19:22], -1, 0, sems, 2),
            push(tile.at[16:19], tile.at[0:3], 1, 0, sems, 3),
            push(low.at[0:3], high_to.at[19:22], -1, -1, sems, 4),
            push(low.at[13:16], high_to.at[0:3], 1, -1, sems, 5),
            push(high.at[0:3], low_to.at[19:22], -1, 1, sems, 6),
            push(high.at[13:16], low_to.at[0:3], 1, 1, sems, 7),
        ]

    def exchange1(kind):
        tile = tile1.at[kind]
        sems = level1_sem.at[kind]
        own = tile.at[4:12, 8:16]
        first, last = tile.at[4:8, 8:16], tile.at[8:12, 8:16]
        return [
            push(own, tile.at[4:12, 16:24], 0, -1, sems, 0),
            push(own, tile.at[4:12, 0:8], 0, 1, sems, 1),
            push(first, tile.at[12:16, 8:16], -1, 0, sems, 2),
            push(last, tile.at[0:4, 8:16], 1, 0, sems, 3),
            push(first, tile.at[12:16, 16:24], -1, -1, sems, 4),
            push(last, tile.at[0:4, 16:24], 1, -1, sems, 5),
            push(first, tile.at[12:16, 0:8], -1, 1, sems, 6),
            push(last, tile.at[0:4, 0:8], 1, 1, sems, 7),
        ]

    def exchange2():
        copies = []
        for dy in (-3, 3, -2, 2, -1, 1, 0):
            for dx in (-1, 1, 0, -2, 2):
                if (dx or dy) and (abs(dx) < 2 or abs(dy) < 2):
                    target = got2.at[2 - dx, 3 - dy]
                    copies.append(push(got2.at[2, 3], target, dx, dy, level2_sem, len(copies)))
        return copies

    def unpack2():
        for across in range(5):
            for place in range(7):
                if across in (0, 4) and abs(place - 3) > 1:
                    continue
                for x in range(4):
                    slab = 4 * across + x - 2
                    if 0 <= slab < 16:
                        src2[slab, 2 * place : 2 * place + 2] = got2[
                            across, place, 2 * x : 2 * x + 2
                        ]

    def assemble0(kind):
        def one(slab):
            src0[kind, slab, 0:4] = low_in[kind, slab]
            src0[kind, slab, 4:12] = tile0[kind, slab]
            src0[kind, slab, 12:16] = high_in[kind, slab]

        each(0, 22, one)

    level0 = (22, 16, 4, 8, 1, 1, 16, 3)
    level1 = (16, 24, 8, 8, 2, 2, 8, 4)
    level2 = (16, 16, 6, 2, 1, 4, 4, 6)
    spread0 = (24, 16, 4, 8, 1, 1, 16, 4)
    spread1 = (20, 16, 6, 4, 1, 2, 8, 6)
    spread2 = (20, 16, 6, 2, 1, 4, 4, 8)

    def inside(level, slab):
        place = gx * level[6] + (slab - level[7])
        return jnp.logical_and(place >= 0, place < ngx * level[6])

    def gain_at(level, slab):
        return jnp.where(inside(level, slab), GAIN, 0.0)

    def edge_masks(level, row, rows):
        own_row, own_rows, step = level[2:5]
        place = lax.broadcasted_iota(jnp.int32, (rows, NZ), 0) + (gy * own_rows + (row - own_row))
        at_top = jnp.logical_and(place >= ngy * own_rows - step, place < ngy * own_rows)
        at_low = jnp.logical_and(place >= 0, place < step)
        return at_top, at_low

    def around(level, masks, ref, slab, row, rows):
        step, lanes = level[4:6]
        row = row + 8
        centre = ref[slab, row : row + rows]
        above = jnp.where(masks[0], centre, ref[slab, row + step : row + step + rows])
        below = jnp.where(masks[1], centre, ref[slab, row - step : row - step + rows])
        right = jnp.where(lane >= NZ - lanes, centre, pltpu.roll(centre, NZ - lanes, 1))
        left = jnp.where(lane < lanes, centre, pltpu.roll(centre, lanes, 1))
        along = ref[slab + 1, row : row + rows] + ref[slab - 1, row : row + rows]
        return centre, along + (above + below) + (left + right)

    def sweep(level, ref, to, source, first, last):
        rows = level[1]
        masks = edge_masks(level, 0, rows)

        def one(slab):
            centre, total = around(level, masks, ref, slab, 0, rows)
            fresh = KEEP * centre + gain_at(level, slab) * (total + source[slab])
            to[slab, 8 : 8 + rows] = fresh

        each(first, last, one)

    def smooth_down(level, source, va, vb):
        slabs, rows = level[:2]

        def one(slab):
            va[slab, 8 : 8 + rows] = gain_at(level, slab) * source[slab]

        each(0, slabs, one)
        sweep(level, va, vb, source, 1, slabs - 1)
        sweep(level, vb, va, source, 2, slabs - 2)

    def restrict_to(level, source, ref, visit):
        row, _, step, lanes, tile, margin = level[2:8]
        masks = edge_masks(level, row, TY)
        odd_row = lax.rem(lax.div(row8, step), 2) == 1
        odd_lane = lax.rem(lax.div(lane, lanes), 2) == 1

        def rest(slab):
            centre, total = around(level, masks, ref, slab, row, TY)
            return source[slab, row : row + TY] + total - 6.0 * centre

        def one(pair):
            total = rest(margin + 2 * pair) + rest(margin + 1 + 2 * pair)
            total = total + jnp.where(
                odd_row, pltpu.roll(total, step, 0), pltpu.roll(total, TY - step, 0)
            )
            total = total + jnp.where(
                odd_lane, pltpu.roll(total, lanes, 1), pltpu.roll(total, NZ - lanes, 1)
            )
            visit(pair, 0.5 * total)

        each(0, tile // 2, one)

    def smooth_up(level, start, source, va, vb, first=0):
        slabs, rows = level[:2]

        def one(slab):
            va[slab, 8 : 8 + rows] = jnp.where(inside(level, slab), start(slab), 0.0)

        each(first, slabs - first, one)
        sweep(level, va, vb, source, first + 1, slabs - first - 1)
        sweep(level, vb, va, source, first + 2, slabs - first - 2)

    def spread_down(level, source, va, vb, first, last):
        slabs, rows = level[:2]

        def one(slab):
            va[slab, 8 : 8 + rows] = gain_at(level, slab) * source[slab]

        each(first, last, one)
        sweep(level, va, vb, source, first - 1, last + 1)
        sweep(level, vb, va, source, first - 2, last + 2)
        masks = edge_masks(level, 0, rows)

        def rest(slab):
            centre, total = around(level, masks, va, slab, 0, rows)
            return source[slab] + total - 6.0 * centre

        begin, end = first - 3, last + 3
        pairs = list(range(begin // 2, (end + 1) // 2))
        for pair in pairs:
            both = [rest(slab) for slab in (2 * pair, 2 * pair + 1) if begin <= slab < end]
            folded[pair] = both[0] + both[1] if len(both) == 2 else both[0]
        return pairs

    def fold(level, pairs, visit):
        lanes = level[5]
        odd_lane = lax.rem(lax.div(lane, lanes), 2) == 1
        for place, pair in enumerate(pairs):
            total = folded[pair, pl.ds(0, 8, 2)] + folded[pair, pl.ds(1, 8, 2)]
            total = total + jnp.where(
                odd_lane, pltpu.roll(total, lanes, 1), pltpu.roll(total, NZ - lanes, 1)
            )
            visit(place, 0.5 * total)

    near0 = exchange0(0)
    hear(relays_x, 0, 1)
    tell(relays_x, 0, 2)

    def to_part1(place, values):
        part1[place + 4, 4:12] = values

    def to_part2(place, values):
        part2[place + 5, 3:11] = values

    fold(spread0, spread_down(spread0, part0, pa0, pb0, 4, 20), to_part1)
    fold(spread1, spread_down(spread1, part1, pa1, pb1, 4, 16), to_part2)
    spread_down(spread2, part2, pa2, pb2, 5, 15)
    modes = product(
        halves(folded[1:9].reshape(8 * 16, NZ)), (along_z[0], along_z[1])
    ).reshape(8, 16, NZ)
    row16 = lax.broadcasted_iota(jnp.int32, (16, NZ), 0)
    lane16 = lax.div(lax.broadcasted_iota(jnp.int32, (16, NZ), 1), 16)
    group_of = lax.rem(gy + 5 + lax.div(row16, 2), 8)
    gather1[gy] = jnp.sum(jnp.where((lane16 == group_of)[None], modes, 0.0), axis=1)

    def spread(ref, mine, count, target, place):
        def one(step):
            return pltpu.make_async_remote_copy(
                src_ref=ref.at[mine],
                dst_ref=ref.at[mine],
                send_sem=gather_sem.at[0, place],
                recv_sem=gather_sem.at[1, place],
                device_id=target(lax.rem(mine + step, count)),
                device_id_type=MESH,
            )

        @pl.loop(0, count - 1)
        def _(turn):
            away = lax.div(turn + 1, 2)
            one(count // 2 + away * (2 * lax.rem(turn, 2) - 1)).start()

        rest_of = ref.at[0 : count - 1]
        return pltpu.make_async_remote_copy(
            src_ref=rest_of,
            dst_ref=rest_of,
            send_sem=gather_sem.at[0, place],
            recv_sem=gather_sem.at[1, place],
            device_id=target(lax.rem(mine + 1, count)),
            device_id_type=MESH,
        )

    hear(relays_y, 4, 1)
    along = spread(gather1, gy, ngy, lambda other: (gx, other), 0)
    hear(relays_x, 0, 2)
    tell(relays_x, 0, 3)

    def flux_xy(i, dx, dy):
        return (here(3, i, dx + 1, dy) - here(3, i, dx, dy)) - (
            here(2, i, dx, dy + 1) - here(2, i, dx, dy)
        )

    def flux_yz(i, dy):
        a_y = here(3, i, 0, dy)
        return (here(4, i, 0, dy + 1) - here(4, i, 0, dy)) - (ahead_z(a_y) - a_y)

    def flux_zx(i, dx):
        a_x = here(2, i, dx, 0)
        return (ahead_z(a_x) - a_x) - (here(4, i, dx + 1, 0) - here(4, i, dx, 0))

    def rate_part(i):
        re, im = here(0, i), here(1, i)
        condense = pin[i] - (re * re + im * im) - 6.0
        rates[0, i] += condense * re
        rates[1, i] += condense * im
        under_x = jnp.where(lane == 0, here(2, i), 0.0)
        under_y = jnp.where(lane == 0, here(3, i), 0.0)
        xy, yz, zx = flux_xy(i, 0, 0), flux_yz(i, 0), flux_zx(i, 0)
        rates[2, i] -= KAPPA2 * ((xy - flux_xy(i, 0, -1)) - (zx - (behind_z(zx) + under_x)))
        rates[3, i] -= KAPPA2 * ((yz - (behind_z(yz) - under_y)) - (xy - flux_xy(i, -1, 0)))
        rates[4, i] -= KAPPA2 * ((zx - flux_zx(i, -1)) - (yz - flux_yz(i, -1)))

    each(0, TX, rate_part)

    receive(near0)
    assemble0(0)
    smooth_down(level0, src0.at[0], va0, vb0)

    def to_level1(pair, values):
        tile1[0, pair + 4, 8:16] = values

    restrict_to(level0, src0.at[0], va0, to_level1)
    near1 = exchange1(0)

    def keep0(i):
        values = va0[i + 3, 12:20]
        tile0[1, i + 3] = values
        low_out[1, i] = values[0:4]
        high_out[1, i] = values[4:8]

    each(0, TX, keep0)
    late0 = exchange0(1)

    along.wait_recv()
    groups = max(1, ngy // 8)
    chip, core = lax.div(gx, 2), lax.rem(gx, 2)
    lane8 = lax.div(lax.broadcasted_iota(jnp.int32, (8, NZ), 1), 16)
    for group in range(groups):
        total = jnp.zeros((8, NZ), jnp.float32)
        for sender in range(ngy):
            low, high = sender - 3 - 8 * group, sender + 3 - 8 * group
            if high >= 0 and low < 8:
                held = jnp.logical_and(lane8 >= low, lane8 <= high)
                total = total + jnp.where(held, gather1[sender], 0.0)
        gather2[core, chip, :, 128 * group : 128 * group + 128] = total
    hear(relays_x, 0, 3)
    across = spread(
        gather2.at[core], chip, ngx // 2, lambda other: (2 * other + core, gy), 1
    )

    receive(near1)
    smooth_down(level1, tile1.at[0], va1, vb1)

    def to_level2(pair, values):
        got2[2, 3, pl.ds(2 * pair, 1)] = values[0:1]
        got2[2, 3, pl.ds(2 * pair + 1, 1)] = values[4:5]

    restrict_to(level1, tile1.at[0], va1, to_level2)
    near2 = exchange2()

    def keep1(i):
        tile1[1, i + 4, 8:16] = va1[i + 4, 16:24]

    each(0, 8, keep1)
    late1 = exchange1(1)

    across.wait_recv()
    swap = pltpu.make_async_remote_copy(
        src_ref=gather2.at[core],
        dst_ref=gather2.at[core],
        send_sem=gather_sem.at[0, 2],
        recv_sem=gather_sem.at[1, 2],
        device_id=(gx + 1 - 2 * core, gy),
        device_id_type=MESH,
    )
    swap.start()
    swap.wait_recv()
    shares = gather2[...].reshape(8 * ngx, 128 * groups)
    spectral = product((along_x[0], along_x[1]), halves(shares))
    spectral = product(halves(spectral), (along_y[0], along_y[1])) * inverse[...]
    spectral = product((back_x[0, :, : 2 * ngx], back_x[1, :, : 2 * ngx]), halves(spectral))
    spectral = halves(spectral)
    for place in range(5):
        column = product(spectral, (back_yz[0, place], back_yz[1, place]))
        for x in range(6):
            coarse[x, 2 * place + 2 : 2 * place + 4] = column[2 * x : 2 * x + 2]

    receive(near2)
    unpack2()
    smooth_down(level2, src2, va2, vb2)
    smooth_up(
        level2,
        lambda slab: va2[slab, 8:24] + coarse[lax.div(slab, 2) - 1],
        src2,
        va2,
        vb2,
        first=2,
    )
    receive(late1)

    def start1(slab):
        x = lax.div(slab, 2) + 4
        parts = []
        for place in range(3):
            row = 12 + 2 * place
            parts.append(jnp.where(row8 < 4, va2[x, row : row + 1], va2[x, row + 1 : row + 2]))
        return tile1[1, slab] + jnp.concatenate(parts, 0)

    smooth_up(level1, start1, tile1.at[0], va1, vb1)
    receive(late0)
    assemble0(1)
    smooth_up(
        level0,
        lambda slab: src0[1, slab] + va1[lax.div(slab + 1, 2) + 2, 12:28],
        src0.at[0],
        va0,
        vb0,
    )

    not_top = jnp.logical_or(row8 < TY - 1, gy < ngy - 1)

    def finish(i):
        potential = va0[i + 3, 12:20]
        above = jnp.where(not_top, va0[i + 3, 13:21], 0.0)
        potential_ref[i] = potential
        re, im = here(0, i), here(1, i)
        out_ref[0, i] = re + DT * (rates[0, i] + potential * im)
        out_ref[1, i] = im + DT * (rates[1, i] - potential * re)
        out_ref[2, i] = here(2, i) + DT * (rates[2, i] - (va0[i + 4, 12:20] - potential))
        out_ref[3, i] = here(3, i) + DT * (rates[3, i] - (above - potential))
        out_ref[4, i] = here(4, i) + DT * (rates[4, i] - (ahead_z(potential) - potential))

    each(0, TX, finish)

    for copy, outward in sent:
        pl.when(outward)(lambda: copy.wait_send())
    along.wait_send()
    across.wait_send()
    swap.wait_send()


def solution(mesh):
    ngx, ngy = mesh.shape["gx"], mesh.shape["gy"]
    tables = coarse_tables(ngx, ngy)
    groups = max(1, ngy // 8)
    width = 128 * groups
    f32, bf16 = jnp.float32, jnp.bfloat16
    vmem, dma = pltpu.VMEM, pltpu.SemaphoreType.DMA

    def body(state, pinning, lead_values):
        return pl.pallas_call(
            functools.partial(kernel, ngx, ngy),
            out_shape=(vmem(state.shape, f32), vmem(pinning.shape, f32)),
            in_specs=[pl.BlockSpec(memory_space=pltpu.HBM)] * 9,
            out_specs=(
                pl.BlockSpec(memory_space=pltpu.VMEM),
                pl.BlockSpec(memory_space=pltpu.VMEM),
            ),
            scratch_shapes=[
                vmem((5, TX + 2, 24, NZ), f32),
                vmem((TX, TY, NZ), f32),
                vmem((2, TY, NZ), f32),
                vmem(tables[0].shape, bf16),
                vmem(tables[1].shape, bf16),
                vmem(tables[2].shape, bf16),
                vmem(tables[3].shape, f32),
                vmem((2, 16, 128), bf16),
                vmem((2, 5, width, 128), bf16),
                vmem((2, 5, TX, 1, NZ), f32),
                vmem((2, 5, TX, 1, NZ), f32),
                vmem((2, 1, NZ), f32),
                vmem((5, TX, TY, NZ), f32),
                vmem((5, TX, TY, NZ), f32),
                vmem((2, 22, TY, NZ), f32),
                vmem((2, TX, 4, NZ), f32),
                vmem((2, TX, 4, NZ), f32),
                vmem((2, 22, 4, NZ), f32),
                vmem((2, 22, 4, NZ), f32),
                vmem((2, 22, 16, NZ), f32),
                vmem((22, 32, NZ), f32),
                vmem((22, 32, NZ), f32),
                vmem((2, 16, 24, NZ), f32),
                vmem((16, 40, NZ), f32),
                vmem((16, 40, NZ), f32),
                vmem((5, 7, TY, NZ), f32),
                vmem((16, 16, NZ), f32),
                vmem((16, 32, NZ), f32),
                vmem((16, 32, NZ), f32),
                vmem((24, 16, NZ), f32),
                vmem((24, 32, NZ), f32),
                vmem((24, 32, NZ), f32),
                vmem((20, 16, NZ), f32),
                vmem((20, 32, NZ), f32),
                vmem((20, 32, NZ), f32),
                vmem((20, 16, NZ), f32),
                vmem((20, 32, NZ), f32),
                vmem((20, 32, NZ), f32),
                vmem((12, 16, NZ), f32),
                vmem((6, 16, NZ), f32),
                vmem((ngy, 8, NZ), f32),
                vmem((2, ngx // 2, 8, width), f32),
                dma((8,)),
                dma,
                dma((2, 6)),
                dma((2, 2, 8)),
                dma((2, 2, 8)),
                dma((2, 26)),
                dma((2, 3)),
                pltpu.SemaphoreType.REGULAR((6, 2)),
            ],
            compiler_params=pltpu.CompilerParams(
                collective_id=0, has_side_effects=True, vmem_limit_bytes=60 * 1024 * 1024
            ),
            name="film_step",
        )(state, pinning, lead_values, *[jnp.asarray(table) for table in tables])
    placed = (P(None, "gx", "gy", None), P("gx", "gy", None), P(None, "gy", None))
    return jax.shard_map(
        body,
        mesh=mesh,
        in_specs=placed,
        out_specs=(P(None, "gx", "gy", None), P("gx", "gy", None)),
        check_vma=False,
    )
```

```python
import functools
import math

import jax
import jax.numpy as jnp
import ml_dtypes
import numpy as np
from jax import lax
from jax.experimental import pallas as pl
from jax.experimental.pallas import tpu as pltpu
from jax.sharding import PartitionSpec as P

MESH = pl.DeviceIdType.MESH
OMEGA = 0.8
DT = 0.05
KAPPA2 = 2.0
KEEP = 1.0 - OMEGA
GAIN = OMEGA / 6.0
TX, TY, NZ = 16, 8, 128


def chebyshev_powers(function, terms):
    fit = np.polynomial.chebyshev.Chebyshev.interpolate(
        lambda u: function(np.sqrt(np.maximum(8.0 * (u + 1.0), 0.0))), terms, domain=[-1, 1]
    )
    return [float(c) for c in np.polynomial.chebyshev.cheb2poly(fit.coef)]


COS_POWERS = chebyshev_powers(np.cos, 8)
SIN_POWERS = chebyshev_powers(lambda a: np.sinc(a / np.pi), 8)


def horner(powers, u):
    total = powers[-1] * u + powers[-2]
    for power in powers[-3::-1]:
        total = total * u + power
    return total


def cos_sin(angle):
    u = angle * angle * 0.125 - 1.0
    return horner(COS_POWERS, u), horner(SIN_POWERS, u) * angle


def sine_table(count):
    modes = np.arange(1, count + 1, dtype=np.float64)
    return np.sqrt(2.0 / (count + 1)) * np.sin(np.pi / (count + 1) * modes[:, None] * modes[None])


def sine_values(count):
    return 2.0 - 2.0 * np.cos(np.pi / (count + 1) * np.arange(1, count + 1, dtype=np.float64))


def cosine_table(count):
    modes = np.arange(count, dtype=np.float64)
    weights = np.where(modes == 0.0, 1.0, 2.0) / count
    return np.sqrt(weights)[:, None] * np.cos(
        np.pi / count * modes[:, None] * (modes[None] + 0.5)
    )


def cosine_values(count):
    return 2.0 - 2.0 * np.cos(np.pi / count * np.arange(count, dtype=np.float64))


def split_pair(table):
    high = table.astype(ml_dtypes.bfloat16)
    low = (table - high.astype(np.float64)).astype(ml_dtypes.bfloat16)
    return np.stack([high, low])


def coarse_tables(ngx, ngy):
    nx, ny, nz = 2 * ngx, ngy, 16
    groups = max(1, ngy // 8)
    width = 128 * groups
    tx, ty, tz = sine_table(nx), cosine_table(ny), cosine_table(nz)
    lanes = np.arange(128)
    along_z = np.tile(tz[:, lanes // 8].T / 8.0, (1, 8))
    along_x = np.zeros((nx, ngx, 8))
    for cell in range(8):
        place = 2 * np.arange(ngx) + cell - 3
        within = (place >= 0) & (place < nx)
        along_x[:, within, cell] = tx[:, place[within]]
    along_x = along_x.reshape(nx, ngx // 2, 2, 8).swapaxes(1, 2).reshape(nx, 8 * ngx)
    along_y = np.zeros((width, width))
    inverse = np.zeros((nx, width))
    values = (
        sine_values(nx)[:, None, None]
        + cosine_values(ny)[None, :, None]
        + cosine_values(nz)[None, None, :]
    )
    inverse[:, : ny * nz] = (1.0 / values).reshape(nx, ny * nz)
    along_y[: ny * nz, : ny * nz] = np.kron(ty.T, np.eye(nz))
    back_x = np.zeros((ngx, 16, 128))
    for cell in range(12):
        place = 2 * np.arange(ngx) + cell // 2 - 2
        within = (place >= 0) & (place < nx)
        back_x[within, cell, :nx] = tx.T[place[within]]
    back_yz = np.zeros((ny + 4, width, 128))
    for y in range(ny):
        back_yz[2 + y, : ny * nz] = np.kron(ty[:, y : y + 1], tz[:, lanes // 8])
    return (
        split_pair(along_z),
        split_pair(along_x),
        split_pair(along_y),
        inverse.astype(np.float32),
        split_pair(back_x),
        split_pair(back_yz),
    )


def halves(values):
    high = values.astype(jnp.bfloat16)
    return high, (values - high.astype(jnp.float32)).astype(jnp.bfloat16)


def product(left, right):
    dot = functools.partial(jnp.dot, preferred_element_type=jnp.float32)
    return dot(left[0], right[0]) + (dot(left[0], right[1]) + dot(left[1], right[0]))


def kernel(
    ngx,
    ngy,
    state_ref,
    pinning_ref,
    lead_ref,
    along_z_ref,
    along_x_ref,
    along_y_ref,
    inverse_ref,
    back_x_ref,
    back_yz_ref,
    out_ref,
    potential_ref,
    ext,
    pin,
    lead,
    along_z,
    along_x,
    along_y,
    inverse,
    back_x,
    back_yz,
    face_out,
    face_in,
    diag_in,
    rates,
    work,
    tile0,
    low_out,
    high_out,
    low_in,
    high_in,
    src0,
    va0,
    vb0,
    tile1,
    va1,
    vb1,
    share,
    got_share,
    got2,
    src2,
    va2,
    vb2,
    part0,
    pa0,
    pb0,
    part1,
    pa1,
    pb1,
    part2,
    pa2,
    pb2,
    folded,
    coarse,
    gather1,
    gather2,
    local_sem,
    state_sem,
    halo_sem,
    level0_sem,
    level1_sem,
    share_sem,
    level2_sem,
    gather_sem,
    relay_sem,
):
    gx, gy = lax.axis_index("gx"), lax.axis_index("gy")

    def device(dx, dy):
        return (lax.rem(gx + dx % ngx, ngx), lax.rem(gy + dy % ngy, ngy))

    def each(first, last, visit):
        def one(place, carry):
            visit(place)
            return carry

        lax.fori_loop(first, last, one, 0, unroll=True)

    own_state = pltpu.make_async_copy(state_ref, ext.at[:, 1:17, 8:16], state_sem)
    own_state.start()
    got_share[...] = jnp.zeros(got_share.shape, jnp.float32)
    barrier = pltpu.get_barrier_semaphore()
    def within(dx, dy):
        tests = [gx >= -dx] * (dx < 0) + [gx < ngx - dx] * (dx > 0)
        tests += [gy >= -dy] * (dy < 0) + [gy < ngy - dy] * (dy > 0)
        return functools.reduce(jnp.logical_and, tests)

    near = [
        (dx, dy)
        for dy in range(-4, 5)
        for dx in range(-2, 3)
        if (dx or dy) and abs(dx) * abs(dy) < 4 and (dx == 0 or abs(dy) < 4)
    ]
    for dx, dy in near:

        @pl.when(within(dx, dy))
        def _():
            pl.semaphore_signal(
                barrier, inc=1, device_id=device(dx, dy), device_id_type=MESH
            )

    present = sum(within(dx, dy).astype(jnp.int32) for dx, dy in near)

    locals_ = [
        pltpu.make_async_copy(source, target, local_sem.at[place])
        for place, (source, target) in enumerate(
            [
                (pinning_ref, pin),
                (lead_ref, lead),
                (along_z_ref, along_z),
                (along_x_ref, along_x),
                (along_y_ref, along_y),
                (inverse_ref, inverse),
                (back_x_ref.at[:, gx], back_x),
                (back_yz_ref.at[:, pl.ds(gy, 5)], back_yz),
            ]
        )
    ]
    for ref in (part0, pa0, pb0, part1, pa1, pb1, part2, pa2, pb2):
        ref[...] = jnp.zeros(ref.shape, jnp.float32)

    def clear(*refs):
        for ref in refs:
            ref[...] = jnp.zeros(ref.shape, jnp.float32)

    @pl.when(gx == 0)
    def _():
        clear(tile0.at[:, 0:3], low_in.at[:, 0:3], high_in.at[:, 0:3])
        clear(tile1.at[:, 0:4], got2.at[0:2])

    @pl.when(gx == 1)
    def _():
        clear(got2.at[0:1])

    @pl.when(gx == ngx - 1)
    def _():
        clear(tile0.at[:, 19:22], low_in.at[:, 19:22], high_in.at[:, 19:22])
        clear(tile1.at[:, 12:16], got2.at[3:5])

    @pl.when(gx == ngx - 2)
    def _():
        clear(got2.at[4:5])

    for place in range(3):

        @pl.when(gy == place)
        def _():
            clear(got2.at[:, 0 : 3 - place])

        @pl.when(gy == ngy - 1 - place)
        def _():
            clear(got2.at[:, 4 + place : 7])

    @pl.when(gy == 0)
    def _():
        clear(low_in, tile1.at[:, :, 0:8])

    @pl.when(gy == ngy - 1)
    def _():
        clear(high_in, tile1.at[:, :, 16:24])

    own_state.wait()
    face_out[0] = ext[:, 1:17, 8:9, :]
    face_out[1] = ext[:, 1:17, 15:16, :]
    pl.semaphore_wait(barrier, present)

    sent = []

    def push(source, target, dx, dy, sems, place):
        copy = pltpu.make_async_remote_copy(
            src_ref=source,
            dst_ref=target,
            send_sem=sems.at[0, place],
            recv_sem=sems.at[1, place],
            device_id=device(dx, dy),
            device_id_type=MESH,
        )
        outward = within(dx, dy)
        pl.when(outward)(lambda: copy.start())
        sent.append((copy, outward))
        return copy, within(-dx, -dy)

    def receive(copies):
        for copy, inward in copies:
            pl.when(inward)(lambda: copy.wait_recv())

    halo = [
        push(face_out.at[0], face_in.at[0], 0, -1, halo_sem, 0),
        push(face_out.at[1], face_in.at[1], 0, 1, halo_sem, 1),
        push(ext.at[:, 1, 8:16], ext.at[:, 17, 8:16], -1, 0, halo_sem, 2),
        push(ext.at[:, 16, 8:16], ext.at[:, 0, 8:16], 1, 0, halo_sem, 3),
        push(face_out.at[1, 3, 0], diag_in.at[0], -1, 1, halo_sem, 4),
        push(face_out.at[0, 2, 15], diag_in.at[1], 1, -1, halo_sem, 5),
    ]
    for copy in locals_:
        copy.start()

    def relays(reach, count):
        steps = []
        while reach < count - 1:
            steps.append(reach)
            reach *= 2
        return steps

    relays_x = [(reach, 0) for reach in relays(2, ngx)]
    relays_y = [(0, reach) for reach in relays(4, ngy)]

    def tell(steps, first, place):
        if place < len(steps):
            dx, dy = steps[place]
            for side, sign in enumerate((-1, 1)):

                @pl.when(within(sign * dx, sign * dy))
                def _():
                    pl.semaphore_signal(
                        relay_sem.at[first + place, side],
                        inc=1,
                        device_id=device(sign * dx, sign * dy),
                        device_id_type=MESH,
                    )

    def hear(steps, first, place):
        if place < len(steps):
            dx, dy = steps[place]
            for side, sign in enumerate((-1, 1)):

                @pl.when(within(-sign * dx, -sign * dy))
                def _():
                    pl.semaphore_wait(relay_sem.at[first + place, side], 1)

    tell(relays_y, 4, 0)
    tell(relays_x, 0, 0)

    lane = lax.broadcasted_iota(jnp.int32, (1, NZ), 1)
    row8 = lax.broadcasted_iota(jnp.int32, (TY, NZ), 0)

    def ahead_z(values):
        return jnp.where(lane == NZ - 1, 0.0, pltpu.roll(values, NZ - 1, 1))

    def behind_z(values):
        return jnp.where(lane == 0, 0.0, pltpu.roll(values, 1, 1))

    def here(field, slab, dx=0, dy=0):
        return ext[field, slab + (1 + dx), 8 + dy : 16 + dy, :]

    def link(c, s, re, im, next_re, next_im):
        moved_re = c * next_re + s * next_im
        moved_im = c * next_im - s * next_re
        current = re * moved_im - im * moved_re
        return moved_re, moved_im, c * re - s * im, c * im + s * re, current

    def own_part(i):
        re, im = here(0, i), here(1, i)
        c, s = cos_sin(here(4, i))
        moved_re, moved_im, back_re, back_im, current = link(
            c, s, re, im, ahead_z(re), ahead_z(im)
        )
        rates[0, i] = moved_re + behind_z(back_re)
        rates[1, i] = moved_im + behind_z(back_im)
        rates[4, i] = current
        work[0, i] = behind_z(current) - current
        work[1, i], work[2, i] = cos_sin(here(2, i))
        work[3, i], work[4, i] = cos_sin(here(3, i))

    each(0, TX, own_part)
    hear(relays_y, 4, 0)
    tell(relays_y, 4, 1)
    hear(relays_x, 0, 0)
    tell(relays_x, 0, 1)
    for copy in locals_:
        copy.wait()
    work[0, 0] += jnp.where(gx == 0, 1.0, 0.0) * lead[0]
    work[0, TX - 1] += jnp.where(gx == ngx - 1, 1.0, 0.0) * lead[1]

    receive(halo)
    ext[:, 1:17, 16:17, :] = face_in[0]
    ext[:, 1:17, 7:8, :] = face_in[1]
    ext[3, 17, 7:8, :] = diag_in[0]
    ext[2, 0, 16:17, :] = diag_in[1]

    @pl.when(gx == 0)
    def _():
        ext[:, 0, :, :] = jnp.zeros((5, 24, NZ), jnp.float32)

    @pl.when(gx == ngx - 1)
    def _():
        ext[:, 17, :, :] = jnp.zeros((5, 24, NZ), jnp.float32)

    @pl.when(gy == 0)
    def _():
        ext[:, :, 7:8, :] = jnp.zeros((5, 18, 1, NZ), jnp.float32)

    @pl.when(gy == ngy - 1)
    def _():
        ext[:, :, 16:17, :] = jnp.zeros((5, 18, 1, NZ), jnp.float32)

    def source_part(i, carry):
        from_re, from_im, from_current = carry
        re, im = here(0, i), here(1, i)
        moved_re, moved_im, back_re, back_im, current = link(
            work[1, i], work[2, i], re, im, here(0, i, 1), here(1, i, 1)
        )
        up_re, up_im, _, _, up_current = link(
            work[3, i], work[4, i], re, im, here(0, i, 0, 1), here(1, i, 0, 1)
        )
        c, s = cos_sin(here(3, i, 0, -1))
        _, _, down_re, down_im, down_current = link(
            c, s, here(0, i, 0, -1), here(1, i, 0, -1), re, im
        )
        rates[0, i] += (moved_re + from_re) + (up_re + down_re)
        rates[1, i] += (moved_im + from_im) + (up_im + down_im)
        rates[2, i] = current
        rates[3, i] = up_current
        source = work[0, i] - (current - from_current) - (up_current - down_current)
        tile0[0, i + 3] = source
        part0[i + 4, 12:20] = source
        low_out[0, i] = source[0:4]
        high_out[0, i] = source[4:8]
        return back_re, back_im, current

    c, s = cos_sin(here(2, -1))
    _, _, back_re, back_im, current = link(
        c, s, here(0, -1), here(1, -1), here(0, 0), here(1, 0)
    )
    lax.fori_loop(0, TX, source_part, (back_re, back_im, current), unroll=True)

    def exchange0(kind):
        tile, low, high = tile0.at[kind], low_out.at[kind], high_out.at[kind]
        low_to, high_to = low_in.at[kind], high_in.at[kind]
        sems = level0_sem.at[kind]
        return [
            push(low, high_to.at[3:19], 0, -1, sems, 0),
            push(high, low_to.at[3:19], 0, 1, sems, 1),
            push(tile.at[3:6], tile.at[19:22], -1, 0, sems, 2),
            push(tile.at[16:19], tile.at[0:3], 1, 0, sems, 3),
            push(low.at[0:3], high_to.at[19:22], -1, -1, sems, 4),
            push(low.at[13:16], high_to.at[0:3], 1, -1, sems, 5),
            push(high.at[0:3], low_to.at[19:22], -1, 1, sems, 6),
            push(high.at[13:16], low_to.at[0:3], 1, 1, sems, 7),
        ]

    def exchange1(kind):
        tile = tile1.at[kind]
        sems = level1_sem.at[kind]
        own = tile.at[4:12, 8:16]
        first, last = tile.at[4:8, 8:16], tile.at[8:12, 8:16]
        return [
            push(own, tile.at[4:12, 16:24], 0, -1, sems, 0),
            push(own, tile.at[4:12, 0:8], 0, 1, sems, 1),
            push(first, tile.at[12:16, 8:16], -1, 0, sems, 2),
            push(last, tile.at[0:4, 8:16], 1, 0, sems, 3),
            push(first, tile.at[12:16, 16:24], -1, -1, sems, 4),
            push(last, tile.at[0:4, 16:24], 1, -1, sems, 5),
            push(first, tile.at[12:16, 0:8], -1, 1, sems, 6),
            push(last, tile.at[0:4, 0:8], 1, 1, sems, 7),
        ]

    def exchange2():
        copies = []
        for dy in (-3, 3, -2, 2, -1, 1, 0):
            for dx in (-1, 1, 0, -2, 2):
                if (dx or dy) and (abs(dx) < 2 or abs(dy) < 2):
                    target = got2.at[2 - dx, 3 - dy]
                    copies.append(push(got2.at[2, 3], target, dx, dy, level2_sem, len(copies)))
        return copies

    def unpack2():
        for across in range(5):
            for place in range(7):
                if across in (0, 4) and abs(place - 3) > 1:
                    continue
                for x in range(4):
                    slab = 4 * across + x - 2
                    if 0 <= slab < 16:
                        src2[slab, 2 * place : 2 * place + 2] = got2[
                            across, place, 2 * x : 2 * x + 2
                        ]

    def assemble0(kind):
        def one(slab):
            src0[kind, slab, 0:4] = low_in[kind, slab]
            src0[kind, slab, 4:12] = tile0[kind, slab]
            src0[kind, slab, 12:16] = high_in[kind, slab]

        each(0, 22, one)

    level0 = (22, 16, 4, 8, 1, 1, 16, 3)
    level1 = (16, 24, 8, 8, 2, 2, 8, 4)
    level2 = (16, 16, 6, 2, 1, 4, 4, 6)
    spread0 = (24, 16, 4, 8, 1, 1, 16, 4)
    spread1 = (20, 16, 6, 4, 1, 2, 8, 6)
    spread2 = (20, 16, 6, 2, 1, 4, 4, 8)

    def inside(level, slab):
        place = gx * level[6] + (slab - level[7])
        return jnp.logical_and(place >= 0, place < ngx * level[6])

    def gain_at(level, slab):
        return jnp.where(inside(level, slab), GAIN, 0.0)

    def edge_masks(level, row, rows):
        own_row, own_rows, step = level[2:5]
        place = lax.broadcasted_iota(jnp.int32, (rows, NZ), 0) + (gy * own_rows + (row - own_row))
        at_top = jnp.logical_and(place >= ngy * own_rows - step, place < ngy * own_rows)
        at_low = jnp.logical_and(place >= 0, place < step)
        return at_top, at_low

    def around(level, masks, ref, slab, row, rows):
        step, lanes = level[4:6]
        row = row + 8
        centre = ref[slab, row : row + rows]
        above = jnp.where(masks[0], centre, ref[slab, row + step : row + step + rows])
        below = jnp.where(masks[1], centre, ref[slab, row - step : row - step + rows])
        right = jnp.where(lane >= NZ - lanes, centre, pltpu.roll(centre, NZ - lanes, 1))
        left = jnp.where(lane < lanes, centre, pltpu.roll(centre, lanes, 1))
        along = ref[slab + 1, row : row + rows] + ref[slab - 1, row : row + rows]
        return centre, along + (above + below) + (left + right)

    def sweep(level, ref, to, source, first, last):
        rows = level[1]
        masks = edge_masks(level, 0, rows)

        def one(slab):
            centre, total = around(level, masks, ref, slab, 0, rows)
            fresh = KEEP * centre + gain_at(level, slab) * (total + source[slab])
            to[slab, 8 : 8 + rows] = fresh

        each(first, last, one)

    def smooth_down(level, source, va, vb):
        slabs, rows = level[:2]

        def one(slab):
            va[slab, 8 : 8 + rows] = gain_at(level, slab) * source[slab]

        each(0, slabs, one)
        sweep(level, va, vb, source, 1, slabs - 1)
        sweep(level, vb, va, source, 2, slabs - 2)

    def restrict_to(level, source, ref, visit):
        row, _, step, lanes, tile, margin = level[2:8]
        masks = edge_masks(level, row, TY)
        odd_row = lax.rem(lax.div(row8, step), 2) == 1
        odd_lane = lax.rem(lax.div(lane, lanes), 2) == 1

        def rest(slab):
            centre, total = around(level, masks, ref, slab, row, TY)
            return source[slab, row : row + TY] + total - 6.0 * centre

        def one(pair):
            total = rest(margin + 2 * pair) + rest(margin + 1 + 2 * pair)
            total = total + jnp.where(
                odd_row, pltpu.roll(total, step, 0), pltpu.roll(total, TY - step, 0)
            )
            total = total + jnp.where(
                odd_lane, pltpu.roll(total, lanes, 1), pltpu.roll(total, NZ - lanes, 1)
            )
            visit(pair, 0.5 * total)

        each(0, tile // 2, one)

    def smooth_up(level, start, source, va, vb, first=0):
        slabs, rows = level[:2]

        def one(slab):
            va[slab, 8 : 8 + rows] = jnp.where(inside(level, slab), start(slab), 0.0)

        each(first, slabs - first, one)
        sweep(level, va, vb, source, first + 1, slabs - first - 1)
        sweep(level, vb, va, source, first + 2, slabs - first - 2)

    def spread_down(level, source, va, vb, first, last):
        rows = level[1]
        masks = edge_masks(level, 0, rows)
        inner = source.at[:, 8 : 8 + rows]

        def two(slab):
            centre, total = around(level, masks, source, slab, 0, rows)
            fresh = gain_at(level, slab) * ((1.0 + KEEP) * centre + GAIN * total)
            vb[slab, 8 : 8 + rows] = fresh

        each(first - 1, last + 1, two)
        sweep(level, vb, va, inner, first - 2, last + 2)

        def rest(slab):
            centre, total = around(level, masks, va, slab, 0, rows)
            return inner[slab] + total - 6.0 * centre

        begin, end = first - 3, last + 3
        pairs = list(range(begin // 2, (end + 1) // 2))
        for pair in pairs:
            both = [rest(slab) for slab in (2 * pair, 2 * pair + 1) if begin <= slab < end]
            folded[pair] = both[0] + both[1] if len(both) == 2 else both[0]
        return pairs

    def fold(level, pairs, visit):
        lanes = level[5]
        odd_lane = lax.rem(lax.div(lane, lanes), 2) == 1
        for place, pair in enumerate(pairs):
            total = folded[pair, pl.ds(0, 8, 2)] + folded[pair, pl.ds(1, 8, 2)]
            total = total + jnp.where(
                odd_lane, pltpu.roll(total, lanes, 1), pltpu.roll(total, NZ - lanes, 1)
            )
            visit(place, total)

    near0 = exchange0(0)
    hear(relays_x, 0, 1)
    tell(relays_x, 0, 2)

    def half_at(level, slab):
        return jnp.where(inside(level, slab), 0.5, 0.0)

    def to_part1(place, values):
        part1[place + 4, 12:20] = half_at(spread1, place + 4) * values

    def to_part2(place, values):
        part2[place + 5, 11:19] = half_at(spread2, place + 5) * values

    fold(spread0, spread_down(spread0, part0, pa0, pb0, 4, 20), to_part1)
    fold(spread1, spread_down(spread1, part1, pa1, pb1, 4, 16), to_part2)
    spread_down(spread2, part2, pa2, pb2, 5, 15)
    modes = product(
        halves(folded[1:9].reshape(8 * 16, NZ)), (along_z[0], along_z[1])
    ).reshape(8, 16, NZ)
    row16 = lax.broadcasted_iota(jnp.int32, (16, NZ), 0)
    lane16 = lax.div(lax.broadcasted_iota(jnp.int32, (16, NZ), 1), 16)
    group_of = lax.rem(gy + 5 + lax.div(row16, 2), 8)
    gather1[gy] = jnp.sum(jnp.where((lane16 == group_of)[None], modes, 0.0), axis=1)

    def spread(ref, mine, count, target, place):
        def one(step):
            return pltpu.make_async_remote_copy(
                src_ref=ref.at[mine],
                dst_ref=ref.at[mine],
                send_sem=gather_sem.at[0, place],
                recv_sem=gather_sem.at[1, place],
                device_id=target(lax.rem(mine + step, count)),
                device_id_type=MESH,
            )

        @pl.loop(0, count - 1)
        def _(turn):
            away = lax.div(turn + 1, 2)
            one(count // 2 + away * (2 * lax.rem(turn, 2) - 1)).start()

        rest_of = ref.at[0 : count - 1]
        return pltpu.make_async_remote_copy(
            src_ref=rest_of,
            dst_ref=rest_of,
            send_sem=gather_sem.at[0, place],
            recv_sem=gather_sem.at[1, place],
            device_id=target(lax.rem(mine + 1, count)),
            device_id_type=MESH,
        )

    hear(relays_y, 4, 1)
    along = spread(gather1, gy, ngy, lambda other: (gx, other), 0)
    hear(relays_x, 0, 2)
    tell(relays_x, 0, 3)

    around2 = [(dx, dy) for dy in range(-2, 3) for dx in range(-1, 2)]
    for dx, dy in around2:
        for x in range(4):
            share[dx + 1, dy + 2, 2 * x : 2 * x + 2] = part2[
                4 * dx + x + 8, 2 * dy + 14 : 2 * dy + 16
            ]
    shared = [
        push(share.at[1 + dx, 2 + dy], got_share.at[1 - dx, 2 - dy], dx, dy, share_sem, place)
        for place, (dx, dy) in enumerate(pair for pair in around2 if pair != (0, 0))
    ]

    receive(near0)
    assemble0(0)
    smooth_down(level0, src0.at[0], va0, vb0)

    def to_level1(pair, values):
        tile1[0, pair + 4, 8:16] = values

    restrict_to(level0, src0.at[0], va0, to_level1)
    near1 = exchange1(0)

    receive(shared)
    total = share[1, 2]
    for dx, dy in around2:
        if dx or dy:
            total = total + got_share[1 + dx, 2 + dy]
    got2[2, 3] = total
    near2 = exchange2()

    def flux_xy(i, dx, dy):
        return (here(3, i, dx + 1, dy) - here(3, i, dx, dy)) - (
            here(2, i, dx, dy + 1) - here(2, i, dx, dy)
        )

    def flux_yz(i, dy):
        a_y = here(3, i, 0, dy)
        return (here(4, i, 0, dy + 1) - here(4, i, 0, dy)) - (ahead_z(a_y) - a_y)

    def flux_zx(i, dx):
        a_x = here(2, i, dx, 0)
        return (ahead_z(a_x) - a_x) - (here(4, i, dx + 1, 0) - here(4, i, dx, 0))

    def rate_part(i):
        re, im = here(0, i), here(1, i)
        condense = pin[i] - (re * re + im * im) - 6.0
        rates[0, i] += condense * re
        rates[1, i] += condense * im
        under_x = jnp.where(lane == 0, here(2, i), 0.0)
        under_y = jnp.where(lane == 0, here(3, i), 0.0)
        xy, yz, zx = flux_xy(i, 0, 0), flux_yz(i, 0), flux_zx(i, 0)
        rates[2, i] -= KAPPA2 * ((xy - flux_xy(i, 0, -1)) - (zx - (behind_z(zx) + under_x)))
        rates[3, i] -= KAPPA2 * ((yz - (behind_z(yz) - under_y)) - (xy - flux_xy(i, -1, 0)))
        rates[4, i] -= KAPPA2 * ((zx - flux_zx(i, -1)) - (yz - flux_yz(i, -1)))

    each(0, TX, rate_part)

    along.wait_recv()
    groups = max(1, ngy // 8)
    chip, core = lax.div(gx, 2), lax.rem(gx, 2)
    lane8 = lax.div(lax.broadcasted_iota(jnp.int32, (8, NZ), 1), 16)
    for group in range(groups):
        total = jnp.zeros((8, NZ), jnp.float32)
        for sender in range(ngy):
            low, high = sender - 3 - 8 * group, sender + 3 - 8 * group
            if high >= 0 and low < 8:
                held = jnp.logical_and(lane8 >= low, lane8 <= high)
                total = total + jnp.where(held, gather1[sender], 0.0)
        gather2[core, chip, :, 128 * group : 128 * group + 128] = total
    hear(relays_x, 0, 3)
    across = spread(
        gather2.at[core], chip, ngx // 2, lambda other: (2 * other + core, gy), 1
    )

    def keep0(i):
        values = va0[i + 3, 12:20]
        tile0[1, i + 3] = values
        low_out[1, i] = values[0:4]
        high_out[1, i] = values[4:8]

    each(0, TX, keep0)
    late0 = exchange0(1)

    receive(near1)
    smooth_down(level1, tile1.at[0], va1, vb1)

    def keep1(i):
        tile1[1, i + 4, 8:16] = va1[i + 4, 16:24]

    each(0, 8, keep1)
    late1 = exchange1(1)
    receive(near2)
    unpack2()
    smooth_down(level2, src2, va2, vb2)

    across.wait_recv()
    swap = pltpu.make_async_remote_copy(
        src_ref=gather2.at[core],
        dst_ref=gather2.at[core],
        send_sem=gather_sem.at[0, 2],
        recv_sem=gather_sem.at[1, 2],
        device_id=(gx + 1 - 2 * core, gy),
        device_id_type=MESH,
    )
    swap.start()
    swap.wait_recv()
    shares = gather2[...].reshape(8 * ngx, 128 * groups)
    spectral = product((along_x[0], along_x[1]), halves(shares))
    spectral = product(halves(spectral), (along_y[0], along_y[1])) * inverse[...]
    spectral = product((back_x[0, :, : 2 * ngx], back_x[1, :, : 2 * ngx]), halves(spectral))
    spectral = halves(spectral)
    for place in range(5):
        column = product(spectral, (back_yz[0, place], back_yz[1, place]))
        for x in range(6):
            coarse[x, 2 * place + 2 : 2 * place + 4] = column[2 * x : 2 * x + 2]

    smooth_up(
        level2,
        lambda slab: va2[slab, 8:24] + coarse[lax.div(slab, 2) - 1],
        src2,
        va2,
        vb2,
        first=2,
    )
    receive(late1)

    def start1(slab):
        x = lax.div(slab, 2) + 4
        parts = []
        for place in range(3):
            row = 12 + 2 * place
            parts.append(jnp.where(row8 < 4, va2[x, row : row + 1], va2[x, row + 1 : row + 2]))
        return tile1[1, slab] + jnp.concatenate(parts, 0)

    smooth_up(level1, start1, tile1.at[0], va1, vb1)
    receive(late0)
    assemble0(1)
    smooth_up(
        level0,
        lambda slab: src0[1, slab] + va1[lax.div(slab + 1, 2) + 2, 12:28],
        src0.at[0],
        va0,
        vb0,
    )

    not_top = jnp.logical_or(row8 < TY - 1, gy < ngy - 1)

    def finish(i):
        potential = va0[i + 3, 12:20]
        above = jnp.where(not_top, va0[i + 3, 13:21], 0.0)
        potential_ref[i] = potential
        re, im = here(0, i), here(1, i)
        out_ref[0, i] = re + DT * (rates[0, i] + potential * im)
        out_ref[1, i] = im + DT * (rates[1, i] - potential * re)
        out_ref[2, i] = here(2, i) + DT * (rates[2, i] - (va0[i + 4, 12:20] - potential))
        out_ref[3, i] = here(3, i) + DT * (rates[3, i] - (above - potential))
        out_ref[4, i] = here(4, i) + DT * (rates[4, i] - (ahead_z(potential) - potential))

    each(0, TX, finish)

    for copy, outward in sent:
        pl.when(outward)(lambda: copy.wait_send())
    along.wait_send()
    across.wait_send()
    swap.wait_send()


def solution(mesh):
    ngx, ngy = mesh.shape["gx"], mesh.shape["gy"]
    tables = coarse_tables(ngx, ngy)
    groups = max(1, ngy // 8)
    width = 128 * groups
    f32, bf16 = jnp.float32, jnp.bfloat16
    vmem, dma = pltpu.VMEM, pltpu.SemaphoreType.DMA

    def body(state, pinning, lead_values):
        return pl.pallas_call(
            functools.partial(kernel, ngx, ngy),
            out_shape=(vmem(state.shape, f32), vmem(pinning.shape, f32)),
            in_specs=[pl.BlockSpec(memory_space=pltpu.HBM)] * 9,
            out_specs=(
                pl.BlockSpec(memory_space=pltpu.VMEM),
                pl.BlockSpec(memory_space=pltpu.VMEM),
            ),
            scratch_shapes=[
                vmem((5, TX + 2, 24, NZ), f32),
                vmem((TX, TY, NZ), f32),
                vmem((2, TY, NZ), f32),
                vmem(tables[0].shape, bf16),
                vmem(tables[1].shape, bf16),
                vmem(tables[2].shape, bf16),
                vmem(tables[3].shape, f32),
                vmem((2, 16, 128), bf16),
                vmem((2, 5, width, 128), bf16),
                vmem((2, 5, TX, 1, NZ), f32),
                vmem((2, 5, TX, 1, NZ), f32),
                vmem((2, 1, NZ), f32),
                vmem((5, TX, TY, NZ), f32),
                vmem((5, TX, TY, NZ), f32),
                vmem((2, 22, TY, NZ), f32),
                vmem((2, TX, 4, NZ), f32),
                vmem((2, TX, 4, NZ), f32),
                vmem((2, 22, 4, NZ), f32),
                vmem((2, 22, 4, NZ), f32),
                vmem((2, 22, 16, NZ), f32),
                vmem((22, 32, NZ), f32),
                vmem((22, 32, NZ), f32),
                vmem((2, 16, 24, NZ), f32),
                vmem((16, 40, NZ), f32),
                vmem((16, 40, NZ), f32),
                vmem((3, 5, TY, NZ), f32),
                vmem((3, 5, TY, NZ), f32),
                vmem((5, 7, TY, NZ), f32),
                vmem((16, 16, NZ), f32),
                vmem((16, 32, NZ), f32),
                vmem((16, 32, NZ), f32),
                vmem((24, 32, NZ), f32),
                vmem((24, 32, NZ), f32),
                vmem((24, 32, NZ), f32),
                vmem((20, 32, NZ), f32),
                vmem((20, 32, NZ), f32),
                vmem((20, 32, NZ), f32),
                vmem((20, 32, NZ), f32),
                vmem((20, 32, NZ), f32),
                vmem((20, 32, NZ), f32),
                vmem((12, 16, NZ), f32),
                vmem((6, 16, NZ), f32),
                vmem((ngy, 8, NZ), f32),
                vmem((2, ngx // 2, 8, width), f32),
                dma((8,)),
                dma,
                dma((2, 6)),
                dma((2, 2, 8)),
                dma((2, 2, 8)),
                dma((2, 14)),
                dma((2, 26)),
                dma((2, 3)),
                pltpu.SemaphoreType.REGULAR((6, 2)),
            ],
            compiler_params=pltpu.CompilerParams(
                collective_id=0, has_side_effects=True, vmem_limit_bytes=60 * 1024 * 1024
            ),
            name="film_step",
        )(state, pinning, lead_values, *[jnp.asarray(table) for table in tables])
    placed = (P(None, "gx", "gy", None), P("gx", "gy", None), P(None, "gy", None))
    return jax.shard_map(
        body,
        mesh=mesh,
        in_specs=placed,
        out_specs=(P(None, "gx", "gy", None), P("gx", "gy", None)),
        check_vma=False,
    )
```

```python
import functools
import math

import jax
import jax.numpy as jnp
import ml_dtypes
import numpy as np
from jax import lax
from jax.experimental import pallas as pl
from jax.experimental.pallas import tpu as pltpu
from jax.sharding import PartitionSpec as P

MESH = pl.DeviceIdType.MESH
OMEGA = 0.8
DT = 0.05
KAPPA2 = 2.0
KEEP = 1.0 - OMEGA
GAIN = OMEGA / 6.0
TX, TY, NZ = 16, 8, 128


def chebyshev_powers(function, terms):
    fit = np.polynomial.chebyshev.Chebyshev.interpolate(
        lambda u: function(np.sqrt(np.maximum(8.0 * (u + 1.0), 0.0))), terms, domain=[-1, 1]
    )
    return [float(c) for c in np.polynomial.chebyshev.cheb2poly(fit.coef)]


COS_POWERS = chebyshev_powers(np.cos, 8)
SIN_POWERS = chebyshev_powers(lambda a: np.sinc(a / np.pi), 8)


def horner(powers, u):
    total = powers[-1] * u + powers[-2]
    for power in powers[-3::-1]:
        total = total * u + power
    return total


def cos_sin(angle):
    u = angle * angle * 0.125 - 1.0
    return horner(COS_POWERS, u), horner(SIN_POWERS, u) * angle


def sine_table(count):
    modes = np.arange(1, count + 1, dtype=np.float64)
    return np.sqrt(2.0 / (count + 1)) * np.sin(np.pi / (count + 1) * modes[:, None] * modes[None])


def sine_values(count):
    return 2.0 - 2.0 * np.cos(np.pi / (count + 1) * np.arange(1, count + 1, dtype=np.float64))


def cosine_table(count):
    modes = np.arange(count, dtype=np.float64)
    weights = np.where(modes == 0.0, 1.0, 2.0) / count
    return np.sqrt(weights)[:, None] * np.cos(
        np.pi / count * modes[:, None] * (modes[None] + 0.5)
    )


def cosine_values(count):
    return 2.0 - 2.0 * np.cos(np.pi / count * np.arange(count, dtype=np.float64))


def split_pair(table):
    high = table.astype(ml_dtypes.bfloat16)
    low = (table - high.astype(np.float64)).astype(ml_dtypes.bfloat16)
    return np.stack([high, low])


def coarse_tables(ngx, ngy):
    nx, ny, nz = 2 * ngx, ngy, 16
    groups = max(1, ngy // 8)
    width = 128 * groups
    tx, ty, tz = sine_table(nx), cosine_table(ny), cosine_table(nz)
    lanes = np.arange(128)
    along_z = np.tile(tz[:, lanes // 8].T / 8.0, (1, 8))
    along_x = np.zeros((nx, ngx, 8))
    for cell in range(8):
        place = 2 * np.arange(ngx) + cell - 3
        within = (place >= 0) & (place < nx)
        along_x[:, within, cell] = tx[:, place[within]]
    along_x = along_x.reshape(nx, ngx // 2, 2, 8).swapaxes(1, 2).reshape(nx, 8 * ngx)
    along_y = np.zeros((width, width))
    inverse = np.zeros((nx, width))
    values = (
        sine_values(nx)[:, None, None]
        + cosine_values(ny)[None, :, None]
        + cosine_values(nz)[None, None, :]
    )
    inverse[:, : ny * nz] = (1.0 / values).reshape(nx, ny * nz)
    along_y[: ny * nz, : ny * nz] = np.kron(ty.T, np.eye(nz))
    back_x = np.zeros((ngx, 16, 128))
    for cell in range(12):
        place = 2 * np.arange(ngx) + cell // 2 - 2
        within = (place >= 0) & (place < nx)
        back_x[within, cell, :nx] = tx.T[place[within]]
    back_yz = np.zeros((ny + 4, width, 128))
    for y in range(ny):
        back_yz[2 + y, : ny * nz] = np.kron(ty[:, y : y + 1], tz[:, lanes // 8])
    return (
        split_pair(along_z),
        split_pair(along_x),
        split_pair(along_y),
        inverse.astype(np.float32),
        split_pair(back_x),
        split_pair(back_yz),
    )


def halves(values):
    high = values.astype(jnp.bfloat16)
    return high, (values - high.astype(jnp.float32)).astype(jnp.bfloat16)


def product(left, right):
    dot = functools.partial(jnp.dot, preferred_element_type=jnp.float32)
    return dot(left[0], right[0]) + (dot(left[0], right[1]) + dot(left[1], right[0]))


def kernel(
    ngx,
    ngy,
    state_ref,
    pinning_ref,
    lead_ref,
    along_z_ref,
    along_x_ref,
    along_y_ref,
    inverse_ref,
    back_x_ref,
    back_yz_ref,
    out_ref,
    potential_ref,
    ext,
    pin,
    lead,
    along_z,
    along_x,
    along_y,
    inverse,
    back_x,
    back_yz,
    face_out,
    face_in,
    diag_in,
    rates,
    work,
    tile0,
    low_out,
    high_out,
    low_in,
    high_in,
    src0,
    va0,
    vb0,
    got1,
    tile1,
    va1,
    vb1,
    share,
    got_share,
    got2,
    src2,
    va2,
    vb2,
    part0,
    pa0,
    pb0,
    part1,
    pa1,
    pb1,
    part2,
    pa2,
    pb2,
    folded,
    coarse,
    gather1,
    gather2,
    local_sem,
    state_sem,
    halo_sem,
    level0_sem,
    level1_sem,
    share_sem,
    level2_sem,
    gather_sem,
    relay_sem,
):
    gx, gy = lax.axis_index("gx"), lax.axis_index("gy")

    def device(dx, dy):
        return (lax.rem(gx + dx % ngx, ngx), lax.rem(gy + dy % ngy, ngy))

    def each(first, last, visit):
        def one(place, carry):
            visit(place)
            return carry

        lax.fori_loop(first, last, one, 0, unroll=True)

    own_state = pltpu.make_async_copy(state_ref, ext.at[:, 1:17, 8:16], state_sem)
    own_state.start()
    got_share[...] = jnp.zeros(got_share.shape, jnp.float32)
    barrier = pltpu.get_barrier_semaphore()
    def within(dx, dy):
        tests = [gx >= -dx] * (dx < 0) + [gx < ngx - dx] * (dx > 0)
        tests += [gy >= -dy] * (dy < 0) + [gy < ngy - dy] * (dy > 0)
        return functools.reduce(jnp.logical_and, tests)

    near = [
        (dx, dy)
        for dy in range(-4, 5)
        for dx in range(-2, 3)
        if (dx or dy) and abs(dx) * abs(dy) < 4 and (dx == 0 or abs(dy) < 4)
    ]
    for dx, dy in near:

        @pl.when(within(dx, dy))
        def _():
            pl.semaphore_signal(
                barrier, inc=1, device_id=device(dx, dy), device_id_type=MESH
            )

    present = sum(within(dx, dy).astype(jnp.int32) for dx, dy in near)

    locals_ = [
        pltpu.make_async_copy(source, target, local_sem.at[place])
        for place, (source, target) in enumerate(
            [
                (pinning_ref, pin),
                (lead_ref, lead),
                (along_z_ref, along_z),
                (along_x_ref, along_x),
                (along_y_ref, along_y),
                (inverse_ref, inverse),
                (back_x_ref.at[:, gx], back_x),
                (back_yz_ref.at[:, pl.ds(gy, 5)], back_yz),
            ]
        )
    ]
    own_state.wait()
    face_out[0] = ext[:, 1:17, 8:9, :]
    face_out[1] = ext[:, 1:17, 15:16, :]
    pl.semaphore_wait(barrier, present)

    sent = []

    def push(source, target, dx, dy, sems, place):
        copy = pltpu.make_async_remote_copy(
            src_ref=source,
            dst_ref=target,
            send_sem=sems.at[0, place],
            recv_sem=sems.at[1, place],
            device_id=device(dx, dy),
            device_id_type=MESH,
        )
        outward = within(dx, dy)
        pl.when(outward)(lambda: copy.start())
        sent.append((copy, outward))
        return copy, within(-dx, -dy)

    def receive(copies):
        for copy, inward in copies:
            pl.when(inward)(lambda: copy.wait_recv())

    halo = [
        push(face_out.at[0], face_in.at[0], 0, -1, halo_sem, 0),
        push(face_out.at[1], face_in.at[1], 0, 1, halo_sem, 1),
        push(ext.at[:, 1, 8:16], ext.at[:, 17, 8:16], -1, 0, halo_sem, 2),
        push(ext.at[:, 16, 8:16], ext.at[:, 0, 8:16], 1, 0, halo_sem, 3),
        push(face_out.at[1, 3, 0], diag_in.at[0], -1, 1, halo_sem, 4),
        push(face_out.at[0, 2, 15], diag_in.at[1], 1, -1, halo_sem, 5),
    ]
    for copy in locals_:
        copy.start()

    for ref in (part0, pa0, pb0, part1, pa1, pb1, part2, pa2, pb2):
        ref[...] = jnp.zeros(ref.shape, jnp.float32)

    def clear(*refs):
        for ref in refs:
            ref[...] = jnp.zeros(ref.shape, jnp.float32)

    @pl.when(gx == 0)
    def _():
        clear(tile0.at[:, 0:3], low_in.at[:, 0:3], high_in.at[:, 0:3])
        clear(got1.at[:, :, 0:1], got2.at[0:2])

    @pl.when(gx == 1)
    def _():
        clear(got2.at[0:1])

    @pl.when(gx == ngx - 1)
    def _():
        clear(tile0.at[:, 19:22], low_in.at[:, 19:22], high_in.at[:, 19:22])
        clear(got1.at[:, :, 3:4], got2.at[3:5])

    @pl.when(gx == ngx - 2)
    def _():
        clear(got2.at[4:5])

    for place in range(3):

        @pl.when(gy == place)
        def _():
            clear(got2.at[:, 0 : 3 - place])

        @pl.when(gy == ngy - 1 - place)
        def _():
            clear(got2.at[:, 4 + place : 7])

    @pl.when(gy == 0)
    def _():
        clear(low_in, got1.at[:, 0:1])

    @pl.when(gy == ngy - 1)
    def _():
        clear(high_in, got1.at[:, 2:3])

    def relays(reach, count):
        steps = []
        while reach < count - 1:
            steps.append(reach)
            reach *= 2
        return steps

    relays_x = [(reach, 0) for reach in relays(2, ngx)]
    relays_y = [(0, reach) for reach in relays(4, ngy)]

    def tell(steps, first, place):
        if place < len(steps):
            dx, dy = steps[place]
            for side, sign in enumerate((-1, 1)):

                @pl.when(within(sign * dx, sign * dy))
                def _():
                    pl.semaphore_signal(
                        relay_sem.at[first + place, side],
                        inc=1,
                        device_id=device(sign * dx, sign * dy),
                        device_id_type=MESH,
                    )

    def hear(steps, first, place):
        if place < len(steps):
            dx, dy = steps[place]
            for side, sign in enumerate((-1, 1)):

                @pl.when(within(-sign * dx, -sign * dy))
                def _():
                    pl.semaphore_wait(relay_sem.at[first + place, side], 1)

    tell(relays_y, 4, 0)
    tell(relays_x, 0, 0)

    lane = lax.broadcasted_iota(jnp.int32, (1, NZ), 1)
    row8 = lax.broadcasted_iota(jnp.int32, (TY, NZ), 0)

    def ahead_z(values):
        return jnp.where(lane == NZ - 1, 0.0, pltpu.roll(values, NZ - 1, 1))

    def behind_z(values):
        return jnp.where(lane == 0, 0.0, pltpu.roll(values, 1, 1))

    def here(field, slab, dx=0, dy=0):
        return ext[field, slab + (1 + dx), 8 + dy : 16 + dy, :]

    def link(c, s, re, im, next_re, next_im):
        moved_re = c * next_re + s * next_im
        moved_im = c * next_im - s * next_re
        current = re * moved_im - im * moved_re
        return moved_re, moved_im, c * re - s * im, c * im + s * re, current

    def own_part(i):
        re, im = here(0, i), here(1, i)
        c, s = cos_sin(here(4, i))
        moved_re, moved_im, back_re, back_im, current = link(
            c, s, re, im, ahead_z(re), ahead_z(im)
        )
        rates[0, i] = moved_re + behind_z(back_re)
        rates[1, i] = moved_im + behind_z(back_im)
        rates[4, i] = current
        work[0, i] = behind_z(current) - current
        work[1, i], work[2, i] = cos_sin(here(2, i))
        work[3, i], work[4, i] = cos_sin(here(3, i))

    each(0, TX, own_part)
    hear(relays_y, 4, 0)
    tell(relays_y, 4, 1)
    hear(relays_x, 0, 0)
    tell(relays_x, 0, 1)
    for copy in locals_:
        copy.wait()
    work[0, 0] += jnp.where(gx == 0, 1.0, 0.0) * lead[0]
    work[0, TX - 1] += jnp.where(gx == ngx - 1, 1.0, 0.0) * lead[1]

    receive(halo)
    ext[:, 1:17, 16:17, :] = face_in[0]
    ext[:, 1:17, 7:8, :] = face_in[1]
    ext[3, 17, 7:8, :] = diag_in[0]
    ext[2, 0, 16:17, :] = diag_in[1]

    @pl.when(gx == 0)
    def _():
        ext[:, 0, :, :] = jnp.zeros((5, 24, NZ), jnp.float32)

    @pl.when(gx == ngx - 1)
    def _():
        ext[:, 17, :, :] = jnp.zeros((5, 24, NZ), jnp.float32)

    @pl.when(gy == 0)
    def _():
        ext[:, :, 7:8, :] = jnp.zeros((5, 18, 1, NZ), jnp.float32)

    @pl.when(gy == ngy - 1)
    def _():
        ext[:, :, 16:17, :] = jnp.zeros((5, 18, 1, NZ), jnp.float32)

    def source_part(i, carry):
        from_re, from_im, from_current = carry
        re, im = here(0, i), here(1, i)
        moved_re, moved_im, back_re, back_im, current = link(
            work[1, i], work[2, i], re, im, here(0, i, 1), here(1, i, 1)
        )
        up_re, up_im, _, _, up_current = link(
            work[3, i], work[4, i], re, im, here(0, i, 0, 1), here(1, i, 0, 1)
        )
        c, s = cos_sin(here(3, i, 0, -1))
        _, _, down_re, down_im, down_current = link(
            c, s, here(0, i, 0, -1), here(1, i, 0, -1), re, im
        )
        rates[0, i] += (moved_re + from_re) + (up_re + down_re)
        rates[1, i] += (moved_im + from_im) + (up_im + down_im)
        rates[2, i] = current
        rates[3, i] = up_current
        source = work[0, i] - (current - from_current) - (up_current - down_current)
        tile0[0, i + 3] = source
        part0[i + 4, 12:20] = source
        low_out[0, i] = source[0:4]
        high_out[0, i] = source[4:8]
        return back_re, back_im, current

    c, s = cos_sin(here(2, -1))
    _, _, back_re, back_im, current = link(
        c, s, here(0, -1), here(1, -1), here(0, 0), here(1, 0)
    )
    lax.fori_loop(0, TX, source_part, (back_re, back_im, current), unroll=True)

    def exchange0(kind):
        tile, low, high = tile0.at[kind], low_out.at[kind], high_out.at[kind]
        low_to, high_to = low_in.at[kind], high_in.at[kind]
        sems = level0_sem.at[kind]
        return [
            push(low, high_to.at[3:19], 0, -1, sems, 0),
            push(high, low_to.at[3:19], 0, 1, sems, 1),
            push(tile.at[3:6], tile.at[19:22], -1, 0, sems, 2),
            push(tile.at[16:19], tile.at[0:3], 1, 0, sems, 3),
            push(low.at[0:3], high_to.at[19:22], -1, -1, sems, 4),
            push(low.at[13:16], high_to.at[0:3], 1, -1, sems, 5),
            push(high.at[0:3], low_to.at[19:22], -1, 1, sems, 6),
            push(high.at[13:16], low_to.at[0:3], 1, 1, sems, 7),
        ]

    odd_row1, odd_lane1 = lax.rem(row8, 2) == 1, lax.rem(lane, 2) == 1

    def exchange1(kind):
        for half in range(2):
            a, b, c, d = (tile1[kind, 4 + 4 * half + x, 8:16] for x in range(4))
            got1[kind, 1, 1 + half] = jnp.where(
                odd_row1, jnp.where(odd_lane1, d, c), jnp.where(odd_lane1, b, a)
            )
        got = got1.at[kind]
        sems = level1_sem.at[kind]
        first, last = got.at[1, 1], got.at[1, 2]
        return [
            push(got.at[1, 1:3], got.at[2, 1:3], 0, -1, sems, 0),
            push(got.at[1, 1:3], got.at[0, 1:3], 0, 1, sems, 1),
            push(first, got.at[1, 3], -1, 0, sems, 2),
            push(last, got.at[1, 0], 1, 0, sems, 3),
            push(first, got.at[2, 3], -1, -1, sems, 4),
            push(last, got.at[2, 0], 1, -1, sems, 5),
            push(first, got.at[0, 3], -1, 1, sems, 6),
            push(last, got.at[0, 0], 1, 1, sems, 7),
        ]

    def unpack1(kind):
        for place in range(3):
            for column in range(4):
                if place == 1 and column in (1, 2):
                    continue
                packed = got1[kind, place, column]
                even = jnp.where(odd_lane1, pltpu.roll(packed, 1, 1), packed)
                odd = jnp.where(odd_lane1, packed, pltpu.roll(packed, NZ - 1, 1))
                for x, values in enumerate((even, odd)):
                    rows = slice(8 * place, 8 * place + 8)
                    tile1[kind, 4 * column + x, rows] = jnp.where(
                        odd_row1, pltpu.roll(values, 1, 0), values
                    )
                    tile1[kind, 4 * column + 2 + x, rows] = jnp.where(
                        odd_row1, values, pltpu.roll(values, TY - 1, 0)
                    )

    def exchange2():
        copies = []
        for dy in (-3, 3, -2, 2, -1, 1, 0):
            for dx in (-1, 1, 0, -2, 2):
                if (dx or dy) and (abs(dx) < 2 or abs(dy) < 2):
                    target = got2.at[2 - dx, 3 - dy]
                    copies.append(push(got2.at[2, 3], target, dx, dy, level2_sem, len(copies)))
        return copies

    def unpack2():
        for across in range(5):
            for place in range(7):
                if across in (0, 4) and abs(place - 3) > 1:
                    continue
                for x in range(4):
                    slab = 4 * across + x - 2
                    if 0 <= slab < 16:
                        src2[slab, 2 * place : 2 * place + 2] = got2[
                            across, place, 2 * x : 2 * x + 2
                        ]

    def assemble0(kind):
        def one(slab):
            src0[kind, slab, 0:4] = low_in[kind, slab]
            src0[kind, slab, 4:12] = tile0[kind, slab]
            src0[kind, slab, 12:16] = high_in[kind, slab]

        each(0, 22, one)

    level0 = (22, 16, 4, 8, 1, 1, 16, 3)
    level1 = (16, 24, 8, 8, 2, 2, 8, 4)
    level2 = (16, 16, 6, 2, 1, 4, 4, 6)
    spread0 = (24, 16, 4, 8, 1, 1, 16, 4)
    spread1 = (20, 16, 6, 4, 1, 2, 8, 6)
    spread2 = (20, 16, 6, 2, 1, 4, 4, 8)

    def inside(level, slab):
        place = gx * level[6] + (slab - level[7])
        return jnp.logical_and(place >= 0, place < ngx * level[6])

    def gain_at(level, slab):
        return jnp.where(inside(level, slab), GAIN, 0.0)

    def edge_masks(level, row, rows):
        own_row, own_rows, step = level[2:5]
        place = lax.broadcasted_iota(jnp.int32, (rows, NZ), 0) + (gy * own_rows + (row - own_row))
        at_top = jnp.logical_and(place >= ngy * own_rows - step, place < ngy * own_rows)
        at_low = jnp.logical_and(place >= 0, place < step)
        return at_top, at_low

    def around(level, masks, ref, slab, row, rows):
        step, lanes = level[4:6]
        row = row + 8
        centre = ref[slab, row : row + rows]
        above = jnp.where(masks[0], centre, ref[slab, row + step : row + step + rows])
        below = jnp.where(masks[1], centre, ref[slab, row - step : row - step + rows])
        right = jnp.where(lane >= NZ - lanes, centre, pltpu.roll(centre, NZ - lanes, 1))
        left = jnp.where(lane < lanes, centre, pltpu.roll(centre, lanes, 1))
        along = ref[slab + 1, row : row + rows] + ref[slab - 1, row : row + rows]
        return centre, along + (above + below) + (left + right)

    def sweep(level, ref, to, source, first, last):
        rows = level[1]
        masks = edge_masks(level, 0, rows)

        def one(slab):
            centre, total = around(level, masks, ref, slab, 0, rows)
            fresh = KEEP * centre + gain_at(level, slab) * (total + source[slab])
            to[slab, 8 : 8 + rows] = fresh

        each(first, last, one)

    def smooth_down(level, source, va, vb):
        slabs, rows = level[:2]

        def one(slab):
            va[slab, 8 : 8 + rows] = gain_at(level, slab) * source[slab]

        each(0, slabs, one)
        sweep(level, va, vb, source, 1, slabs - 1)
        sweep(level, vb, va, source, 2, slabs - 2)

    def restrict_to(level, source, ref, visit):
        row, _, step, lanes, tile, margin = level[2:8]
        masks = edge_masks(level, row, TY)
        odd_row = lax.rem(lax.div(row8, step), 2) == 1
        odd_lane = lax.rem(lax.div(lane, lanes), 2) == 1

        def rest(slab):
            centre, total = around(level, masks, ref, slab, row, TY)
            return source[slab, row : row + TY] + total - 6.0 * centre

        def one(pair):
            total = rest(margin + 2 * pair) + rest(margin + 1 + 2 * pair)
            total = total + jnp.where(
                odd_row, pltpu.roll(total, step, 0), pltpu.roll(total, TY - step, 0)
            )
            total = total + jnp.where(
                odd_lane, pltpu.roll(total, lanes, 1), pltpu.roll(total, NZ - lanes, 1)
            )
            visit(pair, 0.5 * total)

        each(0, tile // 2, one)

    def smooth_up(level, start, source, va, vb, first=0):
        slabs, rows = level[:2]

        def one(slab):
            va[slab, 8 : 8 + rows] = jnp.where(inside(level, slab), start(slab), 0.0)

        each(first, slabs - first, one)
        sweep(level, va, vb, source, first + 1, slabs - first - 1)
        sweep(level, vb, va, source, first + 2, slabs - first - 2)

    def spread_down(level, source, va, vb, first, last):
        rows = level[1]
        masks = edge_masks(level, 0, rows)
        inner = source.at[:, 8 : 8 + rows]

        def two(slab):
            centre, total = around(level, masks, source, slab, 0, rows)
            fresh = gain_at(level, slab) * ((1.0 + KEEP) * centre + GAIN * total)
            vb[slab, 8 : 8 + rows] = fresh

        each(first - 1, last + 1, two)
        sweep(level, vb, va, inner, first - 2, last + 2)

        def rest(slab):
            centre, total = around(level, masks, va, slab, 0, rows)
            return inner[slab] + total - 6.0 * centre

        begin, end = first - 3, last + 3
        pairs = list(range(begin // 2, (end + 1) // 2))
        for pair in pairs:
            both = [rest(slab) for slab in (2 * pair, 2 * pair + 1) if begin <= slab < end]
            folded[pair] = both[0] + both[1] if len(both) == 2 else both[0]
        return pairs

    def fold(level, pairs, visit):
        lanes = level[5]
        odd_lane = lax.rem(lax.div(lane, lanes), 2) == 1
        for place, pair in enumerate(pairs):
            total = folded[pair, pl.ds(0, 8, 2)] + folded[pair, pl.ds(1, 8, 2)]
            total = total + jnp.where(
                odd_lane, pltpu.roll(total, lanes, 1), pltpu.roll(total, NZ - lanes, 1)
            )
            visit(place, total)

    near0 = exchange0(0)
    hear(relays_x, 0, 1)
    tell(relays_x, 0, 2)

    def half_at(level, slab):
        return jnp.where(inside(level, slab), 0.5, 0.0)

    def to_part1(place, values):
        part1[place + 4, 12:20] = half_at(spread1, place + 4) * values

    def to_part2(place, values):
        part2[place + 5, 11:19] = half_at(spread2, place + 5) * values

    fold(spread0, spread_down(spread0, part0, pa0, pb0, 4, 20), to_part1)
    fold(spread1, spread_down(spread1, part1, pa1, pb1, 4, 16), to_part2)
    spread_down(spread2, part2, pa2, pb2, 5, 15)
    modes = product(
        halves(folded[1:9].reshape(8 * 16, NZ)), (along_z[0], along_z[1])
    ).reshape(8, 16, NZ)
    row16 = lax.broadcasted_iota(jnp.int32, (16, NZ), 0)
    lane16 = lax.div(lax.broadcasted_iota(jnp.int32, (16, NZ), 1), 16)
    group_of = lax.rem(gy + 5 + lax.div(row16, 2), 8)
    gather1[gy] = jnp.sum(jnp.where((lane16 == group_of)[None], modes, 0.0), axis=1)

    def spread(ref, mine, count, target, place):
        def one(step):
            return pltpu.make_async_remote_copy(
                src_ref=ref.at[mine],
                dst_ref=ref.at[mine],
                send_sem=gather_sem.at[0, place],
                recv_sem=gather_sem.at[1, place],
                device_id=target(lax.rem(mine + step, count)),
                device_id_type=MESH,
            )

        @pl.loop(0, count - 1)
        def _(turn):
            away = lax.div(turn + 1, 2)
            one(count // 2 + away * (2 * lax.rem(turn, 2) - 1)).start()

        rest_of = ref.at[0 : count - 1]
        return pltpu.make_async_remote_copy(
            src_ref=rest_of,
            dst_ref=rest_of,
            send_sem=gather_sem.at[0, place],
            recv_sem=gather_sem.at[1, place],
            device_id=target(lax.rem(mine + 1, count)),
            device_id_type=MESH,
        )

    hear(relays_y, 4, 1)
    along = spread(gather1, gy, ngy, lambda other: (gx, other), 0)
    hear(relays_x, 0, 2)
    tell(relays_x, 0, 3)

    around2 = [(dx, dy) for dy in range(-2, 3) for dx in range(-1, 2)]
    for dx, dy in around2:
        for x in range(4):
            share[dx + 1, dy + 2, 2 * x : 2 * x + 2] = part2[
                4 * dx + x + 8, 2 * dy + 14 : 2 * dy + 16
            ]
    shared = [
        push(share.at[1 + dx, 2 + dy], got_share.at[1 - dx, 2 - dy], dx, dy, share_sem, place)
        for place, (dx, dy) in enumerate(pair for pair in around2 if pair != (0, 0))
    ]

    receive(near0)
    assemble0(0)
    smooth_down(level0, src0.at[0], va0, vb0)

    def to_level1(pair, values):
        tile1[0, pair + 4, 8:16] = values

    restrict_to(level0, src0.at[0], va0, to_level1)
    near1 = exchange1(0)

    along.wait_recv()
    groups = max(1, ngy // 8)
    chip, core = lax.div(gx, 2), lax.rem(gx, 2)
    lane8 = lax.div(lax.broadcasted_iota(jnp.int32, (8, NZ), 1), 16)
    for group in range(groups):
        total = jnp.zeros((8, NZ), jnp.float32)
        for sender in range(ngy):
            low, high = sender - 3 - 8 * group, sender + 3 - 8 * group
            if high >= 0 and low < 8:
                held = jnp.logical_and(lane8 >= low, lane8 <= high)
                total = total + jnp.where(held, gather1[sender], 0.0)
        gather2[core, chip, :, 128 * group : 128 * group + 128] = total
    hear(relays_x, 0, 3)
    across = spread(
        gather2.at[core], chip, ngx // 2, lambda other: (2 * other + core, gy), 1
    )

    receive(shared)
    total = share[1, 2]
    for dx, dy in around2:
        if dx or dy:
            total = total + got_share[1 + dx, 2 + dy]
    got2[2, 3] = total
    near2 = exchange2()

    receive(near1)
    unpack1(0)
    smooth_down(level1, tile1.at[0], va1, vb1)

    def keep1(i):
        tile1[1, i + 4, 8:16] = va1[i + 4, 16:24]

    each(0, 8, keep1)
    late1 = exchange1(1)
    def flux_xy(i, dx, dy):
        return (here(3, i, dx + 1, dy) - here(3, i, dx, dy)) - (
            here(2, i, dx, dy + 1) - here(2, i, dx, dy)
        )

    def flux_yz(i, dy):
        a_y = here(3, i, 0, dy)
        return (here(4, i, 0, dy + 1) - here(4, i, 0, dy)) - (ahead_z(a_y) - a_y)

    def flux_zx(i, dx):
        a_x = here(2, i, dx, 0)
        return (ahead_z(a_x) - a_x) - (here(4, i, dx + 1, 0) - here(4, i, dx, 0))

    def rate_part(i):
        re, im = here(0, i), here(1, i)
        condense = pin[i] - (re * re + im * im) - 6.0
        rates[0, i] += condense * re
        rates[1, i] += condense * im
        under_x = jnp.where(lane == 0, here(2, i), 0.0)
        under_y = jnp.where(lane == 0, here(3, i), 0.0)
        xy, yz, zx = flux_xy(i, 0, 0), flux_yz(i, 0), flux_zx(i, 0)
        rates[2, i] -= KAPPA2 * ((xy - flux_xy(i, 0, -1)) - (zx - (behind_z(zx) + under_x)))
        rates[3, i] -= KAPPA2 * ((yz - (behind_z(yz) - under_y)) - (xy - flux_xy(i, -1, 0)))
        rates[4, i] -= KAPPA2 * ((zx - flux_zx(i, -1)) - (yz - flux_yz(i, -1)))

    each(0, TX, rate_part)

    def keep0(i):
        values = va0[i + 3, 12:20]
        tile0[1, i + 3] = values
        low_out[1, i] = values[0:4]
        high_out[1, i] = values[4:8]

    each(0, TX, keep0)
    late0 = exchange0(1)

    across.wait_recv()
    swap = pltpu.make_async_remote_copy(
        src_ref=gather2.at[core],
        dst_ref=gather2.at[core],
        send_sem=gather_sem.at[0, 2],
        recv_sem=gather_sem.at[1, 2],
        device_id=(gx + 1 - 2 * core, gy),
        device_id_type=MESH,
    )
    swap.start()
    receive(near2)
    unpack2()
    smooth_down(level2, src2, va2, vb2)
    swap.wait_recv()
    shares = gather2[...].reshape(8 * ngx, 128 * groups)
    spectral = product((along_x[0], along_x[1]), halves(shares))
    spectral = product(halves(spectral), (along_y[0], along_y[1])) * inverse[...]
    spectral = product((back_x[0, :, : 2 * ngx], back_x[1, :, : 2 * ngx]), halves(spectral))
    spectral = halves(spectral)
    for place in range(5):
        column = product(spectral, (back_yz[0, place], back_yz[1, place]))
        for x in range(6):
            coarse[x, 2 * place + 2 : 2 * place + 4] = column[2 * x : 2 * x + 2]

    smooth_up(
        level2,
        lambda slab: va2[slab, 8:24] + coarse[lax.div(slab, 2) - 1],
        src2,
        va2,
        vb2,
        first=2,
    )
    receive(late1)
    unpack1(1)

    def start1(slab):
        x = lax.div(slab, 2) + 4
        parts = []
        for place in range(3):
            row = 12 + 2 * place
            parts.append(jnp.where(row8 < 4, va2[x, row : row + 1], va2[x, row + 1 : row + 2]))
        return tile1[1, slab] + jnp.concatenate(parts, 0)

    smooth_up(level1, start1, tile1.at[0], va1, vb1)
    receive(late0)
    assemble0(1)
    smooth_up(
        level0,
        lambda slab: src0[1, slab] + va1[lax.div(slab + 1, 2) + 2, 12:28],
        src0.at[0],
        va0,
        vb0,
    )

    not_top = jnp.logical_or(row8 < TY - 1, gy < ngy - 1)

    def finish(i):
        potential = va0[i + 3, 12:20]
        above = jnp.where(not_top, va0[i + 3, 13:21], 0.0)
        potential_ref[i] = potential
        re, im = here(0, i), here(1, i)
        out_ref[0, i] = re + DT * (rates[0, i] + potential * im)
        out_ref[1, i] = im + DT * (rates[1, i] - potential * re)
        out_ref[2, i] = here(2, i) + DT * (rates[2, i] - (va0[i + 4, 12:20] - potential))
        out_ref[3, i] = here(3, i) + DT * (rates[3, i] - (above - potential))
        out_ref[4, i] = here(4, i) + DT * (rates[4, i] - (ahead_z(potential) - potential))

    each(0, TX, finish)

    for copy, outward in sent:
        pl.when(outward)(lambda: copy.wait_send())
    along.wait_send()
    across.wait_send()
    swap.wait_send()


def hand_over(state_ref, potential_ref, out_ref, out_potential_ref, sems):
    copies = [
        pltpu.make_async_copy(state_ref.at[field], out_ref.at[field], sems.at[field])
        for field in range(5)
    ]
    copies.append(pltpu.make_async_copy(potential_ref, out_potential_ref, sems.at[5]))
    for copy in copies:
        copy.start()
    for copy in copies:
        copy.wait()


def solution(mesh):
    ngx, ngy = mesh.shape["gx"], mesh.shape["gy"]
    tables = coarse_tables(ngx, ngy)
    groups = max(1, ngy // 8)
    width = 128 * groups
    f32, bf16 = jnp.float32, jnp.bfloat16
    vmem, dma = pltpu.VMEM, pltpu.SemaphoreType.DMA

    def body(state, pinning, lead_values):
        stepped = pl.pallas_call(
            functools.partial(kernel, ngx, ngy),
            out_shape=(vmem(state.shape, f32), vmem(pinning.shape, f32)),
            in_specs=[pl.BlockSpec(memory_space=pltpu.HBM)] * 9,
            out_specs=(
                pl.BlockSpec(memory_space=pltpu.VMEM),
                pl.BlockSpec(memory_space=pltpu.VMEM),
            ),
            scratch_shapes=[
                vmem((5, TX + 2, 24, NZ), f32),
                vmem((TX, TY, NZ), f32),
                vmem((2, TY, NZ), f32),
                vmem(tables[0].shape, bf16),
                vmem(tables[1].shape, bf16),
                vmem(tables[2].shape, bf16),
                vmem(tables[3].shape, f32),
                vmem((2, 16, 128), bf16),
                vmem((2, 5, width, 128), bf16),
                vmem((2, 5, TX, 1, NZ), f32),
                vmem((2, 5, TX, 1, NZ), f32),
                vmem((2, 1, NZ), f32),
                vmem((5, TX, TY, NZ), f32),
                vmem((5, TX, TY, NZ), f32),
                vmem((2, 22, TY, NZ), f32),
                vmem((2, TX, 4, NZ), f32),
                vmem((2, TX, 4, NZ), f32),
                vmem((2, 22, 4, NZ), f32),
                vmem((2, 22, 4, NZ), f32),
                vmem((2, 22, 16, NZ), f32),
                vmem((22, 32, NZ), f32),
                vmem((22, 32, NZ), f32),
                vmem((2, 3, 4, TY, NZ), f32),
                vmem((2, 16, 24, NZ), f32),
                vmem((16, 40, NZ), f32),
                vmem((16, 40, NZ), f32),
                vmem((3, 5, TY, NZ), f32),
                vmem((3, 5, TY, NZ), f32),
                vmem((5, 7, TY, NZ), f32),
                vmem((16, 16, NZ), f32),
                vmem((16, 32, NZ), f32),
                vmem((16, 32, NZ), f32),
                vmem((24, 32, NZ), f32),
                vmem((24, 32, NZ), f32),
                vmem((24, 32, NZ), f32),
                vmem((20, 32, NZ), f32),
                vmem((20, 32, NZ), f32),
                vmem((20, 32, NZ), f32),
                vmem((20, 32, NZ), f32),
                vmem((20, 32, NZ), f32),
                vmem((20, 32, NZ), f32),
                vmem((12, 16, NZ), f32),
                vmem((6, 16, NZ), f32),
                vmem((ngy, 8, NZ), f32),
                vmem((2, ngx // 2, 8, width), f32),
                dma((8,)),
                dma,
                dma((2, 6)),
                dma((2, 2, 8)),
                dma((2, 2, 8)),
                dma((2, 14)),
                dma((2, 26)),
                dma((2, 3)),
                pltpu.SemaphoreType.REGULAR((6, 2)),
            ],
            compiler_params=pltpu.CompilerParams(
                collective_id=0, has_side_effects=True, vmem_limit_bytes=60 * 1024 * 1024
            ),
            name="film_step",
        )(state, pinning, lead_values, *[jnp.asarray(table) for table in tables])
        return pl.pallas_call(
            hand_over,
            out_shape=(
                jax.ShapeDtypeStruct(state.shape, f32),
                jax.ShapeDtypeStruct(pinning.shape, f32),
            ),
            in_specs=[pl.BlockSpec(memory_space=pl.ANY)] * 2,
            out_specs=[pl.BlockSpec(memory_space=pl.ANY)] * 2,
            scratch_shapes=[dma((6,))],
            compiler_params=pltpu.CompilerParams(vmem_limit_bytes=4 * 1024 * 1024),
            name="hand_over",
        )(*stepped)
    placed = (P(None, "gx", "gy", None), P("gx", "gy", None), P(None, "gy", None))
    return jax.shard_map(
        body,
        mesh=mesh,
        in_specs=placed,
        out_specs=(P(None, "gx", "gy", None), P("gx", "gy", None)),
        check_vma=False,
    )
```

```python
import functools
import math

import jax
import jax.numpy as jnp
import ml_dtypes
import numpy as np
from jax import lax
from jax.experimental import pallas as pl
from jax.experimental.pallas import tpu as pltpu
from jax.sharding import PartitionSpec as P

MESH = pl.DeviceIdType.MESH
OMEGA = 0.8
DT = 0.05
KAPPA2 = 2.0
KEEP = 1.0 - OMEGA
GAIN = OMEGA / 6.0
TX, TY, NZ = 16, 8, 128


def chebyshev_powers(function, terms):
    fit = np.polynomial.chebyshev.Chebyshev.interpolate(
        lambda u: function(np.sqrt(np.maximum(8.0 * (u + 1.0), 0.0))), terms, domain=[-1, 1]
    )
    return [float(c) for c in np.polynomial.chebyshev.cheb2poly(fit.coef)]


COS_POWERS = chebyshev_powers(np.cos, 8)
SIN_POWERS = chebyshev_powers(lambda a: np.sinc(a / np.pi), 8)


def horner(powers, u):
    total = powers[-1] * u + powers[-2]
    for power in powers[-3::-1]:
        total = total * u + power
    return total


def cos_sin(angle):
    u = angle * angle * 0.125 - 1.0
    return horner(COS_POWERS, u), horner(SIN_POWERS, u) * angle


def sine_table(count):
    modes = np.arange(1, count + 1, dtype=np.float64)
    return np.sqrt(2.0 / (count + 1)) * np.sin(np.pi / (count + 1) * modes[:, None] * modes[None])


def sine_values(count):
    return 2.0 - 2.0 * np.cos(np.pi / (count + 1) * np.arange(1, count + 1, dtype=np.float64))


def cosine_table(count):
    modes = np.arange(count, dtype=np.float64)
    weights = np.where(modes == 0.0, 1.0, 2.0) / count
    return np.sqrt(weights)[:, None] * np.cos(
        np.pi / count * modes[:, None] * (modes[None] + 0.5)
    )


def cosine_values(count):
    return 2.0 - 2.0 * np.cos(np.pi / count * np.arange(count, dtype=np.float64))


def split_pair(table):
    high = table.astype(ml_dtypes.bfloat16)
    low = (table - high.astype(np.float64)).astype(ml_dtypes.bfloat16)
    return np.stack([high, low])


def coarse_tables(ngx, ngy):
    nx, ny, nz = 2 * ngx, ngy, 16
    groups = max(1, ngy // 8)
    width = 128 * groups
    tx, ty, tz = sine_table(nx), cosine_table(ny), cosine_table(nz)
    lanes = np.arange(128)
    along_z = np.tile(tz[:, lanes // 8].T / 8.0, (1, 8))
    along_x = np.zeros((nx, ngx, 8))
    for cell in range(8):
        place = 2 * np.arange(ngx) + cell - 3
        within = (place >= 0) & (place < nx)
        along_x[:, within, cell] = tx[:, place[within]]
    along_x = np.moveaxis(along_x.reshape(nx, ngx // 2, 2, 8), 2, 0).reshape(2, nx, 4 * ngx)
    along_y = np.zeros((width, width))
    inverse = np.zeros((nx, width))
    values = (
        sine_values(nx)[:, None, None]
        + cosine_values(ny)[None, :, None]
        + cosine_values(nz)[None, None, :]
    )
    inverse[:, : ny * nz] = (1.0 / values).reshape(nx, ny * nz)
    along_y[: ny * nz, : ny * nz] = np.kron(ty.T, np.eye(nz))
    back_x = np.zeros((ngx, 16, 128))
    for cell in range(12):
        place = 2 * np.arange(ngx) + cell // 2 - 2
        within = (place >= 0) & (place < nx)
        back_x[within, cell, :nx] = tx.T[place[within]]
    back_yz = np.zeros((ny + 4, width, 128))
    for y in range(ny):
        back_yz[2 + y, : ny * nz] = np.kron(ty[:, y : y + 1], tz[:, lanes // 8])
    return (
        split_pair(along_z),
        split_pair(along_x),
        split_pair(along_y),
        inverse.astype(np.float32),
        split_pair(back_x),
        split_pair(back_yz),
    )


def halves(values):
    high = values.astype(jnp.bfloat16)
    return high, (values - high.astype(jnp.float32)).astype(jnp.bfloat16)


def product(left, right):
    dot = functools.partial(jnp.dot, preferred_element_type=jnp.float32)
    return dot(left[0], right[0]) + (dot(left[0], right[1]) + dot(left[1], right[0]))


def kernel(
    ngx,
    ngy,
    state_ref,
    pinning_ref,
    lead_ref,
    along_z_ref,
    along_x_ref,
    along_y_ref,
    inverse_ref,
    back_x_ref,
    back_yz_ref,
    out_ref,
    potential_ref,
    ext,
    pin,
    lead,
    along_z,
    along_x,
    along_y,
    inverse,
    back_x,
    back_yz,
    face_out,
    face_in,
    diag_in,
    rates,
    work,
    tile0,
    low_out,
    high_out,
    low_in,
    high_in,
    src0,
    va0,
    vb0,
    got1,
    tile1,
    va1,
    vb1,
    share,
    got_share,
    got2,
    src2,
    va2,
    vb2,
    part0,
    pa0,
    pb0,
    part1,
    pa1,
    pb1,
    part2,
    pa2,
    pb2,
    folded,
    coarse,
    gather1,
    gather2,
    local_sem,
    state_sem,
    halo_sem,
    level0_sem,
    level1_sem,
    share_sem,
    level2_sem,
    gather_sem,
    relay_sem,
):
    gx, gy = lax.axis_index("gx"), lax.axis_index("gy")

    def device(dx, dy):
        return (lax.rem(gx + dx % ngx, ngx), lax.rem(gy + dy % ngy, ngy))

    def each(first, last, visit):
        def one(place, carry):
            visit(place)
            return carry

        lax.fori_loop(first, last, one, 0, unroll=True)

    own_state = pltpu.make_async_copy(state_ref, ext.at[:, 1:17, 8:16], state_sem)
    own_state.start()
    got_share[...] = jnp.zeros(got_share.shape, jnp.float32)
    barrier = pltpu.get_barrier_semaphore()
    def within(dx, dy):
        tests = [gx >= -dx] * (dx < 0) + [gx < ngx - dx] * (dx > 0)
        tests += [gy >= -dy] * (dy < 0) + [gy < ngy - dy] * (dy > 0)
        return functools.reduce(jnp.logical_and, tests)

    near = [
        (dx, dy)
        for dy in range(-4, 5)
        for dx in range(-2, 3)
        if (dx or dy) and abs(dx) * abs(dy) < 4 and (dx == 0 or abs(dy) < 4)
    ]
    near.sort(key=lambda pair: abs(pair[0]) + abs(pair[1]))
    for dx, dy in near:

        @pl.when(within(dx, dy))
        def _():
            pl.semaphore_signal(
                barrier, inc=1, device_id=device(dx, dy), device_id_type=MESH
            )

    present = sum(within(dx, dy).astype(jnp.int32) for dx, dy in near)

    locals_ = [
        pltpu.make_async_copy(source, target, local_sem.at[place])
        for place, (source, target) in enumerate(
            [
                (pinning_ref, pin),
                (lead_ref, lead),
                (along_z_ref, along_z),
                (along_x_ref, along_x),
                (along_y_ref, along_y),
                (inverse_ref, inverse),
                (back_x_ref.at[:, gx], back_x),
                (back_yz_ref.at[:, pl.ds(gy, 5)], back_yz),
            ]
        )
    ]
    own_state.wait()
    face_out[0] = ext[:, 1:17, 8:9, :]
    face_out[1] = ext[:, 1:17, 15:16, :]
    pl.semaphore_wait(barrier, present)

    sent = []

    def push(source, target, dx, dy, sems, place):
        copy = pltpu.make_async_remote_copy(
            src_ref=source,
            dst_ref=target,
            send_sem=sems.at[0, place],
            recv_sem=sems.at[1, place],
            device_id=device(dx, dy),
            device_id_type=MESH,
        )
        outward = within(dx, dy)
        pl.when(outward)(lambda: copy.start())
        sent.append((copy, outward))
        return copy, within(-dx, -dy)

    def receive(copies):
        for copy, inward in copies:
            pl.when(inward)(lambda: copy.wait_recv())

    halo = [
        push(face_out.at[0], face_in.at[0], 0, -1, halo_sem, 0),
        push(face_out.at[1], face_in.at[1], 0, 1, halo_sem, 1),
        push(ext.at[:, 1, 8:16], ext.at[:, 17, 8:16], -1, 0, halo_sem, 2),
        push(ext.at[:, 16, 8:16], ext.at[:, 0, 8:16], 1, 0, halo_sem, 3),
        push(face_out.at[1, 3, 0], diag_in.at[0], -1, 1, halo_sem, 4),
        push(face_out.at[0, 2, 15], diag_in.at[1], 1, -1, halo_sem, 5),
    ]
    for copy in locals_:
        copy.start()

    for ref in (part0, pa0, pb0, part1, pa1, pb1, part2, pa2, pb2):
        ref[...] = jnp.zeros(ref.shape, jnp.float32)

    def clear(*refs):
        for ref in refs:
            ref[...] = jnp.zeros(ref.shape, jnp.float32)

    @pl.when(gx == 0)
    def _():
        clear(tile0.at[:, 0:3], low_in.at[:, 0:3], high_in.at[:, 0:3])
        clear(got1.at[:, :, 0:1], got2.at[0:2])

    @pl.when(gx == 1)
    def _():
        clear(got2.at[0:1])

    @pl.when(gx == ngx - 1)
    def _():
        clear(tile0.at[:, 19:22], low_in.at[:, 19:22], high_in.at[:, 19:22])
        clear(got1.at[:, :, 3:4], got2.at[3:5])

    @pl.when(gx == ngx - 2)
    def _():
        clear(got2.at[4:5])

    for place in range(3):

        @pl.when(gy == place)
        def _():
            clear(got2.at[:, 0 : 3 - place])

        @pl.when(gy == ngy - 1 - place)
        def _():
            clear(got2.at[:, 4 + place : 7])

    @pl.when(gy == 0)
    def _():
        clear(low_in, got1.at[:, 0:1])

    @pl.when(gy == ngy - 1)
    def _():
        clear(high_in, got1.at[:, 2:3])

    def relays(reach, count):
        steps = []
        while reach < count - 1:
            steps.append(reach)
            reach *= 2
        return steps

    relays_x = [(reach, 0) for reach in relays(2, ngx)]
    relays_y = [(0, reach) for reach in relays(4, ngy)]

    def tell(steps, first, place):
        if place < len(steps):
            dx, dy = steps[place]
            for side, sign in enumerate((-1, 1)):

                @pl.when(within(sign * dx, sign * dy))
                def _():
                    pl.semaphore_signal(
                        relay_sem.at[first + place, side],
                        inc=1,
                        device_id=device(sign * dx, sign * dy),
                        device_id_type=MESH,
                    )

    def hear(steps, first, place):
        if place < len(steps):
            dx, dy = steps[place]
            for side, sign in enumerate((-1, 1)):

                @pl.when(within(-sign * dx, -sign * dy))
                def _():
                    pl.semaphore_wait(relay_sem.at[first + place, side], 1)

    tell(relays_y, 4, 0)
    tell(relays_x, 0, 0)

    lane = lax.broadcasted_iota(jnp.int32, (1, NZ), 1)
    row8 = lax.broadcasted_iota(jnp.int32, (TY, NZ), 0)

    def ahead_z(values):
        return jnp.where(lane == NZ - 1, 0.0, pltpu.roll(values, NZ - 1, 1))

    def behind_z(values):
        return jnp.where(lane == 0, 0.0, pltpu.roll(values, 1, 1))

    def here(field, slab, dx=0, dy=0):
        return ext[field, slab + (1 + dx), 8 + dy : 16 + dy, :]

    def link(c, s, re, im, next_re, next_im):
        moved_re = c * next_re + s * next_im
        moved_im = c * next_im - s * next_re
        current = re * moved_im - im * moved_re
        return moved_re, moved_im, c * re - s * im, c * im + s * re, current

    def own_part(i):
        re, im = here(0, i), here(1, i)
        c, s = cos_sin(here(4, i))
        moved_re, moved_im, back_re, back_im, current = link(
            c, s, re, im, ahead_z(re), ahead_z(im)
        )
        rates[0, i] = moved_re + behind_z(back_re)
        rates[1, i] = moved_im + behind_z(back_im)
        rates[4, i] = current
        work[0, i] = behind_z(current) - current
        work[1, i], work[2, i] = cos_sin(here(2, i))
        work[3, i], work[4, i] = cos_sin(here(3, i))

    each(0, TX, own_part)
    hear(relays_y, 4, 0)
    tell(relays_y, 4, 1)
    hear(relays_x, 0, 0)
    tell(relays_x, 0, 1)
    for copy in locals_:
        copy.wait()
    work[0, 0] += jnp.where(gx == 0, 1.0, 0.0) * lead[0]
    work[0, TX - 1] += jnp.where(gx == ngx - 1, 1.0, 0.0) * lead[1]

    receive(halo)
    ext[:, 1:17, 16:17, :] = face_in[0]
    ext[:, 1:17, 7:8, :] = face_in[1]
    ext[3, 17, 7:8, :] = diag_in[0]
    ext[2, 0, 16:17, :] = diag_in[1]

    @pl.when(gx == 0)
    def _():
        ext[:, 0, :, :] = jnp.zeros((5, 24, NZ), jnp.float32)

    @pl.when(gx == ngx - 1)
    def _():
        ext[:, 17, :, :] = jnp.zeros((5, 24, NZ), jnp.float32)

    @pl.when(gy == 0)
    def _():
        ext[:, :, 7:8, :] = jnp.zeros((5, 18, 1, NZ), jnp.float32)

    @pl.when(gy == ngy - 1)
    def _():
        ext[:, :, 16:17, :] = jnp.zeros((5, 18, 1, NZ), jnp.float32)

    def source_part(i, carry):
        from_re, from_im, from_current = carry
        re, im = here(0, i), here(1, i)
        moved_re, moved_im, back_re, back_im, current = link(
            work[1, i], work[2, i], re, im, here(0, i, 1), here(1, i, 1)
        )
        up_re, up_im, _, _, up_current = link(
            work[3, i], work[4, i], re, im, here(0, i, 0, 1), here(1, i, 0, 1)
        )
        c, s = cos_sin(here(3, i, 0, -1))
        _, _, down_re, down_im, down_current = link(
            c, s, here(0, i, 0, -1), here(1, i, 0, -1), re, im
        )
        rates[0, i] += (moved_re + from_re) + (up_re + down_re)
        rates[1, i] += (moved_im + from_im) + (up_im + down_im)
        rates[2, i] = current
        rates[3, i] = up_current
        source = work[0, i] - (current - from_current) - (up_current - down_current)
        tile0[0, i + 3] = source
        part0[i + 4, 12:20] = source
        low_out[0, i] = source[0:4]
        high_out[0, i] = source[4:8]
        return back_re, back_im, current

    c, s = cos_sin(here(2, -1))
    _, _, back_re, back_im, current = link(
        c, s, here(0, -1), here(1, -1), here(0, 0), here(1, 0)
    )
    lax.fori_loop(0, TX, source_part, (back_re, back_im, current), unroll=True)

    def exchange0(kind):
        tile, low, high = tile0.at[kind], low_out.at[kind], high_out.at[kind]
        low_to, high_to = low_in.at[kind], high_in.at[kind]
        sems = level0_sem.at[kind]
        return [
            push(low, high_to.at[3:19], 0, -1, sems, 0),
            push(high, low_to.at[3:19], 0, 1, sems, 1),
            push(tile.at[3:6], tile.at[19:22], -1, 0, sems, 2),
            push(tile.at[16:19], tile.at[0:3], 1, 0, sems, 3),
            push(low.at[0:3], high_to.at[19:22], -1, -1, sems, 4),
            push(low.at[13:16], high_to.at[0:3], 1, -1, sems, 5),
            push(high.at[0:3], low_to.at[19:22], -1, 1, sems, 6),
            push(high.at[13:16], low_to.at[0:3], 1, 1, sems, 7),
        ]

    odd_row1, odd_lane1 = lax.rem(row8, 2) == 1, lax.rem(lane, 2) == 1

    def exchange1(kind):
        for half in range(2):
            a, b, c, d = (tile1[kind, 4 + 4 * half + x, 8:16] for x in range(4))
            got1[kind, 1, 1 + half] = jnp.where(
                odd_row1, jnp.where(odd_lane1, d, c), jnp.where(odd_lane1, b, a)
            )
        got = got1.at[kind]
        sems = level1_sem.at[kind]
        first, last = got.at[1, 1], got.at[1, 2]
        return [
            push(got.at[1, 1:3], got.at[2, 1:3], 0, -1, sems, 0),
            push(got.at[1, 1:3], got.at[0, 1:3], 0, 1, sems, 1),
            push(first, got.at[1, 3], -1, 0, sems, 2),
            push(last, got.at[1, 0], 1, 0, sems, 3),
            push(first, got.at[2, 3], -1, -1, sems, 4),
            push(last, got.at[2, 0], 1, -1, sems, 5),
            push(first, got.at[0, 3], -1, 1, sems, 6),
            push(last, got.at[0, 0], 1, 1, sems, 7),
        ]

    def unpack1(kind):
        for place in range(3):
            for column in range(4):
                if place == 1 and column in (1, 2):
                    continue
                packed = got1[kind, place, column]
                even = jnp.where(odd_lane1, pltpu.roll(packed, 1, 1), packed)
                odd = jnp.where(odd_lane1, packed, pltpu.roll(packed, NZ - 1, 1))
                for x, values in enumerate((even, odd)):
                    rows = slice(8 * place, 8 * place + 8)
                    tile1[kind, 4 * column + x, rows] = jnp.where(
                        odd_row1, pltpu.roll(values, 1, 0), values
                    )
                    tile1[kind, 4 * column + 2 + x, rows] = jnp.where(
                        odd_row1, values, pltpu.roll(values, TY - 1, 0)
                    )

    def exchange2():
        copies = []
        for dy in (-3, 3, -2, 2, -1, 1, 0):
            for dx in (-1, 1, 0, -2, 2):
                if (dx or dy) and (abs(dx) < 2 or abs(dy) < 2):
                    target = got2.at[2 - dx, 3 - dy]
                    copies.append(push(got2.at[2, 3], target, dx, dy, level2_sem, len(copies)))
        return copies

    def unpack2():
        for across in range(5):
            for place in range(7):
                if across in (0, 4) and abs(place - 3) > 1:
                    continue
                for x in range(4):
                    slab = 4 * across + x - 2
                    if 0 <= slab < 16:
                        src2[slab, 2 * place : 2 * place + 2] = got2[
                            across, place, 2 * x : 2 * x + 2
                        ]

    def assemble0(kind):
        def one(slab):
            src0[kind, slab, 0:4] = low_in[kind, slab]
            src0[kind, slab, 4:12] = tile0[kind, slab]
            src0[kind, slab, 12:16] = high_in[kind, slab]

        each(0, 22, one)

    level0 = (22, 16, 4, 8, 1, 1, 16, 3)
    level1 = (16, 24, 8, 8, 2, 2, 8, 4)
    level2 = (16, 16, 6, 2, 1, 4, 4, 6)
    spread0 = (24, 16, 4, 8, 1, 1, 16, 4)
    spread1 = (20, 16, 6, 4, 1, 2, 8, 6)
    spread2 = (20, 16, 6, 2, 1, 4, 4, 8)

    def inside(level, slab):
        place = gx * level[6] + (slab - level[7])
        return jnp.logical_and(place >= 0, place < ngx * level[6])

    def gain_at(level, slab):
        return jnp.where(inside(level, slab), GAIN, 0.0)

    def edge_masks(level, row, rows):
        own_row, own_rows, step = level[2:5]
        place = lax.broadcasted_iota(jnp.int32, (rows, NZ), 0) + (gy * own_rows + (row - own_row))
        at_top = jnp.logical_and(place >= ngy * own_rows - step, place < ngy * own_rows)
        at_low = jnp.logical_and(place >= 0, place < step)
        return at_top, at_low

    def around(level, masks, ref, slab, row, rows):
        step, lanes = level[4:6]
        row = row + 8
        centre = ref[slab, row : row + rows]
        above = jnp.where(masks[0], centre, ref[slab, row + step : row + step + rows])
        below = jnp.where(masks[1], centre, ref[slab, row - step : row - step + rows])
        right = jnp.where(lane >= NZ - lanes, centre, pltpu.roll(centre, NZ - lanes, 1))
        left = jnp.where(lane < lanes, centre, pltpu.roll(centre, lanes, 1))
        along = ref[slab + 1, row : row + rows] + ref[slab - 1, row : row + rows]
        return centre, along + (above + below) + (left + right)

    def sweep(level, ref, to, source, first, last):
        rows = level[1]
        masks = edge_masks(level, 0, rows)

        def one(slab):
            centre, total = around(level, masks, ref, slab, 0, rows)
            fresh = KEEP * centre + gain_at(level, slab) * (total + source[slab])
            to[slab, 8 : 8 + rows] = fresh

        each(first, last, one)

    def smooth_down(level, source, va, vb):
        slabs, rows = level[:2]

        def one(slab):
            va[slab, 8 : 8 + rows] = gain_at(level, slab) * source[slab]

        each(0, slabs, one)
        sweep(level, va, vb, source, 1, slabs - 1)
        sweep(level, vb, va, source, 2, slabs - 2)

    def restrict_to(level, source, ref, visit):
        row, _, step, lanes, tile, margin = level[2:8]
        masks = edge_masks(level, row, TY)
        odd_row = lax.rem(lax.div(row8, step), 2) == 1
        odd_lane = lax.rem(lax.div(lane, lanes), 2) == 1

        def rest(slab):
            centre, total = around(level, masks, ref, slab, row, TY)
            return source[slab, row : row + TY] + total - 6.0 * centre

        def one(pair):
            total = rest(margin + 2 * pair) + rest(margin + 1 + 2 * pair)
            total = total + jnp.where(
                odd_row, pltpu.roll(total, step, 0), pltpu.roll(total, TY - step, 0)
            )
            total = total + jnp.where(
                odd_lane, pltpu.roll(total, lanes, 1), pltpu.roll(total, NZ - lanes, 1)
            )
            visit(pair, 0.5 * total)

        each(0, tile // 2, one)

    def smooth_up(level, start, source, va, vb, first=0):
        slabs, rows = level[:2]

        def one(slab):
            va[slab, 8 : 8 + rows] = jnp.where(inside(level, slab), start(slab), 0.0)

        each(first, slabs - first, one)
        sweep(level, va, vb, source, first + 1, slabs - first - 1)
        sweep(level, vb, va, source, first + 2, slabs - first - 2)

    def spread_down(level, source, va, vb, first, last):
        rows = level[1]
        masks = edge_masks(level, 0, rows)
        inner = source.at[:, 8 : 8 + rows]

        def two(slab):
            centre, total = around(level, masks, source, slab, 0, rows)
            fresh = gain_at(level, slab) * ((1.0 + KEEP) * centre + GAIN * total)
            vb[slab, 8 : 8 + rows] = fresh

        each(first - 1, last + 1, two)
        sweep(level, vb, va, inner, first - 2, last + 2)

        def rest(slab):
            centre, total = around(level, masks, va, slab, 0, rows)
            return inner[slab] + total - 6.0 * centre

        begin, end = first - 3, last + 3
        pairs = list(range(begin // 2, (end + 1) // 2))
        for pair in pairs:
            both = [rest(slab) for slab in (2 * pair, 2 * pair + 1) if begin <= slab < end]
            folded[pair] = both[0] + both[1] if len(both) == 2 else both[0]
        return pairs

    def fold(level, pairs, visit):
        lanes = level[5]
        odd_lane = lax.rem(lax.div(lane, lanes), 2) == 1
        for place, pair in enumerate(pairs):
            total = folded[pair, pl.ds(0, 8, 2)] + folded[pair, pl.ds(1, 8, 2)]
            total = total + jnp.where(
                odd_lane, pltpu.roll(total, lanes, 1), pltpu.roll(total, NZ - lanes, 1)
            )
            visit(place, total)

    near0 = exchange0(0)
    hear(relays_x, 0, 1)
    tell(relays_x, 0, 2)

    def half_at(level, slab):
        return jnp.where(inside(level, slab), 0.5, 0.0)

    def to_part1(place, values):
        part1[place + 4, 12:20] = half_at(spread1, place + 4) * values

    def to_part2(place, values):
        part2[place + 5, 11:19] = half_at(spread2, place + 5) * values

    fold(spread0, spread_down(spread0, part0, pa0, pb0, 4, 20), to_part1)
    fold(spread1, spread_down(spread1, part1, pa1, pb1, 4, 16), to_part2)
    spread_down(spread2, part2, pa2, pb2, 5, 15)
    modes = product(
        halves(folded[1:9].reshape(8 * 16, NZ)), (along_z[0], along_z[1])
    ).reshape(8, 16, NZ)
    row16 = lax.broadcasted_iota(jnp.int32, (16, NZ), 0)
    lane16 = lax.div(lax.broadcasted_iota(jnp.int32, (16, NZ), 1), 16)
    group_of = lax.rem(gy + 5 + lax.div(row16, 2), 8)
    gather1[gy] = jnp.sum(jnp.where((lane16 == group_of)[None], modes, 0.0), axis=1)

    def spread(ref, mine, count, target, place):
        def one(step):
            return pltpu.make_async_remote_copy(
                src_ref=ref.at[mine],
                dst_ref=ref.at[mine],
                send_sem=gather_sem.at[0, place],
                recv_sem=gather_sem.at[1, place],
                device_id=target(lax.rem(mine + step, count)),
                device_id_type=MESH,
            )

        @pl.loop(0, count - 1)
        def _(turn):
            away = lax.div(turn + 1, 2)
            one(count // 2 + away * (2 * lax.rem(turn, 2) - 1)).start()

        rest_of = ref.at[0 : count - 1]
        return pltpu.make_async_remote_copy(
            src_ref=rest_of,
            dst_ref=rest_of,
            send_sem=gather_sem.at[0, place],
            recv_sem=gather_sem.at[1, place],
            device_id=target(lax.rem(mine + 1, count)),
            device_id_type=MESH,
        )

    hear(relays_y, 4, 1)
    along = spread(gather1, gy, ngy, lambda other: (gx, other), 0)
    hear(relays_x, 0, 2)
    tell(relays_x, 0, 3)

    around2 = [(dx, dy) for dy in range(-2, 3) for dx in range(-1, 2)]
    for dx, dy in around2:
        for x in range(4):
            share[dx + 1, dy + 2, 2 * x : 2 * x + 2] = part2[
                4 * dx + x + 8, 2 * dy + 14 : 2 * dy + 16
            ]
    shared = [
        push(share.at[1 + dx, 2 + dy], got_share.at[1 - dx, 2 - dy], dx, dy, share_sem, place)
        for place, (dx, dy) in enumerate(pair for pair in around2 if pair != (0, 0))
    ]

    receive(near0)
    assemble0(0)
    smooth_down(level0, src0.at[0], va0, vb0)

    def to_level1(pair, values):
        tile1[0, pair + 4, 8:16] = values

    restrict_to(level0, src0.at[0], va0, to_level1)
    near1 = exchange1(0)

    along.wait_recv()
    groups = max(1, ngy // 8)
    chip, core = lax.div(gx, 2), lax.rem(gx, 2)
    lane8 = lax.div(lax.broadcasted_iota(jnp.int32, (8, NZ), 1), 16)
    for group in range(groups):
        total = jnp.zeros((8, NZ), jnp.float32)
        for sender in range(ngy):
            low, high = sender - 3 - 8 * group, sender + 3 - 8 * group
            if high >= 0 and low < 8:
                held = jnp.logical_and(lane8 >= low, lane8 <= high)
                total = total + jnp.where(held, gather1[sender], 0.0)
        gather2[core, chip, :, 128 * group : 128 * group + 128] = total
    hear(relays_x, 0, 3)
    across = spread(
        gather2.at[core], chip, ngx // 2, lambda other: (2 * other + core, gy), 1
    )

    receive(shared)
    total = share[1, 2]
    for dx, dy in around2:
        if dx or dy:
            total = total + got_share[1 + dx, 2 + dy]
    got2[2, 3] = total
    near2 = exchange2()

    receive(near1)
    unpack1(0)
    smooth_down(level1, tile1.at[0], va1, vb1)

    def keep1(i):
        tile1[1, i + 4, 8:16] = va1[i + 4, 16:24]

    each(0, 8, keep1)
    late1 = exchange1(1)
    def flux_xy(i, dx, dy):
        return (here(3, i, dx + 1, dy) - here(3, i, dx, dy)) - (
            here(2, i, dx, dy + 1) - here(2, i, dx, dy)
        )

    def flux_yz(i, dy):
        a_y = here(3, i, 0, dy)
        return (here(4, i, 0, dy + 1) - here(4, i, 0, dy)) - (ahead_z(a_y) - a_y)

    def flux_zx(i, dx):
        a_x = here(2, i, dx, 0)
        return (ahead_z(a_x) - a_x) - (here(4, i, dx + 1, 0) - here(4, i, dx, 0))

    def rate_part(i):
        re, im = here(0, i), here(1, i)
        condense = pin[i] - (re * re + im * im) - 6.0
        rates[0, i] += condense * re
        rates[1, i] += condense * im
        under_x = jnp.where(lane == 0, here(2, i), 0.0)
        under_y = jnp.where(lane == 0, here(3, i), 0.0)
        xy, yz, zx = flux_xy(i, 0, 0), flux_yz(i, 0), flux_zx(i, 0)
        rates[2, i] -= KAPPA2 * ((xy - flux_xy(i, 0, -1)) - (zx - (behind_z(zx) + under_x)))
        rates[3, i] -= KAPPA2 * ((yz - (behind_z(yz) - under_y)) - (xy - flux_xy(i, -1, 0)))
        rates[4, i] -= KAPPA2 * ((zx - flux_zx(i, -1)) - (yz - flux_yz(i, -1)))

    each(0, TX, rate_part)

    def keep0(i):
        values = va0[i + 3, 12:20]
        tile0[1, i + 3] = values
        low_out[1, i] = values[0:4]
        high_out[1, i] = values[4:8]

    each(0, TX, keep0)
    late0 = exchange0(1)

    receive(near2)
    unpack2()
    smooth_down(level2, src2, va2, vb2)
    across.wait_recv()
    swap = pltpu.make_async_remote_copy(
        src_ref=gather2.at[core],
        dst_ref=gather2.at[core],
        send_sem=gather_sem.at[0, 2],
        recv_sem=gather_sem.at[1, 2],
        device_id=(gx + 1 - 2 * core, gy),
        device_id_type=MESH,
    )
    swap.start()

    def along_x_of(side):
        shares = gather2[side].reshape(4 * ngx, 128 * groups)
        return product((along_x[0, side], along_x[1, side]), halves(shares))

    spectral = along_x_of(core)
    swap.wait_recv()
    spectral = spectral + along_x_of(1 - core)
    spectral = product(halves(spectral), (along_y[0], along_y[1])) * inverse[...]
    spectral = product((back_x[0, :, : 2 * ngx], back_x[1, :, : 2 * ngx]), halves(spectral))
    spectral = halves(spectral)
    for places in ((0, 1), (2, 3), (4,)):
        back = [
            jnp.concatenate([back_yz[part, place] for place in places], axis=1)
            for part in range(2)
        ]
        columns = product(spectral, back)
        for turn, place in enumerate(places):
            for x in range(6):
                coarse[x, 2 * place + 2 : 2 * place + 4] = columns[
                    2 * x : 2 * x + 2, 128 * turn : 128 * turn + 128
                ]

    smooth_up(
        level2,
        lambda slab: va2[slab, 8:24] + coarse[lax.div(slab, 2) - 1],
        src2,
        va2,
        vb2,
        first=2,
    )
    receive(late1)
    unpack1(1)

    def start1(slab):
        x = lax.div(slab, 2) + 4
        parts = []
        for place in range(3):
            row = 12 + 2 * place
            parts.append(jnp.where(row8 < 4, va2[x, row : row + 1], va2[x, row + 1 : row + 2]))
        return tile1[1, slab] + jnp.concatenate(parts, 0)

    smooth_up(level1, start1, tile1.at[0], va1, vb1)
    receive(late0)
    assemble0(1)
    smooth_up(
        level0,
        lambda slab: src0[1, slab] + va1[lax.div(slab + 1, 2) + 2, 12:28],
        src0.at[0],
        va0,
        vb0,
    )

    not_top = jnp.logical_or(row8 < TY - 1, gy < ngy - 1)

    def finish(i):
        potential = va0[i + 3, 12:20]
        above = jnp.where(not_top, va0[i + 3, 13:21], 0.0)
        potential_ref[i] = potential
        re, im = here(0, i), here(1, i)
        out_ref[0, i] = re + DT * (rates[0, i] + potential * im)
        out_ref[1, i] = im + DT * (rates[1, i] - potential * re)
        out_ref[2, i] = here(2, i) + DT * (rates[2, i] - (va0[i + 4, 12:20] - potential))
        out_ref[3, i] = here(3, i) + DT * (rates[3, i] - (above - potential))
        out_ref[4, i] = here(4, i) + DT * (rates[4, i] - (ahead_z(potential) - potential))

    each(0, TX, finish)

    for copy, outward in sent:
        pl.when(outward)(lambda: copy.wait_send())
    along.wait_send()
    across.wait_send()
    swap.wait_send()


def hand_over(state_ref, potential_ref, out_ref, out_potential_ref, sems):
    copies = [
        pltpu.make_async_copy(state_ref.at[field], out_ref.at[field], sems.at[field])
        for field in range(5)
    ]
    copies.append(pltpu.make_async_copy(potential_ref, out_potential_ref, sems.at[5]))
    for copy in copies:
        copy.start()
    for copy in copies:
        copy.wait()


def solution(mesh):
    ngx, ngy = mesh.shape["gx"], mesh.shape["gy"]
    tables = coarse_tables(ngx, ngy)
    groups = max(1, ngy // 8)
    width = 128 * groups
    f32, bf16 = jnp.float32, jnp.bfloat16
    vmem, dma = pltpu.VMEM, pltpu.SemaphoreType.DMA

    def body(state, pinning, lead_values):
        stepped = pl.pallas_call(
            functools.partial(kernel, ngx, ngy),
            out_shape=(vmem(state.shape, f32), vmem(pinning.shape, f32)),
            in_specs=[pl.BlockSpec(memory_space=pltpu.HBM)] * 9,
            out_specs=(
                pl.BlockSpec(memory_space=pltpu.VMEM),
                pl.BlockSpec(memory_space=pltpu.VMEM),
            ),
            scratch_shapes=[
                vmem((5, TX + 2, 24, NZ), f32),
                vmem((TX, TY, NZ), f32),
                vmem((2, TY, NZ), f32),
                vmem(tables[0].shape, bf16),
                vmem(tables[1].shape, bf16),
                vmem(tables[2].shape, bf16),
                vmem(tables[3].shape, f32),
                vmem((2, 16, 128), bf16),
                vmem((2, 5, width, 128), bf16),
                vmem((2, 5, TX, 1, NZ), f32),
                vmem((2, 5, TX, 1, NZ), f32),
                vmem((2, 1, NZ), f32),
                vmem((5, TX, TY, NZ), f32),
                vmem((5, TX, TY, NZ), f32),
                vmem((2, 22, TY, NZ), f32),
                vmem((2, TX, 4, NZ), f32),
                vmem((2, TX, 4, NZ), f32),
                vmem((2, 22, 4, NZ), f32),
                vmem((2, 22, 4, NZ), f32),
                vmem((2, 22, 16, NZ), f32),
                vmem((22, 32, NZ), f32),
                vmem((22, 32, NZ), f32),
                vmem((2, 3, 4, TY, NZ), f32),
                vmem((2, 16, 24, NZ), f32),
                vmem((16, 40, NZ), f32),
                vmem((16, 40, NZ), f32),
                vmem((3, 5, TY, NZ), f32),
                vmem((3, 5, TY, NZ), f32),
                vmem((5, 7, TY, NZ), f32),
                vmem((16, 16, NZ), f32),
                vmem((16, 32, NZ), f32),
                vmem((16, 32, NZ), f32),
                vmem((24, 32, NZ), f32),
                vmem((24, 32, NZ), f32),
                vmem((24, 32, NZ), f32),
                vmem((20, 32, NZ), f32),
                vmem((20, 32, NZ), f32),
                vmem((20, 32, NZ), f32),
                vmem((20, 32, NZ), f32),
                vmem((20, 32, NZ), f32),
                vmem((20, 32, NZ), f32),
                vmem((12, 16, NZ), f32),
                vmem((6, 16, NZ), f32),
                vmem((ngy, 8, NZ), f32),
                vmem((2, ngx // 2, 8, width), f32),
                dma((8,)),
                dma,
                dma((2, 6)),
                dma((2, 2, 8)),
                dma((2, 2, 8)),
                dma((2, 14)),
                dma((2, 26)),
                dma((2, 3)),
                pltpu.SemaphoreType.REGULAR((6, 2)),
            ],
            compiler_params=pltpu.CompilerParams(
                collective_id=0, has_side_effects=True, vmem_limit_bytes=60 * 1024 * 1024
            ),
            name="film_step",
        )(state, pinning, lead_values, *[jnp.asarray(table) for table in tables])
        return pl.pallas_call(
            hand_over,
            out_shape=(
                jax.ShapeDtypeStruct(state.shape, f32),
                jax.ShapeDtypeStruct(pinning.shape, f32),
            ),
            in_specs=[pl.BlockSpec(memory_space=pl.ANY)] * 2,
            out_specs=[pl.BlockSpec(memory_space=pl.ANY)] * 2,
            scratch_shapes=[dma((6,))],
            compiler_params=pltpu.CompilerParams(vmem_limit_bytes=4 * 1024 * 1024),
            name="hand_over",
        )(*stepped)
    placed = (P(None, "gx", "gy", None), P("gx", "gy", None), P(None, "gy", None))
    return jax.shard_map(
        body,
        mesh=mesh,
        in_specs=placed,
        out_specs=(P(None, "gx", "gy", None), P("gx", "gy", None)),
        check_vma=False,
    )
```

```python
import functools
import math

import jax
import jax.numpy as jnp
import ml_dtypes
import numpy as np
from jax import lax
from jax.experimental import pallas as pl
from jax.experimental.pallas import tpu as pltpu
from jax.sharding import PartitionSpec as P

MESH = pl.DeviceIdType.MESH
OMEGA = 0.8
DT = 0.05
KAPPA2 = 2.0
KEEP = 1.0 - OMEGA
GAIN = OMEGA / 6.0
TX, TY, NZ = 16, 8, 128


def chebyshev_powers(function, terms):
    fit = np.polynomial.chebyshev.Chebyshev.interpolate(
        lambda u: function(np.sqrt(np.maximum(8.0 * (u + 1.0), 0.0))), terms, domain=[-1, 1]
    )
    return [float(c) for c in np.polynomial.chebyshev.cheb2poly(fit.coef)]


COS_POWERS = chebyshev_powers(np.cos, 8)
SIN_POWERS = chebyshev_powers(lambda a: np.sinc(a / np.pi), 8)


def horner(powers, u):
    total = powers[-1] * u + powers[-2]
    for power in powers[-3::-1]:
        total = total * u + power
    return total


def cos_sin(angle):
    u = angle * angle * 0.125 - 1.0
    return horner(COS_POWERS, u), horner(SIN_POWERS, u) * angle


def sine_table(count):
    modes = np.arange(1, count + 1, dtype=np.float64)
    return np.sqrt(2.0 / (count + 1)) * np.sin(np.pi / (count + 1) * modes[:, None] * modes[None])


def sine_values(count):
    return 2.0 - 2.0 * np.cos(np.pi / (count + 1) * np.arange(1, count + 1, dtype=np.float64))


def cosine_table(count):
    modes = np.arange(count, dtype=np.float64)
    weights = np.where(modes == 0.0, 1.0, 2.0) / count
    return np.sqrt(weights)[:, None] * np.cos(
        np.pi / count * modes[:, None] * (modes[None] + 0.5)
    )


def cosine_values(count):
    return 2.0 - 2.0 * np.cos(np.pi / count * np.arange(count, dtype=np.float64))


def split_pair(table):
    high = table.astype(ml_dtypes.bfloat16)
    low = (table - high.astype(np.float64)).astype(ml_dtypes.bfloat16)
    return np.stack([high, low])


def coarse_tables(ngx, ngy):
    nx, ny, nz = 2 * ngx, ngy, 16
    groups = max(1, ngy // 8)
    width = 128 * groups
    tx, ty, tz = sine_table(nx), cosine_table(ny), cosine_table(nz)
    lanes = np.arange(128)
    along_z = np.tile(tz[:, lanes // 8].T / 8.0, (1, 8))
    along_x = np.zeros((nx, ngx, 8))
    for cell in range(8):
        place = 2 * np.arange(ngx) + cell - 3
        within = (place >= 0) & (place < nx)
        along_x[:, within, cell] = tx[:, place[within]]
    along_x = np.moveaxis(along_x.reshape(nx, ngx // 2, 2, 8), 2, 0).reshape(2, nx, 4 * ngx)
    along_y = np.zeros((width, width))
    inverse = np.zeros((nx, width))
    values = (
        sine_values(nx)[:, None, None]
        + cosine_values(ny)[None, :, None]
        + cosine_values(nz)[None, None, :]
    )
    inverse[:, : ny * nz] = (1.0 / values).reshape(nx, ny * nz)
    along_y[: ny * nz, : ny * nz] = np.kron(ty.T, np.eye(nz))
    back_x = np.zeros((ngx, 16, 128))
    for cell in range(12):
        place = 2 * np.arange(ngx) + cell // 2 - 2
        within = (place >= 0) & (place < nx)
        back_x[within, cell, :nx] = tx.T[place[within]]
    back_yz = np.zeros((ny + 4, width, 128))
    for y in range(ny):
        back_yz[2 + y, : ny * nz] = np.kron(ty[:, y : y + 1], tz[:, lanes // 8])
    return (
        split_pair(along_z),
        split_pair(along_x),
        split_pair(along_y),
        inverse.astype(np.float32),
        split_pair(back_x),
        split_pair(back_yz),
    )


def halves(values):
    high = values.astype(jnp.bfloat16)
    return high, (values - high.astype(jnp.float32)).astype(jnp.bfloat16)


def product(left, right):
    dot = functools.partial(jnp.dot, preferred_element_type=jnp.float32)
    return dot(left[0], right[0]) + (dot(left[0], right[1]) + dot(left[1], right[0]))


def kernel(
    ngx,
    ngy,
    state_ref,
    pinning_ref,
    lead_ref,
    along_z_ref,
    along_x_ref,
    along_y_ref,
    inverse_ref,
    back_x_ref,
    back_yz_ref,
    out_ref,
    potential_ref,
    ext,
    pin,
    lead,
    along_z,
    along_x,
    along_y,
    inverse,
    back_x,
    back_yz,
    face_out,
    face_in,
    diag_in,
    rates,
    work,
    tile0,
    low_out,
    high_out,
    low_in,
    high_in,
    src0,
    va0,
    vb0,
    got1,
    tile1,
    va1,
    vb1,
    share,
    got_share,
    got2,
    src2,
    va2,
    vb2,
    part0,
    pa0,
    pb0,
    part1,
    pa1,
    pb1,
    part2,
    pa2,
    pb2,
    folded,
    coarse,
    gather1,
    gather2,
    local_sem,
    state_sem,
    halo_sem,
    level0_sem,
    level1_sem,
    share_sem,
    level2_sem,
    gather_sem,
    relay_sem,
):
    gx, gy = lax.axis_index("gx"), lax.axis_index("gy")

    def device(dx, dy):
        return (lax.rem(gx + dx % ngx, ngx), lax.rem(gy + dy % ngy, ngy))

    def each(first, last, visit):
        def one(place, carry):
            visit(place)
            return carry

        lax.fori_loop(first, last, one, 0, unroll=True)

    own_state = pltpu.make_async_copy(state_ref, ext.at[:, 1:17, 8:16], state_sem)
    own_state.start()
    got_share[...] = jnp.zeros(got_share.shape, jnp.float32)
    barrier = pltpu.get_barrier_semaphore()
    def within(dx, dy):
        tests = [gx >= -dx] * (dx < 0) + [gx < ngx - dx] * (dx > 0)
        tests += [gy >= -dy] * (dy < 0) + [gy < ngy - dy] * (dy > 0)
        return functools.reduce(jnp.logical_and, tests)

    near = [
        (dx, dy)
        for dy in range(-4, 5)
        for dx in range(-2, 3)
        if (dx or dy) and abs(dx) * abs(dy) < 4 and (dx == 0 or abs(dy) < 4)
    ]
    near.sort(key=lambda pair: abs(pair[0]) + abs(pair[1]))
    for dx, dy in near:

        @pl.when(within(dx, dy))
        def _():
            pl.semaphore_signal(
                barrier, inc=1, device_id=device(dx, dy), device_id_type=MESH
            )

    present = sum(within(dx, dy).astype(jnp.int32) for dx, dy in near)

    locals_ = [
        pltpu.make_async_copy(source, target, local_sem.at[place])
        for place, (source, target) in enumerate(
            [
                (pinning_ref, pin),
                (lead_ref, lead),
                (along_z_ref, along_z),
                (along_x_ref, along_x),
                (along_y_ref, along_y),
                (inverse_ref, inverse),
                (back_x_ref.at[:, gx], back_x),
                (back_yz_ref.at[:, pl.ds(gy, 5)], back_yz),
            ]
        )
    ]
    own_state.wait()
    staged = (0, 1, 3, 2, 4)
    for turn, field in enumerate(staged):
        face_out[0, turn] = ext[field, 1:17, 8:9, :]
        face_out[1, turn] = ext[field, 1:17, 15:16, :]
    pl.semaphore_wait(barrier, present)

    sent = []

    def push(source, target, dx, dy, sems, place):
        copy = pltpu.make_async_remote_copy(
            src_ref=source,
            dst_ref=target,
            send_sem=sems.at[0, place],
            recv_sem=sems.at[1, place],
            device_id=device(dx, dy),
            device_id_type=MESH,
        )
        outward = within(dx, dy)
        pl.when(outward)(lambda: copy.start())
        sent.append((copy, outward))
        return copy, within(-dx, -dy)

    def receive(copies):
        for copy, inward in copies:
            pl.when(inward)(lambda: copy.wait_recv())

    halo = [
        push(face_out.at[0, 0:2], face_in.at[0, 0:2], 0, -1, halo_sem, 0),
        push(face_out.at[1, 0:3], face_in.at[1, 0:3], 0, 1, halo_sem, 1),
        push(ext.at[0:2, 1, 8:16], ext.at[0:2, 17, 8:16], -1, 0, halo_sem, 2),
        push(ext.at[0:3, 16, 8:16], ext.at[0:3, 0, 8:16], 1, 0, halo_sem, 3),
    ]
    links = [
        push(face_out.at[0, 2:5], face_in.at[0, 2:5], 0, -1, halo_sem, 4),
        push(face_out.at[1, 3:5], face_in.at[1, 3:5], 0, 1, halo_sem, 5),
        push(ext.at[2:5, 1, 8:16], ext.at[2:5, 17, 8:16], -1, 0, halo_sem, 6),
        push(ext.at[3:5, 16, 8:16], ext.at[3:5, 0, 8:16], 1, 0, halo_sem, 7),
        push(face_out.at[1, 2, 0], diag_in.at[0], -1, 1, halo_sem, 8),
        push(face_out.at[0, 3, 15], diag_in.at[1], 1, -1, halo_sem, 9),
    ]
    for copy in locals_:
        copy.start()

    for ref in (part0, pa0, pb0, part1, pa1, pb1, part2, pa2, pb2):
        ref[...] = jnp.zeros(ref.shape, jnp.float32)

    def clear(*refs):
        for ref in refs:
            ref[...] = jnp.zeros(ref.shape, jnp.float32)

    @pl.when(gx == 0)
    def _():
        clear(tile0.at[:, 0:3], low_in.at[:, 0:3], high_in.at[:, 0:3])
        clear(got1.at[:, :, 0:1], got2.at[0:2])

    @pl.when(gx == 1)
    def _():
        clear(got2.at[0:1])

    @pl.when(gx == ngx - 1)
    def _():
        clear(tile0.at[:, 19:22], low_in.at[:, 19:22], high_in.at[:, 19:22])
        clear(got1.at[:, :, 3:4], got2.at[3:5])

    @pl.when(gx == ngx - 2)
    def _():
        clear(got2.at[4:5])

    for place in range(3):

        @pl.when(gy == place)
        def _():
            clear(got2.at[:, 0 : 3 - place])

        @pl.when(gy == ngy - 1 - place)
        def _():
            clear(got2.at[:, 4 + place : 7])

    @pl.when(gy == 0)
    def _():
        clear(low_in, got1.at[:, 0:1])

    @pl.when(gy == ngy - 1)
    def _():
        clear(high_in, got1.at[:, 2:3])

    def relays(reach, count):
        steps = []
        while reach < count - 1:
            steps.append(reach)
            reach *= 2
        return steps

    relays_x = [(reach, 0) for reach in relays(2, ngx)]
    relays_y = [(0, reach) for reach in relays(4, ngy)]

    def tell(steps, first, place):
        if place < len(steps):
            dx, dy = steps[place]
            for side, sign in enumerate((-1, 1)):

                @pl.when(within(sign * dx, sign * dy))
                def _():
                    pl.semaphore_signal(
                        relay_sem.at[first + place, side],
                        inc=1,
                        device_id=device(sign * dx, sign * dy),
                        device_id_type=MESH,
                    )

    def hear(steps, first, place):
        if place < len(steps):
            dx, dy = steps[place]
            for side, sign in enumerate((-1, 1)):

                @pl.when(within(-sign * dx, -sign * dy))
                def _():
                    pl.semaphore_wait(relay_sem.at[first + place, side], 1)

    tell(relays_y, 4, 0)
    tell(relays_x, 0, 0)

    lane = lax.broadcasted_iota(jnp.int32, (1, NZ), 1)
    row8 = lax.broadcasted_iota(jnp.int32, (TY, NZ), 0)

    def ahead_z(values):
        return jnp.where(lane == NZ - 1, 0.0, pltpu.roll(values, NZ - 1, 1))

    def behind_z(values):
        return jnp.where(lane == 0, 0.0, pltpu.roll(values, 1, 1))

    def here(field, slab, dx=0, dy=0):
        return ext[field, slab + (1 + dx), 8 + dy : 16 + dy, :]

    def link(c, s, re, im, next_re, next_im):
        moved_re = c * next_re + s * next_im
        moved_im = c * next_im - s * next_re
        current = re * moved_im - im * moved_re
        return moved_re, moved_im, c * re - s * im, c * im + s * re, current

    def own_part(i):
        re, im = here(0, i), here(1, i)
        c, s = cos_sin(here(4, i))
        moved_re, moved_im, back_re, back_im, current = link(
            c, s, re, im, ahead_z(re), ahead_z(im)
        )
        rates[0, i] = moved_re + behind_z(back_re)
        rates[1, i] = moved_im + behind_z(back_im)
        rates[4, i] = current
        work[0, i] = behind_z(current) - current
        work[1, i], work[2, i] = cos_sin(here(2, i))
        work[3, i], work[4, i] = cos_sin(here(3, i))

    each(0, TX, own_part)
    hear(relays_y, 4, 0)
    tell(relays_y, 4, 1)
    hear(relays_x, 0, 0)
    tell(relays_x, 0, 1)
    for copy in locals_:
        copy.wait()
    work[0, 0] += jnp.where(gx == 0, 1.0, 0.0) * lead[0]
    work[0, TX - 1] += jnp.where(gx == ngx - 1, 1.0, 0.0) * lead[1]

    receive(halo)
    for turn, field in enumerate(staged[:3]):
        if turn < 2:
            ext[field, 1:17, 16:17, :] = face_in[0, turn]
        ext[field, 1:17, 7:8, :] = face_in[1, turn]

    def zero_outside():
        @pl.when(gx == 0)
        def _():
            ext[:, 0, :, :] = jnp.zeros((5, 24, NZ), jnp.float32)

        @pl.when(gx == ngx - 1)
        def _():
            ext[:, 17, :, :] = jnp.zeros((5, 24, NZ), jnp.float32)

        @pl.when(gy == 0)
        def _():
            ext[:, :, 7:8, :] = jnp.zeros((5, 18, 1, NZ), jnp.float32)

        @pl.when(gy == ngy - 1)
        def _():
            ext[:, :, 16:17, :] = jnp.zeros((5, 18, 1, NZ), jnp.float32)

    zero_outside()

    def source_part(i, carry):
        from_re, from_im, from_current = carry
        re, im = here(0, i), here(1, i)
        moved_re, moved_im, back_re, back_im, current = link(
            work[1, i], work[2, i], re, im, here(0, i, 1), here(1, i, 1)
        )
        up_re, up_im, _, _, up_current = link(
            work[3, i], work[4, i], re, im, here(0, i, 0, 1), here(1, i, 0, 1)
        )
        c, s = cos_sin(here(3, i, 0, -1))
        _, _, down_re, down_im, down_current = link(
            c, s, here(0, i, 0, -1), here(1, i, 0, -1), re, im
        )
        rates[0, i] += (moved_re + from_re) + (up_re + down_re)
        rates[1, i] += (moved_im + from_im) + (up_im + down_im)
        rates[2, i] = current
        rates[3, i] = up_current
        source = work[0, i] - (current - from_current) - (up_current - down_current)
        tile0[0, i + 3] = source
        part0[i + 4, 12:20] = source
        low_out[0, i] = source[0:4]
        high_out[0, i] = source[4:8]
        return back_re, back_im, current

    c, s = cos_sin(here(2, -1))
    _, _, back_re, back_im, current = link(
        c, s, here(0, -1), here(1, -1), here(0, 0), here(1, 0)
    )
    lax.fori_loop(0, TX, source_part, (back_re, back_im, current), unroll=True)

    def exchange0(kind):
        tile, low, high = tile0.at[kind], low_out.at[kind], high_out.at[kind]
        low_to, high_to = low_in.at[kind], high_in.at[kind]
        sems = level0_sem.at[kind]
        return [
            push(low, high_to.at[3:19], 0, -1, sems, 0),
            push(high, low_to.at[3:19], 0, 1, sems, 1),
            push(tile.at[3:6], tile.at[19:22], -1, 0, sems, 2),
            push(tile.at[16:19], tile.at[0:3], 1, 0, sems, 3),
            push(low.at[0:3], high_to.at[19:22], -1, -1, sems, 4),
            push(low.at[13:16], high_to.at[0:3], 1, -1, sems, 5),
            push(high.at[0:3], low_to.at[19:22], -1, 1, sems, 6),
            push(high.at[13:16], low_to.at[0:3], 1, 1, sems, 7),
        ]

    odd_row1, odd_lane1 = lax.rem(row8, 2) == 1, lax.rem(lane, 2) == 1

    def exchange1(kind):
        for half in range(2):
            a, b, c, d = (tile1[kind, 4 + 4 * half + x, 8:16] for x in range(4))
            got1[kind, 1, 1 + half] = jnp.where(
                odd_row1, jnp.where(odd_lane1, d, c), jnp.where(odd_lane1, b, a)
            )
        got = got1.at[kind]
        sems = level1_sem.at[kind]
        first, last = got.at[1, 1], got.at[1, 2]
        return [
            push(got.at[1, 1:3], got.at[2, 1:3], 0, -1, sems, 0),
            push(got.at[1, 1:3], got.at[0, 1:3], 0, 1, sems, 1),
            push(first, got.at[1, 3], -1, 0, sems, 2),
            push(last, got.at[1, 0], 1, 0, sems, 3),
            push(first, got.at[2, 3], -1, -1, sems, 4),
            push(last, got.at[2, 0], 1, -1, sems, 5),
            push(first, got.at[0, 3], -1, 1, sems, 6),
            push(last, got.at[0, 0], 1, 1, sems, 7),
        ]

    def unpack1(kind):
        for place in range(3):
            for column in range(4):
                if place == 1 and column in (1, 2):
                    continue
                packed = got1[kind, place, column]
                even = jnp.where(odd_lane1, pltpu.roll(packed, 1, 1), packed)
                odd = jnp.where(odd_lane1, packed, pltpu.roll(packed, NZ - 1, 1))
                for x, values in enumerate((even, odd)):
                    rows = slice(8 * place, 8 * place + 8)
                    tile1[kind, 4 * column + x, rows] = jnp.where(
                        odd_row1, pltpu.roll(values, 1, 0), values
                    )
                    tile1[kind, 4 * column + 2 + x, rows] = jnp.where(
                        odd_row1, values, pltpu.roll(values, TY - 1, 0)
                    )

    def exchange2():
        copies = []
        for dy in (-3, 3, -2, 2, -1, 1, 0):
            for dx in (-1, 1, 0, -2, 2):
                if (dx or dy) and (abs(dx) < 2 or abs(dy) < 2):
                    target = got2.at[2 - dx, 3 - dy]
                    copies.append(push(got2.at[2, 3], target, dx, dy, level2_sem, len(copies)))
        return copies

    def unpack2():
        for across in range(5):
            for place in range(7):
                if across in (0, 4) and abs(place - 3) > 1:
                    continue
                for x in range(4):
                    slab = 4 * across + x - 2
                    if 0 <= slab < 16:
                        src2[slab, 2 * place : 2 * place + 2] = got2[
                            across, place, 2 * x : 2 * x + 2
                        ]

    def assemble0(kind):
        def one(slab):
            src0[kind, slab, 0:4] = low_in[kind, slab]
            src0[kind, slab, 4:12] = tile0[kind, slab]
            src0[kind, slab, 12:16] = high_in[kind, slab]

        each(0, 22, one)

    level0 = (22, 16, 4, 8, 1, 1, 16, 3)
    level1 = (16, 24, 8, 8, 2, 2, 8, 4)
    level2 = (16, 16, 6, 2, 1, 4, 4, 6)
    spread0 = (24, 16, 4, 8, 1, 1, 16, 4)
    spread1 = (20, 16, 6, 4, 1, 2, 8, 6)
    spread2 = (20, 16, 6, 2, 1, 4, 4, 8)

    def inside(level, slab):
        place = gx * level[6] + (slab - level[7])
        return jnp.logical_and(place >= 0, place < ngx * level[6])

    def gain_at(level, slab):
        return jnp.where(inside(level, slab), GAIN, 0.0)

    def edge_masks(level, row, rows):
        own_row, own_rows, step = level[2:5]
        place = lax.broadcasted_iota(jnp.int32, (rows, NZ), 0) + (gy * own_rows + (row - own_row))
        at_top = jnp.logical_and(place >= ngy * own_rows - step, place < ngy * own_rows)
        at_low = jnp.logical_and(place >= 0, place < step)
        return at_top, at_low

    def around(level, masks, ref, slab, row, rows):
        step, lanes = level[4:6]
        row = row + 8
        centre = ref[slab, row : row + rows]
        above = jnp.where(masks[0], centre, ref[slab, row + step : row + step + rows])
        below = jnp.where(masks[1], centre, ref[slab, row - step : row - step + rows])
        right = jnp.where(lane >= NZ - lanes, centre, pltpu.roll(centre, NZ - lanes, 1))
        left = jnp.where(lane < lanes, centre, pltpu.roll(centre, lanes, 1))
        along = ref[slab + 1, row : row + rows] + ref[slab - 1, row : row + rows]
        return centre, along + (above + below) + (left + right)

    def sweep(level, ref, to, source, first, last):
        rows = level[1]
        masks = edge_masks(level, 0, rows)

        def one(slab):
            centre, total = around(level, masks, ref, slab, 0, rows)
            fresh = KEEP * centre + gain_at(level, slab) * (total + source[slab])
            to[slab, 8 : 8 + rows] = fresh

        each(first, last, one)

    def smooth_down(level, source, va, vb):
        slabs, rows = level[:2]

        def one(slab):
            va[slab, 8 : 8 + rows] = gain_at(level, slab) * source[slab]

        each(0, slabs, one)
        sweep(level, va, vb, source, 1, slabs - 1)
        sweep(level, vb, va, source, 2, slabs - 2)

    def restrict_to(level, source, ref, visit):
        row, _, step, lanes, tile, margin = level[2:8]
        masks = edge_masks(level, row, TY)
        odd_row = lax.rem(lax.div(row8, step), 2) == 1
        odd_lane = lax.rem(lax.div(lane, lanes), 2) == 1

        def rest(slab):
            centre, total = around(level, masks, ref, slab, row, TY)
            return source[slab, row : row + TY] + total - 6.0 * centre

        def one(pair):
            total = rest(margin + 2 * pair) + rest(margin + 1 + 2 * pair)
            total = total + jnp.where(
                odd_row, pltpu.roll(total, step, 0), pltpu.roll(total, TY - step, 0)
            )
            total = total + jnp.where(
                odd_lane, pltpu.roll(total, lanes, 1), pltpu.roll(total, NZ - lanes, 1)
            )
            visit(pair, 0.5 * total)

        each(0, tile // 2, one)

    def smooth_up(level, start, source, va, vb, first=0):
        slabs, rows = level[:2]

        def one(slab):
            va[slab, 8 : 8 + rows] = jnp.where(inside(level, slab), start(slab), 0.0)

        each(first, slabs - first, one)
        sweep(level, va, vb, source, first + 1, slabs - first - 1)
        sweep(level, vb, va, source, first + 2, slabs - first - 2)

    def spread_down(level, source, va, vb, first, last):
        rows = level[1]
        masks = edge_masks(level, 0, rows)
        inner = source.at[:, 8 : 8 + rows]

        def two(slab):
            centre, total = around(level, masks, source, slab, 0, rows)
            fresh = gain_at(level, slab) * ((1.0 + KEEP) * centre + GAIN * total)
            vb[slab, 8 : 8 + rows] = fresh

        each(first - 1, last + 1, two)
        sweep(level, vb, va, inner, first - 2, last + 2)

        def rest(slab):
            centre, total = around(level, masks, va, slab, 0, rows)
            return inner[slab] + total - 6.0 * centre

        begin, end = first - 3, last + 3
        pairs = list(range(begin // 2, (end + 1) // 2))
        for pair in pairs:
            both = [rest(slab) for slab in (2 * pair, 2 * pair + 1) if begin <= slab < end]
            folded[pair] = both[0] + both[1] if len(both) == 2 else both[0]
        return pairs

    def fold(level, pairs, visit):
        lanes = level[5]
        odd_lane = lax.rem(lax.div(lane, lanes), 2) == 1
        for place, pair in enumerate(pairs):
            total = folded[pair, pl.ds(0, 8, 2)] + folded[pair, pl.ds(1, 8, 2)]
            total = total + jnp.where(
                odd_lane, pltpu.roll(total, lanes, 1), pltpu.roll(total, NZ - lanes, 1)
            )
            visit(place, total)

    near0 = exchange0(0)
    hear(relays_x, 0, 1)
    tell(relays_x, 0, 2)

    def half_at(level, slab):
        return jnp.where(inside(level, slab), 0.5, 0.0)

    def to_part1(place, values):
        part1[place + 4, 12:20] = half_at(spread1, place + 4) * values

    def to_part2(place, values):
        part2[place + 5, 11:19] = half_at(spread2, place + 5) * values

    fold(spread0, spread_down(spread0, part0, pa0, pb0, 4, 20), to_part1)
    fold(spread1, spread_down(spread1, part1, pa1, pb1, 4, 16), to_part2)
    spread_down(spread2, part2, pa2, pb2, 5, 15)
    modes = product(
        halves(folded[1:9].reshape(8 * 16, NZ)), (along_z[0], along_z[1])
    ).reshape(8, 16, NZ)
    row16 = lax.broadcasted_iota(jnp.int32, (16, NZ), 0)
    lane16 = lax.div(lax.broadcasted_iota(jnp.int32, (16, NZ), 1), 16)
    group_of = lax.rem(gy + 5 + lax.div(row16, 2), 8)
    gather1[gy] = jnp.sum(jnp.where((lane16 == group_of)[None], modes, 0.0), axis=1)

    def spread(ref, mine, count, target, place):
        def one(step):
            return pltpu.make_async_remote_copy(
                src_ref=ref.at[mine],
                dst_ref=ref.at[mine],
                send_sem=gather_sem.at[0, place],
                recv_sem=gather_sem.at[1, place],
                device_id=target(lax.rem(mine + step, count)),
                device_id_type=MESH,
            )

        @pl.loop(0, count - 1)
        def _(turn):
            away = lax.div(turn + 1, 2)
            one(count // 2 + away * (2 * lax.rem(turn, 2) - 1)).start()

        rest_of = ref.at[0 : count - 1]
        return pltpu.make_async_remote_copy(
            src_ref=rest_of,
            dst_ref=rest_of,
            send_sem=gather_sem.at[0, place],
            recv_sem=gather_sem.at[1, place],
            device_id=target(lax.rem(mine + 1, count)),
            device_id_type=MESH,
        )

    hear(relays_y, 4, 1)
    along = spread(gather1, gy, ngy, lambda other: (gx, other), 0)
    hear(relays_x, 0, 2)
    tell(relays_x, 0, 3)

    around2 = [(dx, dy) for dy in range(-2, 3) for dx in range(-1, 2)]
    for dx, dy in around2:
        for x in range(4):
            share[dx + 1, dy + 2, 2 * x : 2 * x + 2] = part2[
                4 * dx + x + 8, 2 * dy + 14 : 2 * dy + 16
            ]
    shared = [
        push(share.at[1 + dx, 2 + dy], got_share.at[1 - dx, 2 - dy], dx, dy, share_sem, place)
        for place, (dx, dy) in enumerate(pair for pair in around2 if pair != (0, 0))
    ]

    receive(near0)
    assemble0(0)
    smooth_down(level0, src0.at[0], va0, vb0)

    def to_level1(pair, values):
        tile1[0, pair + 4, 8:16] = values

    restrict_to(level0, src0.at[0], va0, to_level1)
    near1 = exchange1(0)

    along.wait_recv()
    groups = max(1, ngy // 8)
    chip, core = lax.div(gx, 2), lax.rem(gx, 2)
    lane8 = lax.div(lax.broadcasted_iota(jnp.int32, (8, NZ), 1), 16)
    for group in range(groups):
        total = jnp.zeros((8, NZ), jnp.float32)
        for sender in range(ngy):
            low, high = sender - 3 - 8 * group, sender + 3 - 8 * group
            if high >= 0 and low < 8:
                held = jnp.logical_and(lane8 >= low, lane8 <= high)
                total = total + jnp.where(held, gather1[sender], 0.0)
        gather2[core, chip, :, 128 * group : 128 * group + 128] = total
    hear(relays_x, 0, 3)
    across = spread(
        gather2.at[core], chip, ngx // 2, lambda other: (2 * other + core, gy), 1
    )

    receive(shared)
    total = share[1, 2]
    for dx, dy in around2:
        if dx or dy:
            total = total + got_share[1 + dx, 2 + dy]
    got2[2, 3] = total
    near2 = exchange2()

    receive(near1)
    unpack1(0)
    smooth_down(level1, tile1.at[0], va1, vb1)

    def keep1(i):
        tile1[1, i + 4, 8:16] = va1[i + 4, 16:24]

    each(0, 8, keep1)
    late1 = exchange1(1)
    def flux_xy(i, dx, dy):
        return (here(3, i, dx + 1, dy) - here(3, i, dx, dy)) - (
            here(2, i, dx, dy + 1) - here(2, i, dx, dy)
        )

    def flux_yz(i, dy):
        a_y = here(3, i, 0, dy)
        return (here(4, i, 0, dy + 1) - here(4, i, 0, dy)) - (ahead_z(a_y) - a_y)

    def flux_zx(i, dx):
        a_x = here(2, i, dx, 0)
        return (ahead_z(a_x) - a_x) - (here(4, i, dx + 1, 0) - here(4, i, dx, 0))

    def rate_part(i):
        re, im = here(0, i), here(1, i)
        condense = pin[i] - (re * re + im * im) - 6.0
        rates[0, i] += condense * re
        rates[1, i] += condense * im
        under_x = jnp.where(lane == 0, here(2, i), 0.0)
        under_y = jnp.where(lane == 0, here(3, i), 0.0)
        xy, yz, zx = flux_xy(i, 0, 0), flux_yz(i, 0), flux_zx(i, 0)
        rates[2, i] -= KAPPA2 * ((xy - flux_xy(i, 0, -1)) - (zx - (behind_z(zx) + under_x)))
        rates[3, i] -= KAPPA2 * ((yz - (behind_z(yz) - under_y)) - (xy - flux_xy(i, -1, 0)))
        rates[4, i] -= KAPPA2 * ((zx - flux_zx(i, -1)) - (yz - flux_yz(i, -1)))

    receive(links)
    for turn, field in enumerate(staged[2:], 2):
        ext[field, 1:17, 16:17, :] = face_in[0, turn]
        if turn > 2:
            ext[field, 1:17, 7:8, :] = face_in[1, turn]
    ext[3, 17, 7:8, :] = diag_in[0]
    ext[2, 0, 16:17, :] = diag_in[1]
    zero_outside()
    each(0, TX, rate_part)

    def keep0(i):
        values = va0[i + 3, 12:20]
        tile0[1, i + 3] = values
        low_out[1, i] = values[0:4]
        high_out[1, i] = values[4:8]

    each(0, TX, keep0)
    late0 = exchange0(1)

    receive(near2)
    unpack2()
    smooth_down(level2, src2, va2, vb2)
    across.wait_recv()
    swap = pltpu.make_async_remote_copy(
        src_ref=gather2.at[core],
        dst_ref=gather2.at[core],
        send_sem=gather_sem.at[0, 2],
        recv_sem=gather_sem.at[1, 2],
        device_id=(gx + 1 - 2 * core, gy),
        device_id_type=MESH,
    )
    swap.start()

    def along_x_of(side):
        shares = gather2[side].reshape(4 * ngx, 128 * groups)
        return product((along_x[0, side], along_x[1, side]), halves(shares))

    spectral = along_x_of(core)
    swap.wait_recv()
    spectral = spectral + along_x_of(1 - core)
    spectral = product(halves(spectral), (along_y[0], along_y[1])) * inverse[...]
    spectral = product((back_x[0, :, : 2 * ngx], back_x[1, :, : 2 * ngx]), halves(spectral))
    spectral = halves(spectral)
    for places in ((0, 1), (2, 3), (4,)):
        back = [
            jnp.concatenate([back_yz[part, place] for place in places], axis=1)
            for part in range(2)
        ]
        columns = product(spectral, back)
        for turn, place in enumerate(places):
            for x in range(6):
                coarse[x, 2 * place + 2 : 2 * place + 4] = columns[
                    2 * x : 2 * x + 2, 128 * turn : 128 * turn + 128
                ]

    smooth_up(
        level2,
        lambda slab: va2[slab, 8:24] + coarse[lax.div(slab, 2) - 1],
        src2,
        va2,
        vb2,
        first=2,
    )
    receive(late1)
    unpack1(1)

    def start1(slab):
        x = lax.div(slab, 2) + 4
        parts = []
        for place in range(3):
            row = 12 + 2 * place
            parts.append(jnp.where(row8 < 4, va2[x, row : row + 1], va2[x, row + 1 : row + 2]))
        return tile1[1, slab] + jnp.concatenate(parts, 0)

    smooth_up(level1, start1, tile1.at[0], va1, vb1)
    receive(late0)
    assemble0(1)
    smooth_up(
        level0,
        lambda slab: src0[1, slab] + va1[lax.div(slab + 1, 2) + 2, 12:28],
        src0.at[0],
        va0,
        vb0,
    )

    not_top = jnp.logical_or(row8 < TY - 1, gy < ngy - 1)

    def finish(i):
        potential = va0[i + 3, 12:20]
        above = jnp.where(not_top, va0[i + 3, 13:21], 0.0)
        potential_ref[i] = potential
        re, im = here(0, i), here(1, i)
        out_ref[0, i] = re + DT * (rates[0, i] + potential * im)
        out_ref[1, i] = im + DT * (rates[1, i] - potential * re)
        out_ref[2, i] = here(2, i) + DT * (rates[2, i] - (va0[i + 4, 12:20] - potential))
        out_ref[3, i] = here(3, i) + DT * (rates[3, i] - (above - potential))
        out_ref[4, i] = here(4, i) + DT * (rates[4, i] - (ahead_z(potential) - potential))

    each(0, TX, finish)

    for copy, outward in sent:
        pl.when(outward)(lambda: copy.wait_send())
    along.wait_send()
    across.wait_send()
    swap.wait_send()


def hand_over(state_ref, potential_ref, out_ref, out_potential_ref, sems):
    copies = [
        pltpu.make_async_copy(state_ref.at[field], out_ref.at[field], sems.at[field])
        for field in range(5)
    ]
    copies.append(pltpu.make_async_copy(potential_ref, out_potential_ref, sems.at[5]))
    for copy in copies:
        copy.start()
    for copy in copies:
        copy.wait()


def solution(mesh):
    ngx, ngy = mesh.shape["gx"], mesh.shape["gy"]
    tables = coarse_tables(ngx, ngy)
    groups = max(1, ngy // 8)
    width = 128 * groups
    f32, bf16 = jnp.float32, jnp.bfloat16
    vmem, dma = pltpu.VMEM, pltpu.SemaphoreType.DMA

    def body(state, pinning, lead_values):
        stepped = pl.pallas_call(
            functools.partial(kernel, ngx, ngy),
            out_shape=(vmem(state.shape, f32), vmem(pinning.shape, f32)),
            in_specs=[pl.BlockSpec(memory_space=pltpu.HBM)] * 9,
            out_specs=(
                pl.BlockSpec(memory_space=pltpu.VMEM),
                pl.BlockSpec(memory_space=pltpu.VMEM),
            ),
            scratch_shapes=[
                vmem((5, TX + 2, 24, NZ), f32),
                vmem((TX, TY, NZ), f32),
                vmem((2, TY, NZ), f32),
                vmem(tables[0].shape, bf16),
                vmem(tables[1].shape, bf16),
                vmem(tables[2].shape, bf16),
                vmem(tables[3].shape, f32),
                vmem((2, 16, 128), bf16),
                vmem((2, 5, width, 128), bf16),
                vmem((2, 5, TX, 1, NZ), f32),
                vmem((2, 5, TX, 1, NZ), f32),
                vmem((2, 1, NZ), f32),
                vmem((5, TX, TY, NZ), f32),
                vmem((5, TX, TY, NZ), f32),
                vmem((2, 22, TY, NZ), f32),
                vmem((2, TX, 4, NZ), f32),
                vmem((2, TX, 4, NZ), f32),
                vmem((2, 22, 4, NZ), f32),
                vmem((2, 22, 4, NZ), f32),
                vmem((2, 22, 16, NZ), f32),
                vmem((22, 32, NZ), f32),
                vmem((22, 32, NZ), f32),
                vmem((2, 3, 4, TY, NZ), f32),
                vmem((2, 16, 24, NZ), f32),
                vmem((16, 40, NZ), f32),
                vmem((16, 40, NZ), f32),
                vmem((3, 5, TY, NZ), f32),
                vmem((3, 5, TY, NZ), f32),
                vmem((5, 7, TY, NZ), f32),
                vmem((16, 16, NZ), f32),
                vmem((16, 32, NZ), f32),
                vmem((16, 32, NZ), f32),
                vmem((24, 32, NZ), f32),
                vmem((24, 32, NZ), f32),
                vmem((24, 32, NZ), f32),
                vmem((20, 32, NZ), f32),
                vmem((20, 32, NZ), f32),
                vmem((20, 32, NZ), f32),
                vmem((20, 32, NZ), f32),
                vmem((20, 32, NZ), f32),
                vmem((20, 32, NZ), f32),
                vmem((12, 16, NZ), f32),
                vmem((6, 16, NZ), f32),
                vmem((ngy, 8, NZ), f32),
                vmem((2, ngx // 2, 8, width), f32),
                dma((8,)),
                dma,
                dma((2, 10)),
                dma((2, 2, 8)),
                dma((2, 2, 8)),
                dma((2, 14)),
                dma((2, 26)),
                dma((2, 3)),
                pltpu.SemaphoreType.REGULAR((6, 2)),
            ],
            compiler_params=pltpu.CompilerParams(
                collective_id=0, has_side_effects=True, vmem_limit_bytes=60 * 1024 * 1024
            ),
            name="film_step",
        )(state, pinning, lead_values, *[jnp.asarray(table) for table in tables])
        return pl.pallas_call(
            hand_over,
            out_shape=(
                jax.ShapeDtypeStruct(state.shape, f32),
                jax.ShapeDtypeStruct(pinning.shape, f32),
            ),
            in_specs=[pl.BlockSpec(memory_space=pl.ANY)] * 2,
            out_specs=[pl.BlockSpec(memory_space=pl.ANY)] * 2,
            scratch_shapes=[dma((6,))],
            compiler_params=pltpu.CompilerParams(vmem_limit_bytes=4 * 1024 * 1024),
            name="hand_over",
        )(*stepped)
    placed = (P(None, "gx", "gy", None), P("gx", "gy", None), P(None, "gy", None))
    return jax.shard_map(
        body,
        mesh=mesh,
        in_specs=placed,
        out_specs=(P(None, "gx", "gy", None), P("gx", "gy", None)),
        check_vma=False,
    )
```

```python
import functools
import math

import jax
import jax.numpy as jnp
import ml_dtypes
import numpy as np
from jax import lax
from jax.experimental import pallas as pl
from jax.experimental.pallas import tpu as pltpu
from jax.sharding import PartitionSpec as P

MESH = pl.DeviceIdType.MESH
OMEGA = 0.8
DT = 0.05
KAPPA2 = 2.0
KEEP = 1.0 - OMEGA
GAIN = OMEGA / 6.0
TX, TY, NZ = 16, 8, 128


def chebyshev_powers(function, terms):
    fit = np.polynomial.chebyshev.Chebyshev.interpolate(
        lambda u: function(np.sqrt(np.maximum(8.0 * (u + 1.0), 0.0))), terms, domain=[-1, 1]
    )
    return [float(c) for c in np.polynomial.chebyshev.cheb2poly(fit.coef)]


COS_POWERS = chebyshev_powers(np.cos, 8)
SIN_POWERS = chebyshev_powers(lambda a: np.sinc(a / np.pi), 8)


def horner(powers, u):
    total = powers[-1] * u + powers[-2]
    for power in powers[-3::-1]:
        total = total * u + power
    return total


def cos_sin(angle):
    u = angle * angle * 0.125 - 1.0
    return horner(COS_POWERS, u), horner(SIN_POWERS, u) * angle


def sine_table(count):
    modes = np.arange(1, count + 1, dtype=np.float64)
    return np.sqrt(2.0 / (count + 1)) * np.sin(np.pi / (count + 1) * modes[:, None] * modes[None])


def sine_values(count):
    return 2.0 - 2.0 * np.cos(np.pi / (count + 1) * np.arange(1, count + 1, dtype=np.float64))


def cosine_table(count):
    modes = np.arange(count, dtype=np.float64)
    weights = np.where(modes == 0.0, 1.0, 2.0) / count
    return np.sqrt(weights)[:, None] * np.cos(
        np.pi / count * modes[:, None] * (modes[None] + 0.5)
    )


def cosine_values(count):
    return 2.0 - 2.0 * np.cos(np.pi / count * np.arange(count, dtype=np.float64))


def split_pair(table):
    high = table.astype(ml_dtypes.bfloat16)
    low = (table - high.astype(np.float64)).astype(ml_dtypes.bfloat16)
    return np.stack([high, low])


def coarse_tables(ngx, ngy):
    nx, ny, nz = 2 * ngx, ngy, 16
    groups = max(1, ngy // 8)
    width = 128 * groups
    tx, ty, tz = sine_table(nx), cosine_table(ny), cosine_table(nz)
    lanes = np.arange(128)
    along_z = np.tile(tz[:, lanes // 8].T / 8.0, (1, 8))
    along_x = np.zeros((nx, ngx, 8))
    for cell in range(8):
        place = 2 * np.arange(ngx) + cell - 3
        within = (place >= 0) & (place < nx)
        along_x[:, within, cell] = tx[:, place[within]]
    along_x = np.moveaxis(along_x.reshape(nx, ngx // 2, 2, 8), 2, 0).reshape(2, nx, 4 * ngx)
    along_y = np.zeros((width, width))
    inverse = np.zeros((nx, width))
    values = (
        sine_values(nx)[:, None, None]
        + cosine_values(ny)[None, :, None]
        + cosine_values(nz)[None, None, :]
    )
    inverse[:, : ny * nz] = (1.0 / values).reshape(nx, ny * nz)
    along_y[: ny * nz, : ny * nz] = np.kron(ty.T, np.eye(nz))
    back_x = np.zeros((ngx, 16, 128))
    for cell in range(12):
        place = 2 * np.arange(ngx) + cell // 2 - 2
        within = (place >= 0) & (place < nx)
        back_x[within, cell, :nx] = tx.T[place[within]]
    back_yz = np.zeros((ny + 4, width, 128))
    for y in range(ny):
        back_yz[2 + y, : ny * nz] = np.kron(ty[:, y : y + 1], tz[:, lanes // 8])
    return (
        split_pair(along_z),
        split_pair(along_x),
        split_pair(along_y),
        inverse.astype(np.float32),
        split_pair(back_x),
        split_pair(back_yz),
    )


def halves(values):
    high = values.astype(jnp.bfloat16)
    return high, (values - high.astype(jnp.float32)).astype(jnp.bfloat16)


def product(left, right):
    dot = functools.partial(jnp.dot, preferred_element_type=jnp.float32)
    return dot(left[0], right[0]) + (dot(left[0], right[1]) + dot(left[1], right[0]))


def kernel(
    ngx,
    ngy,
    state_ref,
    pinning_ref,
    lead_ref,
    along_z_ref,
    along_x_ref,
    along_y_ref,
    inverse_ref,
    back_x_ref,
    back_yz_ref,
    out_ref,
    potential_ref,
    ext,
    pin,
    lead,
    along_z,
    along_x,
    along_y,
    inverse,
    back_x,
    back_yz,
    face_out,
    face_in,
    diag_in,
    rates,
    work,
    tile0,
    low_out,
    high_out,
    low_in,
    high_in,
    src0,
    va0,
    vb0,
    got1,
    tile1,
    va1,
    vb1,
    share,
    got_share,
    got2,
    src2,
    va2,
    vb2,
    part0,
    pa0,
    pb0,
    part1,
    pa1,
    pb1,
    part2,
    pa2,
    pb2,
    folded,
    coarse,
    gather1,
    gather2,
    local_sem,
    state_sem,
    halo_sem,
    level0_sem,
    level1_sem,
    share_sem,
    level2_sem,
    gather_sem,
    relay_sem,
):
    gx, gy = lax.axis_index("gx"), lax.axis_index("gy")

    def device(dx, dy):
        return (lax.rem(gx + dx % ngx, ngx), lax.rem(gy + dy % ngy, ngy))

    def each(first, last, visit):
        def one(place, carry):
            visit(place)
            return carry

        lax.fori_loop(first, last, one, 0, unroll=True)

    own_state = pltpu.make_async_copy(state_ref, ext.at[:, 1:17, 8:16], state_sem)
    own_state.start()
    got_share[...] = jnp.zeros(got_share.shape, jnp.float32)
    barrier = pltpu.get_barrier_semaphore()
    def within(dx, dy):
        tests = [gx >= -dx] * (dx < 0) + [gx < ngx - dx] * (dx > 0)
        tests += [gy >= -dy] * (dy < 0) + [gy < ngy - dy] * (dy > 0)
        return functools.reduce(jnp.logical_and, tests)

    near = [
        (dx, dy)
        for dy in range(-4, 5)
        for dx in range(-2, 3)
        if (dx or dy) and abs(dx) * abs(dy) < 4 and (dx == 0 or abs(dy) < 4)
    ]
    near.sort(key=lambda pair: abs(pair[0]) + abs(pair[1]))
    for dx, dy in near:

        @pl.when(within(dx, dy))
        def _():
            pl.semaphore_signal(
                barrier, inc=1, device_id=device(dx, dy), device_id_type=MESH
            )

    present = sum(within(dx, dy).astype(jnp.int32) for dx, dy in near)

    locals_ = [
        pltpu.make_async_copy(source, target, local_sem.at[place])
        for place, (source, target) in enumerate(
            [
                (pinning_ref, pin),
                (lead_ref, lead),
                (along_z_ref, along_z),
                (along_x_ref, along_x),
                (along_y_ref, along_y),
                (inverse_ref, inverse),
                (back_x_ref.at[:, gx], back_x),
                (back_yz_ref.at[:, pl.ds(gy, 5)], back_yz),
            ]
        )
    ]
    own_state.wait()
    staged = (0, 1, 3, 2, 4)
    for turn, field in enumerate(staged):
        face_out[0, turn] = ext[field, 1:17, 8:9, :]
        face_out[1, turn] = ext[field, 1:17, 15:16, :]
    pl.semaphore_wait(barrier, present)

    sent = []

    def push(source, target, dx, dy, sems, place):
        copy = pltpu.make_async_remote_copy(
            src_ref=source,
            dst_ref=target,
            send_sem=sems.at[0, place],
            recv_sem=sems.at[1, place],
            device_id=device(dx, dy),
            device_id_type=MESH,
        )
        outward = within(dx, dy)
        pl.when(outward)(lambda: copy.start())
        sent.append((copy, outward))
        return copy, within(-dx, -dy)

    def receive(copies):
        for copy, inward in copies:
            pl.when(inward)(lambda: copy.wait_recv())

    halo = [
        push(face_out.at[0, 0:2], face_in.at[0, 0:2], 0, -1, halo_sem, 0),
        push(face_out.at[1, 0:3], face_in.at[1, 0:3], 0, 1, halo_sem, 1),
        push(ext.at[0:2, 1, 8:16], ext.at[0:2, 17, 8:16], -1, 0, halo_sem, 2),
        push(ext.at[0:3, 16, 8:16], ext.at[0:3, 0, 8:16], 1, 0, halo_sem, 3),
    ]
    links = [
        push(face_out.at[0, 2:5], face_in.at[0, 2:5], 0, -1, halo_sem, 4),
        push(face_out.at[1, 3:5], face_in.at[1, 3:5], 0, 1, halo_sem, 5),
        push(ext.at[2:5, 1, 8:16], ext.at[2:5, 17, 8:16], -1, 0, halo_sem, 6),
        push(ext.at[3:5, 16, 8:16], ext.at[3:5, 0, 8:16], 1, 0, halo_sem, 7),
        push(face_out.at[1, 2, 0], diag_in.at[0], -1, 1, halo_sem, 8),
        push(face_out.at[0, 3, 15], diag_in.at[1], 1, -1, halo_sem, 9),
    ]
    for copy in locals_:
        copy.start()

    for ref in (part0, pa0, pb0, part1, pa1, pb1, part2, pa2, pb2):
        ref[...] = jnp.zeros(ref.shape, jnp.float32)

    def clear(*refs):
        for ref in refs:
            ref[...] = jnp.zeros(ref.shape, jnp.float32)

    @pl.when(gx == 0)
    def _():
        clear(tile0.at[:, 0:3], low_in.at[:, 0:3], high_in.at[:, 0:3])
        clear(got1.at[:, :, 0:1], got2.at[0:2])

    @pl.when(gx == 1)
    def _():
        clear(got2.at[0:1])

    @pl.when(gx == ngx - 1)
    def _():
        clear(tile0.at[:, 19:22], low_in.at[:, 19:22], high_in.at[:, 19:22])
        clear(got1.at[:, :, 3:4], got2.at[3:5])

    @pl.when(gx == ngx - 2)
    def _():
        clear(got2.at[4:5])

    for place in range(3):

        @pl.when(gy == place)
        def _():
            clear(got2.at[:, 0 : 3 - place])

        @pl.when(gy == ngy - 1 - place)
        def _():
            clear(got2.at[:, 4 + place : 7])

    @pl.when(gy == 0)
    def _():
        clear(low_in, got1.at[:, 0:1])

    @pl.when(gy == ngy - 1)
    def _():
        clear(high_in, got1.at[:, 2:3])

    def relays(reach, count):
        steps = []
        while reach < count - 1:
            steps.append(reach)
            reach *= 2
        return steps

    relays_x = [(reach, 0) for reach in relays(2, ngx)]
    relays_y = [(0, reach) for reach in relays(4, ngy)]

    def tell(steps, first, place):
        if place < len(steps):
            dx, dy = steps[place]
            for side, sign in enumerate((-1, 1)):

                @pl.when(within(sign * dx, sign * dy))
                def _():
                    pl.semaphore_signal(
                        relay_sem.at[first + place, side],
                        inc=1,
                        device_id=device(sign * dx, sign * dy),
                        device_id_type=MESH,
                    )

    def hear(steps, first, place):
        if place < len(steps):
            dx, dy = steps[place]
            for side, sign in enumerate((-1, 1)):

                @pl.when(within(-sign * dx, -sign * dy))
                def _():
                    pl.semaphore_wait(relay_sem.at[first + place, side], 1)

    tell(relays_y, 4, 0)
    tell(relays_x, 0, 0)

    lane = lax.broadcasted_iota(jnp.int32, (1, NZ), 1)
    row8 = lax.broadcasted_iota(jnp.int32, (TY, NZ), 0)

    def ahead_z(values):
        return jnp.where(lane == NZ - 1, 0.0, pltpu.roll(values, NZ - 1, 1))

    def behind_z(values):
        return jnp.where(lane == 0, 0.0, pltpu.roll(values, 1, 1))

    def here(field, slab, dx=0, dy=0):
        return ext[field, slab + (1 + dx), 8 + dy : 16 + dy, :]

    def link(c, s, re, im, next_re, next_im):
        moved_re = c * next_re + s * next_im
        moved_im = c * next_im - s * next_re
        current = re * moved_im - im * moved_re
        return moved_re, moved_im, c * re - s * im, c * im + s * re, current

    def own_part(i):
        re, im = here(0, i), here(1, i)
        c, s = cos_sin(here(4, i))
        moved_re, moved_im, back_re, back_im, current = link(
            c, s, re, im, ahead_z(re), ahead_z(im)
        )
        rates[0, i] = moved_re + behind_z(back_re)
        rates[1, i] = moved_im + behind_z(back_im)
        rates[4, i] = current
        work[0, i] = behind_z(current) - current
        work[1, i], work[2, i] = cos_sin(here(2, i))
        work[3, i], work[4, i] = cos_sin(here(3, i))

    each(0, TX, own_part)
    hear(relays_y, 4, 0)
    tell(relays_y, 4, 1)
    hear(relays_x, 0, 0)
    tell(relays_x, 0, 1)
    for copy in locals_:
        copy.wait()
    work[0, 0] += jnp.where(gx == 0, 1.0, 0.0) * lead[0]
    work[0, TX - 1] += jnp.where(gx == ngx - 1, 1.0, 0.0) * lead[1]

    receive(halo)
    for turn, field in enumerate(staged[:3]):
        if turn < 2:
            ext[field, 1:17, 16:17, :] = face_in[0, turn]
        ext[field, 1:17, 7:8, :] = face_in[1, turn]

    def zero_outside():
        @pl.when(gx == 0)
        def _():
            ext[:, 0, :, :] = jnp.zeros((5, 24, NZ), jnp.float32)

        @pl.when(gx == ngx - 1)
        def _():
            ext[:, 17, :, :] = jnp.zeros((5, 24, NZ), jnp.float32)

        @pl.when(gy == 0)
        def _():
            ext[:, :, 7:8, :] = jnp.zeros((5, 18, 1, NZ), jnp.float32)

        @pl.when(gy == ngy - 1)
        def _():
            ext[:, :, 16:17, :] = jnp.zeros((5, 18, 1, NZ), jnp.float32)

    zero_outside()

    def source_part(i, carry):
        from_re, from_im, from_current = carry
        re, im = here(0, i), here(1, i)
        moved_re, moved_im, back_re, back_im, current = link(
            work[1, i], work[2, i], re, im, here(0, i, 1), here(1, i, 1)
        )
        up_re, up_im, _, _, up_current = link(
            work[3, i], work[4, i], re, im, here(0, i, 0, 1), here(1, i, 0, 1)
        )
        c, s = cos_sin(here(3, i, 0, -1))
        _, _, down_re, down_im, down_current = link(
            c, s, here(0, i, 0, -1), here(1, i, 0, -1), re, im
        )
        rates[0, i] += (moved_re + from_re) + (up_re + down_re)
        rates[1, i] += (moved_im + from_im) + (up_im + down_im)
        rates[2, i] = current
        rates[3, i] = up_current
        source = work[0, i] - (current - from_current) - (up_current - down_current)
        tile0[0, i + 3] = source
        part0[i + 4, 12:20] = source
        low_out[0, i] = source[0:4]
        high_out[0, i] = source[4:8]
        return back_re, back_im, current

    c, s = cos_sin(here(2, -1))
    _, _, back_re, back_im, current = link(
        c, s, here(0, -1), here(1, -1), here(0, 0), here(1, 0)
    )
    lax.fori_loop(0, TX, source_part, (back_re, back_im, current), unroll=True)

    def exchange0(kind):
        tile, low, high = tile0.at[kind], low_out.at[kind], high_out.at[kind]
        low_to, high_to = low_in.at[kind], high_in.at[kind]
        sems = level0_sem.at[kind]
        return [
            push(low, high_to.at[3:19], 0, -1, sems, 0),
            push(high, low_to.at[3:19], 0, 1, sems, 1),
            push(tile.at[3:6], tile.at[19:22], -1, 0, sems, 2),
            push(tile.at[16:19], tile.at[0:3], 1, 0, sems, 3),
            push(low.at[0:3], high_to.at[19:22], -1, -1, sems, 4),
            push(low.at[13:16], high_to.at[0:3], 1, -1, sems, 5),
            push(high.at[0:3], low_to.at[19:22], -1, 1, sems, 6),
            push(high.at[13:16], low_to.at[0:3], 1, 1, sems, 7),
        ]

    odd_row1, odd_lane1 = lax.rem(row8, 2) == 1, lax.rem(lane, 2) == 1

    def exchange1(kind):
        for half in range(2):
            a, b, c, d = (tile1[kind, 4 + 4 * half + x, 8:16] for x in range(4))
            got1[kind, 1, 1 + half] = jnp.where(
                odd_row1, jnp.where(odd_lane1, d, c), jnp.where(odd_lane1, b, a)
            )
        got = got1.at[kind]
        sems = level1_sem.at[kind]
        first, last = got.at[1, 1], got.at[1, 2]
        return [
            push(got.at[1, 1:3], got.at[2, 1:3], 0, -1, sems, 0),
            push(got.at[1, 1:3], got.at[0, 1:3], 0, 1, sems, 1),
            push(first, got.at[1, 3], -1, 0, sems, 2),
            push(last, got.at[1, 0], 1, 0, sems, 3),
            push(first, got.at[2, 3], -1, -1, sems, 4),
            push(last, got.at[2, 0], 1, -1, sems, 5),
            push(first, got.at[0, 3], -1, 1, sems, 6),
            push(last, got.at[0, 0], 1, 1, sems, 7),
        ]

    def unpack1(kind):
        for place in range(3):
            for column in range(4):
                if place == 1 and column in (1, 2):
                    continue
                packed = got1[kind, place, column]
                even = jnp.where(odd_lane1, pltpu.roll(packed, 1, 1), packed)
                odd = jnp.where(odd_lane1, packed, pltpu.roll(packed, NZ - 1, 1))
                for x, values in enumerate((even, odd)):
                    rows = slice(8 * place, 8 * place + 8)
                    tile1[kind, 4 * column + x, rows] = jnp.where(
                        odd_row1, pltpu.roll(values, 1, 0), values
                    )
                    tile1[kind, 4 * column + 2 + x, rows] = jnp.where(
                        odd_row1, values, pltpu.roll(values, TY - 1, 0)
                    )

    def exchange2():
        copies = []
        for dy in (-3, 3, -2, 2, -1, 1, 0):
            for dx in (-1, 1, 0, -2, 2):
                if (dx or dy) and (abs(dx) < 2 or abs(dy) < 2):
                    target = got2.at[2 - dx, 3 - dy]
                    copies.append(push(got2.at[2, 3], target, dx, dy, level2_sem, len(copies)))
        return copies

    def unpack2():
        for across in range(5):
            for place in range(7):
                if across in (0, 4) and abs(place - 3) > 1:
                    continue
                for x in range(4):
                    slab = 4 * across + x - 2
                    if 0 <= slab < 16:
                        src2[slab, 2 * place : 2 * place + 2] = got2[
                            across, place, 2 * x : 2 * x + 2
                        ]

    def assemble0(kind):
        def one(slab):
            src0[kind, slab, 0:4] = low_in[kind, slab]
            src0[kind, slab, 4:12] = tile0[kind, slab]
            src0[kind, slab, 12:16] = high_in[kind, slab]

        each(0, 22, one)

    level0 = (22, 16, 4, 8, 1, 1, 16, 3)
    level1 = (16, 24, 8, 8, 2, 2, 8, 4)
    level2 = (16, 16, 6, 2, 1, 4, 4, 6)
    spread0 = (24, 16, 4, 8, 1, 1, 16, 4)
    spread1 = (20, 16, 6, 4, 1, 2, 8, 6)
    spread2 = (20, 16, 6, 2, 1, 4, 4, 8)

    def inside(level, slab):
        place = gx * level[6] + (slab - level[7])
        return jnp.logical_and(place >= 0, place < ngx * level[6])

    def gain_at(level, slab):
        return jnp.where(inside(level, slab), GAIN, 0.0)

    def edge_masks(level, row, rows):
        own_row, own_rows, step = level[2:5]
        place = lax.broadcasted_iota(jnp.int32, (rows, NZ), 0) + (gy * own_rows + (row - own_row))
        at_top = jnp.logical_and(place >= ngy * own_rows - step, place < ngy * own_rows)
        at_low = jnp.logical_and(place >= 0, place < step)
        return at_top, at_low

    def around(level, masks, ref, slab, row, rows):
        step, lanes = level[4:6]
        row = row + 8
        centre = ref[slab, row : row + rows]
        above = jnp.where(masks[0], centre, ref[slab, row + step : row + step + rows])
        below = jnp.where(masks[1], centre, ref[slab, row - step : row - step + rows])
        right = jnp.where(lane >= NZ - lanes, centre, pltpu.roll(centre, NZ - lanes, 1))
        left = jnp.where(lane < lanes, centre, pltpu.roll(centre, lanes, 1))
        along = ref[slab + 1, row : row + rows] + ref[slab - 1, row : row + rows]
        return centre, along + (above + below) + (left + right)

    def sweep(level, ref, to, source, first, last):
        rows = level[1]
        masks = edge_masks(level, 0, rows)

        def one(slab):
            centre, total = around(level, masks, ref, slab, 0, rows)
            fresh = KEEP * centre + gain_at(level, slab) * (total + source[slab])
            to[slab, 8 : 8 + rows] = fresh

        each(first, last, one)

    def smooth_down(level, source, va, vb):
        slabs, rows = level[:2]

        def one(slab):
            va[slab, 8 : 8 + rows] = gain_at(level, slab) * source[slab]

        each(0, slabs, one)
        sweep(level, va, vb, source, 1, slabs - 1)
        sweep(level, vb, va, source, 2, slabs - 2)

    def restrict_to(level, source, ref, visit):
        row, _, step, lanes, tile, margin = level[2:8]
        masks = edge_masks(level, row, TY)
        odd_row = lax.rem(lax.div(row8, step), 2) == 1
        odd_lane = lax.rem(lax.div(lane, lanes), 2) == 1

        def rest(slab):
            centre, total = around(level, masks, ref, slab, row, TY)
            return source[slab, row : row + TY] + total - 6.0 * centre

        def one(pair):
            total = rest(margin + 2 * pair) + rest(margin + 1 + 2 * pair)
            total = total + jnp.where(
                odd_row, pltpu.roll(total, step, 0), pltpu.roll(total, TY - step, 0)
            )
            total = total + jnp.where(
                odd_lane, pltpu.roll(total, lanes, 1), pltpu.roll(total, NZ - lanes, 1)
            )
            visit(pair, 0.5 * total)

        each(0, tile // 2, one)

    def smooth_up(level, start, source, va, vb, first=0):
        slabs, rows = level[:2]

        def one(slab):
            va[slab, 8 : 8 + rows] = jnp.where(inside(level, slab), start(slab), 0.0)

        each(first, slabs - first, one)
        sweep(level, va, vb, source, first + 1, slabs - first - 1)
        sweep(level, vb, va, source, first + 2, slabs - first - 2)

    def spread_down(level, source, va, vb, first, last):
        rows = level[1]
        masks = edge_masks(level, 0, rows)
        inner = source.at[:, 8 : 8 + rows]

        def two(slab):
            centre, total = around(level, masks, source, slab, 0, rows)
            fresh = gain_at(level, slab) * ((1.0 + KEEP) * centre + GAIN * total)
            vb[slab, 8 : 8 + rows] = fresh

        each(first - 1, last + 1, two)
        sweep(level, vb, va, inner, first - 2, last + 2)

        def rest(slab):
            centre, total = around(level, masks, va, slab, 0, rows)
            return inner[slab] + total - 6.0 * centre

        begin, end = first - 3, last + 3
        pairs = list(range(begin // 2, (end + 1) // 2))
        for pair in pairs:
            both = [rest(slab) for slab in (2 * pair, 2 * pair + 1) if begin <= slab < end]
            folded[pair] = both[0] + both[1] if len(both) == 2 else both[0]
        return pairs

    def fold(level, pairs, visit):
        lanes = level[5]
        odd_lane = lax.rem(lax.div(lane, lanes), 2) == 1
        for place, pair in enumerate(pairs):
            total = folded[pair, pl.ds(0, 8, 2)] + folded[pair, pl.ds(1, 8, 2)]
            total = total + jnp.where(
                odd_lane, pltpu.roll(total, lanes, 1), pltpu.roll(total, NZ - lanes, 1)
            )
            visit(place, total)

    near0 = exchange0(0)
    hear(relays_x, 0, 1)
    tell(relays_x, 0, 2)

    def half_at(level, slab):
        return jnp.where(inside(level, slab), 0.5, 0.0)

    def to_part1(place, values):
        part1[place + 4, 12:20] = half_at(spread1, place + 4) * values

    def to_part2(place, values):
        part2[place + 5, 11:19] = half_at(spread2, place + 5) * values

    fold(spread0, spread_down(spread0, part0, pa0, pb0, 4, 20), to_part1)
    fold(spread1, spread_down(spread1, part1, pa1, pb1, 4, 16), to_part2)
    spread_down(spread2, part2, pa2, pb2, 5, 15)
    modes = product(
        halves(folded[1:9].reshape(8 * 16, NZ)), (along_z[0], along_z[1])
    ).reshape(8, 16, NZ)
    row16 = lax.broadcasted_iota(jnp.int32, (16, NZ), 0)
    lane16 = lax.div(lax.broadcasted_iota(jnp.int32, (16, NZ), 1), 16)
    group_of = lax.rem(gy + 5 + lax.div(row16, 2), 8)
    gather1[gy] = jnp.sum(jnp.where((lane16 == group_of)[None], modes, 0.0), axis=1)

    def spread(ref, mine, count, target, place):
        def one(step):
            return pltpu.make_async_remote_copy(
                src_ref=ref.at[mine],
                dst_ref=ref.at[mine],
                send_sem=gather_sem.at[0, place],
                recv_sem=gather_sem.at[1, place],
                device_id=target(lax.rem(mine + step, count)),
                device_id_type=MESH,
            )

        @pl.loop(0, count - 1)
        def _(turn):
            away = lax.div(turn + 1, 2)
            one(count // 2 + away * (2 * lax.rem(turn, 2) - 1)).start()

        rest_of = ref.at[0 : count - 1]
        return pltpu.make_async_remote_copy(
            src_ref=rest_of,
            dst_ref=rest_of,
            send_sem=gather_sem.at[0, place],
            recv_sem=gather_sem.at[1, place],
            device_id=target(lax.rem(mine + 1, count)),
            device_id_type=MESH,
        )

    hear(relays_y, 4, 1)
    along = spread(gather1, gy, ngy, lambda other: (gx, other), 0)
    hear(relays_x, 0, 2)
    tell(relays_x, 0, 3)

    around2 = [(dx, dy) for dy in range(-2, 3) for dx in range(-1, 2)]
    for dx, dy in around2:
        for x in range(4):
            share[dx + 1, dy + 2, 2 * x : 2 * x + 2] = part2[
                4 * dx + x + 8, 2 * dy + 14 : 2 * dy + 16
            ]
    shared = [
        push(share.at[1 + dx, 2 + dy], got_share.at[1 - dx, 2 - dy], dx, dy, share_sem, place)
        for place, (dx, dy) in enumerate(pair for pair in around2 if pair != (0, 0))
    ]

    receive(near0)
    assemble0(0)
    smooth_down(level0, src0.at[0], va0, vb0)

    def to_level1(pair, values):
        tile1[0, pair + 4, 8:16] = values

    restrict_to(level0, src0.at[0], va0, to_level1)
    near1 = exchange1(0)

    along.wait_recv()
    groups = max(1, ngy // 8)
    chip, core = lax.div(gx, 2), lax.rem(gx, 2)
    lane8 = lax.div(lax.broadcasted_iota(jnp.int32, (8, NZ), 1), 16)
    for group in range(groups):
        total = jnp.zeros((8, NZ), jnp.float32)
        for sender in range(ngy):
            low, high = sender - 3 - 8 * group, sender + 3 - 8 * group
            if high >= 0 and low < 8:
                held = jnp.logical_and(lane8 >= low, lane8 <= high)
                total = total + jnp.where(held, gather1[sender], 0.0)
        gather2[core, chip, :, 128 * group : 128 * group + 128] = total
    hear(relays_x, 0, 3)
    across = spread(
        gather2.at[core], chip, ngx // 2, lambda other: (2 * other + core, gy), 1
    )

    def other_core(source, step):
        return pltpu.make_async_remote_copy(
            src_ref=source,
            dst_ref=source,
            send_sem=gather_sem.at[0, 2],
            recv_sem=gather_sem.at[1, 2],
            device_id=(2 * lax.rem(chip + step, ngx // 2) + 1 - core, gy),
            device_id_type=MESH,
        )

    @pl.loop(0, ngx // 2)
    def _(step):
        other_core(gather2.at[core, chip], step).start()

    swap = other_core(gather2.at[core], 0)

    receive(shared)
    total = share[1, 2]
    for dx, dy in around2:
        if dx or dy:
            total = total + got_share[1 + dx, 2 + dy]
    got2[2, 3] = total
    near2 = exchange2()

    receive(near1)
    unpack1(0)
    smooth_down(level1, tile1.at[0], va1, vb1)

    def keep1(i):
        tile1[1, i + 4, 8:16] = va1[i + 4, 16:24]

    each(0, 8, keep1)
    late1 = exchange1(1)
    def flux_xy(i, dx, dy):
        return (here(3, i, dx + 1, dy) - here(3, i, dx, dy)) - (
            here(2, i, dx, dy + 1) - here(2, i, dx, dy)
        )

    def flux_yz(i, dy):
        a_y = here(3, i, 0, dy)
        return (here(4, i, 0, dy + 1) - here(4, i, 0, dy)) - (ahead_z(a_y) - a_y)

    def flux_zx(i, dx):
        a_x = here(2, i, dx, 0)
        return (ahead_z(a_x) - a_x) - (here(4, i, dx + 1, 0) - here(4, i, dx, 0))

    def rate_part(i):
        re, im = here(0, i), here(1, i)
        condense = pin[i] - (re * re + im * im) - 6.0
        rates[0, i] += condense * re
        rates[1, i] += condense * im
        under_x = jnp.where(lane == 0, here(2, i), 0.0)
        under_y = jnp.where(lane == 0, here(3, i), 0.0)
        xy, yz, zx = flux_xy(i, 0, 0), flux_yz(i, 0), flux_zx(i, 0)
        rates[2, i] -= KAPPA2 * ((xy - flux_xy(i, 0, -1)) - (zx - (behind_z(zx) + under_x)))
        rates[3, i] -= KAPPA2 * ((yz - (behind_z(yz) - under_y)) - (xy - flux_xy(i, -1, 0)))
        rates[4, i] -= KAPPA2 * ((zx - flux_zx(i, -1)) - (yz - flux_yz(i, -1)))

    receive(links)
    for turn, field in enumerate(staged[2:], 2):
        ext[field, 1:17, 16:17, :] = face_in[0, turn]
        if turn > 2:
            ext[field, 1:17, 7:8, :] = face_in[1, turn]
    ext[3, 17, 7:8, :] = diag_in[0]
    ext[2, 0, 16:17, :] = diag_in[1]
    zero_outside()
    each(0, TX, rate_part)

    def keep0(i):
        values = va0[i + 3, 12:20]
        tile0[1, i + 3] = values
        low_out[1, i] = values[0:4]
        high_out[1, i] = values[4:8]

    each(0, TX, keep0)
    late0 = exchange0(1)

    receive(near2)
    unpack2()
    smooth_down(level2, src2, va2, vb2)
    across.wait_recv()
    def along_x_of(side):
        shares = gather2[side].reshape(4 * ngx, 128 * groups)
        return product((along_x[0, side], along_x[1, side]), halves(shares))

    spectral = along_x_of(core)
    swap.wait_recv()
    spectral = spectral + along_x_of(1 - core)
    spectral = product(halves(spectral), (along_y[0], along_y[1])) * inverse[...]
    spectral = product((back_x[0, :, : 2 * ngx], back_x[1, :, : 2 * ngx]), halves(spectral))
    spectral = halves(spectral)
    for places in ((0, 1), (2, 3), (4,)):
        back = [
            jnp.concatenate([back_yz[part, place] for place in places], axis=1)
            for part in range(2)
        ]
        columns = product(spectral, back)
        for turn, place in enumerate(places):
            for x in range(6):
                coarse[x, 2 * place + 2 : 2 * place + 4] = columns[
                    2 * x : 2 * x + 2, 128 * turn : 128 * turn + 128
                ]

    smooth_up(
        level2,
        lambda slab: va2[slab, 8:24] + coarse[lax.div(slab, 2) - 1],
        src2,
        va2,
        vb2,
        first=2,
    )
    receive(late1)
    unpack1(1)

    def start1(slab):
        x = lax.div(slab, 2) + 4
        parts = []
        for place in range(3):
            row = 12 + 2 * place
            parts.append(jnp.where(row8 < 4, va2[x, row : row + 1], va2[x, row + 1 : row + 2]))
        return tile1[1, slab] + jnp.concatenate(parts, 0)

    smooth_up(level1, start1, tile1.at[0], va1, vb1)
    receive(late0)
    assemble0(1)
    smooth_up(
        level0,
        lambda slab: src0[1, slab] + va1[lax.div(slab + 1, 2) + 2, 12:28],
        src0.at[0],
        va0,
        vb0,
    )

    not_top = jnp.logical_or(row8 < TY - 1, gy < ngy - 1)

    def finish(i):
        potential = va0[i + 3, 12:20]
        above = jnp.where(not_top, va0[i + 3, 13:21], 0.0)
        potential_ref[i] = potential
        re, im = here(0, i), here(1, i)
        out_ref[0, i] = re + DT * (rates[0, i] + potential * im)
        out_ref[1, i] = im + DT * (rates[1, i] - potential * re)
        out_ref[2, i] = here(2, i) + DT * (rates[2, i] - (va0[i + 4, 12:20] - potential))
        out_ref[3, i] = here(3, i) + DT * (rates[3, i] - (above - potential))
        out_ref[4, i] = here(4, i) + DT * (rates[4, i] - (ahead_z(potential) - potential))

    each(0, TX, finish)

    for copy, outward in sent:
        pl.when(outward)(lambda: copy.wait_send())
    along.wait_send()
    across.wait_send()
    swap.wait_send()


def hand_over(state_ref, potential_ref, out_ref, out_potential_ref, sems):
    copies = [
        pltpu.make_async_copy(state_ref.at[field], out_ref.at[field], sems.at[field])
        for field in range(5)
    ]
    copies.append(pltpu.make_async_copy(potential_ref, out_potential_ref, sems.at[5]))
    for copy in copies:
        copy.start()
    for copy in copies:
        copy.wait()


def solution(mesh):
    ngx, ngy = mesh.shape["gx"], mesh.shape["gy"]
    tables = coarse_tables(ngx, ngy)
    groups = max(1, ngy // 8)
    width = 128 * groups
    f32, bf16 = jnp.float32, jnp.bfloat16
    vmem, dma = pltpu.VMEM, pltpu.SemaphoreType.DMA

    def body(state, pinning, lead_values):
        stepped = pl.pallas_call(
            functools.partial(kernel, ngx, ngy),
            out_shape=(vmem(state.shape, f32), vmem(pinning.shape, f32)),
            in_specs=[pl.BlockSpec(memory_space=pltpu.HBM)] * 9,
            out_specs=(
                pl.BlockSpec(memory_space=pltpu.VMEM),
                pl.BlockSpec(memory_space=pltpu.VMEM),
            ),
            scratch_shapes=[
                vmem((5, TX + 2, 24, NZ), f32),
                vmem((TX, TY, NZ), f32),
                vmem((2, TY, NZ), f32),
                vmem(tables[0].shape, bf16),
                vmem(tables[1].shape, bf16),
                vmem(tables[2].shape, bf16),
                vmem(tables[3].shape, f32),
                vmem((2, 16, 128), bf16),
                vmem((2, 5, width, 128), bf16),
                vmem((2, 5, TX, 1, NZ), f32),
                vmem((2, 5, TX, 1, NZ), f32),
                vmem((2, 1, NZ), f32),
                vmem((5, TX, TY, NZ), f32),
                vmem((5, TX, TY, NZ), f32),
                vmem((2, 22, TY, NZ), f32),
                vmem((2, TX, 4, NZ), f32),
                vmem((2, TX, 4, NZ), f32),
                vmem((2, 22, 4, NZ), f32),
                vmem((2, 22, 4, NZ), f32),
                vmem((2, 22, 16, NZ), f32),
                vmem((22, 32, NZ), f32),
                vmem((22, 32, NZ), f32),
                vmem((2, 3, 4, TY, NZ), f32),
                vmem((2, 16, 24, NZ), f32),
                vmem((16, 40, NZ), f32),
                vmem((16, 40, NZ), f32),
                vmem((3, 5, TY, NZ), f32),
                vmem((3, 5, TY, NZ), f32),
                vmem((5, 7, TY, NZ), f32),
                vmem((16, 16, NZ), f32),
                vmem((16, 32, NZ), f32),
                vmem((16, 32, NZ), f32),
                vmem((24, 32, NZ), f32),
                vmem((24, 32, NZ), f32),
                vmem((24, 32, NZ), f32),
                vmem((20, 32, NZ), f32),
                vmem((20, 32, NZ), f32),
                vmem((20, 32, NZ), f32),
                vmem((20, 32, NZ), f32),
                vmem((20, 32, NZ), f32),
                vmem((20, 32, NZ), f32),
                vmem((12, 16, NZ), f32),
                vmem((6, 16, NZ), f32),
                vmem((ngy, 8, NZ), f32),
                vmem((2, ngx // 2, 8, width), f32),
                dma((8,)),
                dma,
                dma((2, 10)),
                dma((2, 2, 8)),
                dma((2, 2, 8)),
                dma((2, 14)),
                dma((2, 26)),
                dma((2, 3)),
                pltpu.SemaphoreType.REGULAR((6, 2)),
            ],
            compiler_params=pltpu.CompilerParams(
                collective_id=0, has_side_effects=True, vmem_limit_bytes=60 * 1024 * 1024
            ),
            name="film_step",
        )(state, pinning, lead_values, *[jnp.asarray(table) for table in tables])
        return pl.pallas_call(
            hand_over,
            out_shape=(
                jax.ShapeDtypeStruct(state.shape, f32),
                jax.ShapeDtypeStruct(pinning.shape, f32),
            ),
            in_specs=[pl.BlockSpec(memory_space=pl.ANY)] * 2,
            out_specs=[pl.BlockSpec(memory_space=pl.ANY)] * 2,
            scratch_shapes=[dma((6,))],
            compiler_params=pltpu.CompilerParams(vmem_limit_bytes=4 * 1024 * 1024),
            name="hand_over",
        )(*stepped)
    placed = (P(None, "gx", "gy", None), P("gx", "gy", None), P(None, "gy", None))
    return jax.shard_map(
        body,
        mesh=mesh,
        in_specs=placed,
        out_specs=(P(None, "gx", "gy", None), P("gx", "gy", None)),
        check_vma=False,
    )
```
